32 devices in a mesh: stars: 32 (over z, y, x, core).
Axes of the slice: x: 2, y: 2, z: 4, core: 2. Of those that a mesh axis runs over, the one named last changes fastest.
Arguments:
- positions: float32 [3, 8192], P(None, 'stars')
- velocities: float32 [3, 8192], P(None, 'stars'), may hold values from -3 to 3
- accelerations: float32 [3, 8192], P(None, 'stars'), may hold values from -360 to 360
- jerk_values: float32 [3, 8192], P(None, 'stars'), may hold values from -120 to 120
- masses: float32 [8192], P('stars'), may hold values from 3.6621095e-05 to 0.00036621094
- star_level: int32 [8192], P('stars'), may hold values from 0 to 3, as said below
- list_fine: int32 [16], replicated, may hold values from 0 to 8191, as said below
- list_mid: int32 [32], replicated, may hold values from 0 to 8191, as said below
- list_all: int32 [112], replicated, may hold values from 0 to 8191, as said below
Outputs:
- final_positions: float32 [3, 8192], P(None, 'stars')
- final_velocities: float32 [3, 8192], P(None, 'stars')
- final_accelerations: float32 [3, 8192], P(None, 'stars')
- final_jerks: float32 [3, 8192], P(None, 'stars')
The draws below stay inside these ranges and needn't reach their ends.
Inputs may be any that keep to these rules, and one draw needn't show every extreme that they name: `star_level`: exactly 16 stars have level 3, 16 level 2, 80 level 1, the rest level 0; the first and the last star have level 3. `list_fine`: the indices of the stars whose star_level is 3, ascending. `list_mid`: the indices of the stars whose star_level is 2 or 3, ascending. `list_all`: the indices of the stars whose star_level is 1, 2 or 3, ascending.
All inputs are finite; a program needn't handle non-finite values.
Results may differ from the reference program's by a relative error of at most 0.0003.
Values sent between devices are 32-bit elements; how exact they have to be, the bound alone decides.
No kernel may reach another device: no remote copies, remote signals or barrier semaphores. Data moves between devices by JAX's collectives and lax.ppermute only.
A program may use at most 64 MiB of HBM per device.

```python
import math
import jax
import jax.numpy as jnp
from jax import lax

STARS = 8192
FINE = 16


def star_levels(key):
    key_score, key_order = jax.random.split(key)
    raw = jax.random.randint(key_score, (STARS,), 0, 1024)
    places = jnp.arange(STARS)
    inner = (places < STARS // 4).astype(jnp.int32)
    order = jax.random.permutation(key_order, STARS).astype(jnp.int32)
    score = raw * (1 + 2 * inner) * STARS + order
    ends = (places == 0) | (places == STARS - 1)
    score = jnp.where(ends, 3080 * STARS + order, score)
    chosen = lax.top_k(score, 7 * FINE)[1].astype(jnp.int32)
    levels = jnp.zeros((STARS,), jnp.int32)
    levels = levels.at[chosen[:FINE]].set(3)
    levels = levels.at[chosen[FINE:2 * FINE]].set(2)
    levels = levels.at[chosen[2 * FINE:]].set(1)
    return (levels, chosen)


def draw_star_level(key, part):
    return star_levels(key)[0]


def draw_list_fine(key, part):
    return jnp.sort(star_levels(key)[1][:FINE]).astype(jnp.int32)


def draw_list_mid(key, part):
    return jnp.sort(star_levels(key)[1][:2 * FINE]).astype(jnp.int32)


def draw_list_all(key, part):
    return jnp.sort(star_levels(key)[1]).astype(jnp.int32)


def draw_positions(key, part):
    levels = star_levels(key)[0]
    key = jax.random.fold_in(key, 7)
    key_radius, key_shape = jax.random.split(key)
    lower = jnp.array([0.1, 0.08, 0.02, 0.01], jnp.float32)[levels]
    upper = jnp.array([2.0, 0.4, 0.06, 0.03], jnp.float32)[levels]
    spread = jax.random.uniform(key_radius, (STARS,), jnp.float32)
    radius = lower * jnp.exp(spread * jnp.log(upper / lower))
    shape = jax.random.uniform(key_shape, (3, STARS), jnp.float32, -1.0, 1.0)
    return (shape * radius[None, :]).astype(jnp.float32)


def draw_accelerations(key, part):
    levels = star_levels(key)[0]
    key = jax.random.fold_in(key, 11)
    scale = jnp.array([3.0, 6.0, 30.0, 60.0], jnp.float32)[levels]
    values = jnp.clip(jax.random.normal(key, (3, STARS), jnp.float32), -6.0, 6.0)
    return (values * scale[None, :]).astype(jnp.float32)


def level_of(own_key, extent, pieces, least, largest):
    def one(dim, blocks):
        draws = jax.random.uniform(jax.random.fold_in(jax.random.fold_in(own_key, 6), dim), (blocks,), jnp.float32, least / len(pieces), largest / len(pieces))
        return jnp.repeat(jnp.exp(draws), extent[dim] // blocks).reshape((-1,) + (1,) * (len(extent) - dim - 1))

    gain = one(*pieces[0])
    for cut in pieces[1:]:
        gain = gain * one(*cut)
    return gain


def noise(rng, dims, scale, limit, cuts=(), kind=jnp.bfloat16):
    values = jax.random.normal(rng, dims, jnp.float32) * scale
    if len(cuts) > 0:
        values = level_of(rng, dims, cuts, -0.22, 0.18) * values
    return jnp.clip(values, min=-limit, max=limit).astype(kind)


def setup_inputs(seed: int = 0) -> dict:
    keys = jax.random.split(jax.random.key(seed), 10)
    positions = draw_positions(jax.random.fold_in(keys[9], 71), 0)
    velocities = noise(keys[1], (3, STARS), 0.5, 3.0, ((1, 32),), jnp.float32)
    accelerations = draw_accelerations(jax.random.fold_in(keys[9], 71), 0)
    jerk_values = noise(keys[3], (3, STARS), 20.0, 120.0, ((1, 32),), jnp.float32)
    masses = jnp.clip(jnp.exp(math.log(0.00036621094) - 2.3025851 * jax.random.uniform(keys[4], (STARS,), jnp.float32) ** level_of(keys[4], (STARS,), ((0, 32),), -0.2, 0.2)), 3.662109520519152e-05, 0.00036621094)
    star_level = draw_star_level(jax.random.fold_in(keys[9], 71), 0)
    list_fine = draw_list_fine(jax.random.fold_in(keys[9], 71), 0)
    list_mid = draw_list_mid(jax.random.fold_in(keys[9], 71), 0)
    list_all = draw_list_all(jax.random.fold_in(keys[9], 71), 0)
    return dict(positions=positions, velocities=velocities, accelerations=accelerations, jerk_values=jerk_values, masses=masses, star_level=star_level, list_fine=list_fine, list_mid=list_mid, list_all=list_all)


softening = 0.0001
step_unit = 1.0 / 128.0

def elapsed(star_level, count):
    period = jnp.left_shift(jnp.ones_like(star_level), 3 - star_level)
    latest = (count - 1) // period * period
    return (count - latest).astype(jnp.float32) * step_unit

def predict(place, motion, pull, change, elapse):
    moved = place + elapse * (motion + elapse * (0.5 * pull + elapse * change / 6.0))
    sped = motion + elapse * (pull + 0.5 * elapse * change)
    return (moved, sped)

def correct(place, motion, pull, change, pull_new, change_new, elapse):
    square = elapse * elapse
    sped = motion + 0.5 * elapse * (pull + pull_new) + square * (change - change_new) / 12.0
    moved = place + 0.5 * elapse * (motion + sped) + square * (pull - pull_new) / 12.0
    return (moved, sped)

def pair_sums(target_place, target_motion, field_place, field_motion, field_mass):
    apart = [field_place[index][None, :] - target_place[index][:, None] for index in range(3)]
    closing = [field_motion[index][None, :] - target_motion[index][:, None] for index in range(3)]
    distance = apart[0] * apart[0] + apart[1] * apart[1] + apart[2] * apart[2] + softening
    inverse = lax.rsqrt(distance)
    inverse_square = inverse * inverse
    weight = field_mass[None, :] * inverse * inverse_square
    rate = 3.0 * (apart[0] * closing[0] + apart[1] * closing[1] + apart[2] * closing[2]) * inverse_square
    pull = jnp.stack([lax.optimization_barrier(jnp.sum(weight * apart[index], axis=1)) for index in range(3)])
    change = jnp.stack([lax.optimization_barrier(jnp.sum(weight * (closing[index] - rate * apart[index]), axis=1)) for index in range(3)])
    return (pull, change)

def block_forces(target_place, target_motion, field_place, field_motion, field_mass):
    total = target_place.shape[1]
    width = math.gcd(total, 16)
    count = total // width
    blocks_place = target_place.reshape(3, count, width).transpose(1, 0, 2)
    blocks_motion = target_motion.reshape(3, count, width).transpose(1, 0, 2)

    def one_block(pair):
        return pair_sums(pair[0], pair[1], field_place, field_motion, field_mass)
    pull, change = lax.map(one_block, (blocks_place, blocks_motion))
    return (pull.transpose(1, 0, 2).reshape(3, total), change.transpose(1, 0, 2).reshape(3, total))

def reference(positions, velocities, accelerations, jerk_values, masses, star_level, list_fine, list_mid, list_all):
    plan = (list_fine, list_mid, list_fine, list_all)
    for step in range(4):
        rows = plan[step]
        elapse = elapsed(star_level, step + 1)
        moved, sped = predict(positions, velocities, accelerations, jerk_values, elapse)
        pull_new, change_new = block_forces(moved[:, rows], sped[:, rows], moved, sped, masses)
        new_place, new_motion = correct(positions[:, rows], velocities[:, rows], accelerations[:, rows], jerk_values[:, rows], pull_new, change_new, elapse[rows])
        positions = positions.at[:, rows].set(new_place)
        velocities = velocities.at[:, rows].set(new_motion)
        accelerations = accelerations.at[:, rows].set(pull_new)
        jerk_values = jerk_values.at[:, rows].set(change_new)
    return (positions, velocities, accelerations, jerk_values)
```

```python
import functools

import jax
import jax.numpy as jnp
from jax import lax
from jax.experimental import pallas as pl
from jax.experimental.pallas import tpu as pltpu
from jax.sharding import PartitionSpec as P

softening = 0.0001
unit = 1.0 / 128.0
lanes = 128
vmem = pl.BlockSpec(memory_space=pltpu.VMEM)
smem = pl.BlockSpec(memory_space=pltpu.SMEM)


def predict(place, motion, pull, change, elapse):
    moved = place + elapse * (motion + elapse * (0.5 * pull + elapse * change * (1.0 / 6.0)))
    sped = motion + elapse * (pull + 0.5 * elapse * change)
    return moved, sped


def correct(place, motion, pull, change, pull_new, change_new, elapse):
    square = elapse * elapse * (1.0 / 12.0)
    sped = motion + 0.5 * elapse * (pull + pull_new) + square * (change - change_new)
    moved = place + 0.5 * elapse * (motion + sped) + square * (pull - pull_new)
    return moved, sped


def pack_kernel(place, motion, pull, change, mass, level, out):
    for part, ref in enumerate((place, motion, pull, change)):
        for half in range(2):
            out[part, 4 * half : 4 * half + 3, :] = ref[:, half * lanes : (half + 1) * lanes]
    for half in range(2):
        row = slice(half, half + 1)
        spare = slice(4 * half + 3, 4 * half + 4)
        out[0, spare, :] = jnp.where(level[row, :] <= 1, mass[row, :], 0.0)
        out[1, spare, :] = mass[row, :]
        out[2, spare, :] = jnp.zeros((1, lanes), jnp.float32)
        out[3, spare, :] = jnp.zeros((1, lanes), jnp.float32)


def plan_kernel(own, fine, mid, every, order, meta):
    first = lax.axis_index("stars") * own
    count_fine, count_mid, count_all = fine.shape[0], mid.shape[0], every.shape[0]
    for index in range(count_mid, order.shape[0]):
        order[index] = 0

    def merge(index, seen):
        star = mid[index]
        order[count_fine + index - seen] = star
        same = star == fine[jnp.minimum(seen, count_fine - 1)]
        return seen + same.astype(jnp.int32)

    lax.fori_loop(0, count_mid, merge, jnp.int32(0))
    for index in range(count_fine) if count_fine <= 16 else ():
        order[index] = fine[index]
    if count_fine > 16:

        @pl.loop(0, count_fine)
        def _(index):
            order[index] = fine[index]

    def tally(index, pair):
        star = every[index]
        return (
            pair[0] + (star < first).astype(jnp.int32),
            pair[1] + (star < first + own).astype(jnp.int32),
        )

    low, high = lax.fori_loop(0, count_all, tally, (jnp.int32(0), jnp.int32(0)), unroll=8)
    meta[0] = low
    meta[1] = high - low


def pair_terms(target, field, total):
    apart = [field[index] - target[index] for index in range(3)]
    closing = [field[3 + index] - target[3 + index] for index in range(3)]
    distance = apart[0] * apart[0] + apart[1] * apart[1] + (apart[2] * apart[2] + softening)
    inverse = lax.rsqrt(distance)
    square = inverse * inverse
    weight = field[6] * inverse * square
    dot = apart[0] * closing[0] + apart[1] * closing[1] + apart[2] * closing[2]
    rate = 3.0 * dot * square
    pulled = [weight * apart[index] for index in range(3)]
    return [total[index] + pulled[index] for index in range(3)] + [
        total[3 + index] + (weight * closing[index] - rate * pulled[index]) for index in range(3)
    ]


def main_kernel(
    devices,
    own_count,
    sizes,
    order,
    every,
    meta,
    field,
    own,
    level,
    out_place,
    out_motion,
    out_pull,
    out_change,
    ahead,
    slab,
    table,
    names,
    guess,
    mid_field,
    mid_state,
    mid_names,
    result,
):
    count_fine, count_mid, count_all = sizes
    blocks, blocks_fine = count_mid // 8, count_fine // 8
    groups = mid_field.shape[0]
    sub = lax.broadcasted_iota(jnp.int32, (8, lanes), 0)
    lane = lax.broadcasted_iota(jnp.int32, (8, lanes), 1)

    def spread(column):
        return jnp.broadcast_to(column, (8, lanes))

    def lane_total(value):
        return spread(jnp.sum(value, axis=1, keepdims=True))

    def loop(count, body):
        if count <= 4:
            for index in range(count):
                body(index)
        else:
            pl.loop(0, count)(body)

    def rows8(index):
        return pl.ds(index * 8 if isinstance(index, int) else pl.multiple_of(index * 8, 8), 8)

    def look_ahead(index):
        place, motion, pull, change = [field[pl.ds(index * 32 + 8 * part, 8), :] for part in range(4)]
        for step in range(4):
            moved, sped = predict(place, motion, pull, change, (step + 1) * unit)
            ahead[step, index, 0] = moved
            ahead[step, index, 1] = sped

    @pl.loop(0, devices // 4)
    def _(index):
        for inner in range(4):
            look_ahead(index * 4 + inner)

    def fetch(block):
        name = jnp.zeros((8, lanes), jnp.int32)
        for row in range(8):
            star = order[block * 8 + row]
            base = (star // own_count) * 32 + ((star % own_count) // lanes) * 4
            for part in range(4):
                slab[part, 4 * row : 4 * row + 4, :] = field[pl.ds(base + 8 * part, 4), :]
            name = jnp.where(sub == row, star, name)
        names[rows8(block), :] = name
        hit = (name % lanes) == lane
        for part in range(4):
            for component in range(3):
                value = slab[part, pl.ds(component, 8, stride=4), :]
                table[3 * part + component, rows8(block), :] = lane_total(jnp.where(hit, value, 0.0))
        mass = slab[1, pl.ds(3, 8, stride=4), :]
        table[12, rows8(block), :] = lane_total(jnp.where(hit, mass, 0.0))

    loop(blocks, fetch)

    def turn(ref, group, *at):
        total = jnp.zeros((8, lanes), ref.dtype)
        for inner in range(min(16, blocks)):
            value = ref[(*at, rows8(group * 16 + inner), slice(None))]
            total = total + jnp.where(lane == sub + inner * 8, value, jnp.zeros_like(value))
        return jnp.sum(total, axis=0, keepdims=True)

    def fixed(group):
        mid_field[group, 6:7, :] = turn(table, group, 12)
        found = turn(names, group)
        if blocks * 8 < lanes:
            found = jnp.where(lane[0:1, :] < blocks * 8, found, -1)
        mid_names[group, 0:1, :] = found

    loop(groups, fixed)

    def elapse_of(step, fine):
        return unit * (1 if fine or step % 2 == 0 else 2)

    def guess_block(step, fine, block):
        state = [table[index, rows8(block), :] for index in range(12)]
        elapse = elapse_of(step, fine)
        for index in range(3):
            moved, sped = predict(
                state[index], state[3 + index], state[6 + index], state[9 + index], elapse
            )
            guess[index, rows8(block), :] = moved
            guess[3 + index, rows8(block), :] = sped

    def place_mid(group):
        for index in range(6):
            mid_field[group, index : index + 1, :] = turn(guess, group, index)

    def force(step, targets):
        def add(totals, row):
            return [pair_terms(target, row, total) for target, total in zip(targets, totals)]

        def one(index, totals):
            for half in range(2):
                base = 4 * half
                row = [ahead[step, index, 0, base + k : base + k + 1, :] for k in range(3)]
                row += [ahead[step, index, 1, base + k : base + k + 1, :] for k in range(3)]
                row += [field[pl.ds(index * 32 + base + 3, 1), :]]
                totals = add(totals, row)
            return totals

        def some(index, totals):
            for inner in range(4):
                totals = one(index * 4 + inner, totals)
            return totals

        zero = jnp.zeros((8, lanes), jnp.float32)
        totals = [[zero] * 6 for _ in targets]
        for group in range(groups):
            totals = add(totals, [mid_field[group, k : k + 1, :] for k in range(7)])
        totals = lax.fori_loop(0, devices // 4, some, totals)
        return [[lane_total(value) for value in total] for total in totals]

    for step in range(4):
        loop(blocks_fine, functools.partial(guess_block, step, True))
        loop(blocks - blocks_fine, lambda block: guess_block(step, False, block + blocks_fine))
        loop(groups, place_mid)
        if step == 3:
            break

        def advance(pair, step, fine):
            targets = [
                [guess[index, rows8(2 * pair + side), :] for index in range(6)] for side in range(2)
            ]
            elapse = elapse_of(step, fine)
            for side, total in enumerate(force(step, targets)):
                rows = rows8(2 * pair + side)
                for index in range(3):
                    moved, sped = correct(
                        *[table[3 * part + index, rows, :] for part in range(4)],
                        total[index],
                        total[3 + index],
                        elapse,
                    )
                    table[index, rows, :] = moved
                    table[3 + index, rows, :] = sped
                    table[6 + index, rows, :] = total[index]
                    table[9 + index, rows, :] = total[3 + index]

        loop(blocks_fine // 2, functools.partial(advance, step=step, fine=True))
        if step == 1:
            loop(
                (blocks - blocks_fine) // 2,
                lambda pair: advance(pair + blocks_fine // 2, step=1, fine=False),
            )

    def keep(group):
        for index in range(12):
            mid_state[group, index : index + 1, :] = turn(table, group, index)

    loop(groups, keep)
    first = lax.axis_index("stars") * own_count
    low, count = meta[0], meta[1]
    result[...] = jnp.zeros_like(result)

    @pl.loop(0, (count + 7) // 8)
    def _(block):
        name = jnp.full((8, lanes), -1, jnp.int32)
        for row in range(8):
            at = block * 8 + row
            star = every[jnp.minimum(low + at, count_all - 1)]
            name = jnp.where((sub == row) & (at < count), star, name)
        own_hit = [name == lane + (first + half * lanes) for half in range(2)]
        coarse = [own_hit[half] & (level[half : half + 1, :] == 1) for half in range(2)]
        mid_hit = [name == mid_names[group, 0:1, :] for group in range(groups)]

        def find(part, component):
            total = jnp.zeros((8, lanes), jnp.float32)
            for half in range(2):
                at = 4 * half + component
                total = total + jnp.where(coarse[half], own[part, at : at + 1, :], 0.0)
            for group in range(groups):
                at = 3 * part + component
                total = total + jnp.where(mid_hit[group], mid_state[group, at : at + 1, :], 0.0)
            return lane_total(total)

        total = jnp.zeros((8, lanes), jnp.float32)
        for half in range(2):
            total = total + jnp.where(coarse[half], 4 * unit, 0.0)
        for group in range(groups):
            fine = lane + group * lanes < count_fine
            total = total + jnp.where(mid_hit[group], jnp.where(fine, unit, 2 * unit), 0.0)
        elapse = lane_total(total)

        state = [[find(part, index) for index in range(3)] for part in range(4)]
        pairs = [predict(*[state[part][index] for part in range(4)], elapse) for index in range(3)]
        target = [pair[0] for pair in pairs] + [pair[1] for pair in pairs]
        total = force(3, [target])[0]
        for index in range(3):
            moved, sped = correct(
                *[state[part][index] for part in range(4)], total[index], total[3 + index], elapse
            )
            for part, value in enumerate((moved, sped, total[index], total[3 + index])):
                for half in range(2):
                    result[part, half, index] += jnp.where(own_hit[half], value, 0.0)

    for part, ref in enumerate((out_place, out_motion, out_pull, out_change)):
        for half in range(2):
            changed = level[half : half + 1, :] >= 1
            for index in range(3):
                value = jnp.sum(result[part, half, index], axis=0, keepdims=True)
                at = 4 * half + index
                ref[index : index + 1, half * lanes : (half + 1) * lanes] = jnp.where(
                    changed, value, own[part, at : at + 1, :]
                )


def body(devices, place, motion, pull, change, masses, star_level, fine, mid, every):
    own_count = place.shape[1]
    count_mid = mid.shape[0]
    groups = -(-count_mid // lanes)
    mass = masses.reshape(2, lanes)
    level = star_level.reshape(2, lanes)
    own = pl.pallas_call(
        pack_kernel,
        out_shape=jax.ShapeDtypeStruct((4, 8, lanes), jnp.float32),
        in_specs=[vmem] * 6,
        out_specs=vmem,
        name="pack",
    )(place, motion, pull, change, mass, level)
    whole = lax.all_gather(own.reshape(32, lanes), "stars", tiled=True)
    order, meta = pl.pallas_call(
        functools.partial(plan_kernel, own_count),
        out_shape=(
            jax.ShapeDtypeStruct((count_mid + 8,), jnp.int32),
            jax.ShapeDtypeStruct((2,), jnp.int32),
        ),
        in_specs=[smem] * 3,
        out_specs=(smem, smem),
        name="plan",
    )(fine, mid, every)
    sizes = (fine.shape[0], count_mid, every.shape[0])
    result = jax.ShapeDtypeStruct((3, own_count), jnp.float32)
    return pl.pallas_call(
        functools.partial(main_kernel, devices, own_count, sizes),
        out_shape=(result,) * 4,
        in_specs=[smem] * 3 + [vmem] * 3,
        out_specs=(vmem,) * 4,
        scratch_shapes=[
            pltpu.VMEM((4, devices, 2, 8, lanes), jnp.float32),
            pltpu.VMEM((4, 32, lanes), jnp.float32),
            pltpu.VMEM((13, count_mid, lanes), jnp.float32),
            pltpu.VMEM((count_mid, lanes), jnp.int32),
            pltpu.VMEM((6, count_mid, lanes), jnp.float32),
            pltpu.VMEM((groups, 8, lanes), jnp.float32),
            pltpu.VMEM((groups, 16, lanes), jnp.float32),
            pltpu.VMEM((groups, 8, lanes), jnp.int32),
            pltpu.VMEM((4, 2, 3, 8, lanes), jnp.float32),
        ],
        compiler_params=pltpu.CompilerParams(vmem_limit_bytes=56 * 1024 * 1024),
        name="steps",
    )(order, every, meta, whole, own, level)


def solution(mesh):
    split = P(None, "stars")
    return jax.shard_map(
        functools.partial(body, mesh.shape["stars"]),
        mesh=mesh,
        in_specs=(split,) * 4 + (P("stars"),) * 2 + (P(),) * 3,
        out_specs=(split,) * 4,
        check_vma=False,
    )
```

```python
import functools

import jax
import jax.numpy as jnp
from jax import lax
from jax.experimental import pallas as pl
from jax.experimental.pallas import tpu as pltpu
from jax.sharding import PartitionSpec as P

softening = 0.0001
unit = 1.0 / 128.0
lanes = 128
vmem = pl.BlockSpec(memory_space=pltpu.VMEM)
smem = pl.BlockSpec(memory_space=pltpu.SMEM)


def predict(place, motion, pull, change, elapse):
    moved = place + elapse * (motion + elapse * (0.5 * pull + elapse * change * (1.0 / 6.0)))
    sped = motion + elapse * (pull + 0.5 * elapse * change)
    return moved, sped


def correct(place, motion, pull, change, pull_new, change_new, elapse):
    square = elapse * elapse * (1.0 / 12.0)
    sped = motion + 0.5 * elapse * (pull + pull_new) + square * (change - change_new)
    moved = place + 0.5 * elapse * (motion + sped) + square * (pull - pull_new)
    return moved, sped


def pack_kernel(place, motion, pull, change, mass, level, out):
    for part, ref in enumerate((place, motion, pull, change)):
        for half in range(2):
            out[part, 4 * half : 4 * half + 3, :] = ref[:, half * lanes : (half + 1) * lanes]
    for half in range(2):
        row = slice(half, half + 1)
        spare = slice(4 * half + 3, 4 * half + 4)
        out[0, spare, :] = jnp.where(level[row, :] <= 1, mass[row, :], 0.0)
        out[1, spare, :] = mass[row, :]
        out[2, spare, :] = jnp.zeros((1, lanes), jnp.float32)
        out[3, spare, :] = jnp.zeros((1, lanes), jnp.float32)


def plan_kernel(own, fine, mid, every, order, meta):
    first = lax.axis_index("stars") * own
    count_fine, count_mid, count_all = fine.shape[0], mid.shape[0], every.shape[0]
    for index in range(count_mid, order.shape[0]):
        order[index] = 0

    def merge(index, seen):
        star = mid[index]
        order[count_fine + index - seen] = star
        same = star == fine[jnp.minimum(seen, count_fine - 1)]
        return seen + same.astype(jnp.int32)

    lax.fori_loop(0, count_mid, merge, jnp.int32(0))
    for index in range(count_fine) if count_fine <= 16 else ():
        order[index] = fine[index]
    if count_fine > 16:

        @pl.loop(0, count_fine)
        def _(index):
            order[index] = fine[index]

    def tally(index, pair):
        star = every[index]
        return (
            pair[0] + (star < first).astype(jnp.int32),
            pair[1] + (star < first + own).astype(jnp.int32),
        )

    low, high = lax.fori_loop(0, count_all, tally, (jnp.int32(0), jnp.int32(0)), unroll=8)
    meta[0] = low
    meta[1] = high - low


def pair_terms(target, field, total):
    apart = [field[index] - target[index] for index in range(3)]
    closing = [field[3 + index] - target[3 + index] for index in range(3)]
    distance = apart[0] * apart[0] + apart[1] * apart[1] + (apart[2] * apart[2] + softening)
    inverse = lax.rsqrt(distance)
    square = inverse * inverse
    weight = field[6] * inverse * square
    dot = apart[0] * closing[0] + apart[1] * closing[1] + apart[2] * closing[2]
    rate = 3.0 * dot * square
    pulled = [weight * apart[index] for index in range(3)]
    return [total[index] + pulled[index] for index in range(3)] + [
        total[3 + index] + (weight * closing[index] - rate * pulled[index]) for index in range(3)
    ]


def rounds_of(devices):
    bits = devices.bit_length() - 1
    assert devices == 1 << bits
    rounds = []
    high = bits
    while high > 1:
        width = 1 if (high - 1) % 2 else 2
        high -= width
        rounds.append((1 << high, 1 << width))
    if high == 1:
        rounds.append((1, 2))
    return rounds


def gather(block, devices):
    for stride, radix in rounds_of(devices):
        parts = [block]
        for turn in range(1, radix):
            pairs = [(device, device ^ (turn * stride)) for device in range(devices)]
            parts.append(lax.ppermute(block, "stars", pairs))
        block = jnp.concatenate(parts, axis=0)
    return block


def slot_of(apart, devices):
    slot, held = 0, 1
    for stride, radix in rounds_of(devices):
        slot = slot + ((apart // stride) % radix) * held
        held *= radix
    return slot


def main_kernel(
    devices,
    own_count,
    sizes,
    order,
    every,
    meta,
    field,
    own,
    level,
    out_place,
    out_motion,
    out_pull,
    out_change,
    ahead,
    slab,
    table,
    names,
    guess,
    mid_field,
    mid_state,
    mid_names,
    result,
):
    count_fine, count_mid, count_all = sizes
    blocks, blocks_fine = count_mid // 8, count_fine // 8
    groups = mid_field.shape[0]
    sub = lax.broadcasted_iota(jnp.int32, (8, lanes), 0)
    lane = lax.broadcasted_iota(jnp.int32, (8, lanes), 1)

    def spread(column):
        return jnp.broadcast_to(column, (8, lanes))

    def lane_total(value):
        return spread(jnp.sum(value, axis=1, keepdims=True))

    def loop(count, body):
        if count <= 4:
            for index in range(count):
                body(index)
        else:
            pl.loop(0, count)(body)

    def rows8(index):
        return pl.ds(index * 8 if isinstance(index, int) else pl.multiple_of(index * 8, 8), 8)

    def look_ahead(index):
        place, motion, pull, change = [field[pl.ds(index * 32 + 8 * part, 8), :] for part in range(4)]
        for step in range(4):
            moved, sped = predict(place, motion, pull, change, (step + 1) * unit)
            ahead[step, index, 0] = moved
            ahead[step, index, 1] = sped

    @pl.loop(0, devices // 4)
    def _(index):
        for inner in range(4):
            look_ahead(index * 4 + inner)

    me = lax.axis_index("stars")

    def fetch(block):
        name = jnp.zeros((8, lanes), jnp.int32)
        for row in range(8):
            star = order[block * 8 + row]
            base = slot_of((star // own_count) ^ me, devices) * 32 + ((star % own_count) // lanes) * 4
            for part in range(4):
                slab[part, 4 * row : 4 * row + 4, :] = field[pl.ds(base + 8 * part, 4), :]
            name = jnp.where(sub == row, star, name)
        names[rows8(block), :] = name
        hit = (name % lanes) == lane
        for part in range(4):
            for component in range(3):
                value = slab[part, pl.ds(component, 8, stride=4), :]
                table[3 * part + component, rows8(block), :] = lane_total(jnp.where(hit, value, 0.0))
        mass = slab[1, pl.ds(3, 8, stride=4), :]
        table[12, rows8(block), :] = lane_total(jnp.where(hit, mass, 0.0))

    loop(blocks, fetch)

    def turn(ref, group, *at):
        total = jnp.zeros((8, lanes), ref.dtype)
        for inner in range(min(16, blocks)):
            value = ref[(*at, rows8(group * 16 + inner), slice(None))]
            total = total + jnp.where(lane == sub + inner * 8, value, jnp.zeros_like(value))
        return jnp.sum(total, axis=0, keepdims=True)

    def fixed(group):
        mid_field[group, 6:7, :] = turn(table, group, 12)
        found = turn(names, group)
        if blocks * 8 < lanes:
            found = jnp.where(lane[0:1, :] < blocks * 8, found, -1)
        mid_names[group, 0:1, :] = found

    loop(groups, fixed)

    def elapse_of(step, fine):
        return unit * (1 if fine or step % 2 == 0 else 2)

    def guess_block(step, fine, block):
        state = [table[index, rows8(block), :] for index in range(12)]
        elapse = elapse_of(step, fine)
        for index in range(3):
            moved, sped = predict(
                state[index], state[3 + index], state[6 + index], state[9 + index], elapse
            )
            guess[index, rows8(block), :] = moved
            guess[3 + index, rows8(block), :] = sped

    def place_mid(group):
        for index in range(6):
            mid_field[group, index : index + 1, :] = turn(guess, group, index)

    def force(step, targets):
        def add(totals, row):
            return [pair_terms(target, row, total) for target, total in zip(targets, totals)]

        def one(index, totals):
            for half in range(2):
                base = 4 * half
                row = [ahead[step, index, 0, base + k : base + k + 1, :] for k in range(3)]
                row += [ahead[step, index, 1, base + k : base + k + 1, :] for k in range(3)]
                row += [field[pl.ds(index * 32 + base + 3, 1), :]]
                totals = add(totals, row)
            return totals

        def some(index, totals):
            for inner in range(4):
                totals = one(index * 4 + inner, totals)
            return totals

        zero = jnp.zeros((8, lanes), jnp.float32)
        totals = [[zero] * 6 for _ in targets]
        for group in range(groups):
            totals = add(totals, [mid_field[group, k : k + 1, :] for k in range(7)])
        totals = lax.fori_loop(0, devices // 4, some, totals)
        return [[lane_total(value) for value in total] for total in totals]

    for step in range(4):
        loop(blocks_fine, functools.partial(guess_block, step, True))
        loop(blocks - blocks_fine, lambda block: guess_block(step, False, block + blocks_fine))
        loop(groups, place_mid)
        if step == 3:
            break

        def advance(pair, step, fine):
            targets = [
                [guess[index, rows8(2 * pair + side), :] for index in range(6)] for side in range(2)
            ]
            elapse = elapse_of(step, fine)
            for side, total in enumerate(force(step, targets)):
                rows = rows8(2 * pair + side)
                for index in range(3):
                    moved, sped = correct(
                        *[table[3 * part + index, rows, :] for part in range(4)],
                        total[index],
                        total[3 + index],
                        elapse,
                    )
                    table[index, rows, :] = moved
                    table[3 + index, rows, :] = sped
                    table[6 + index, rows, :] = total[index]
                    table[9 + index, rows, :] = total[3 + index]

        loop(blocks_fine // 2, functools.partial(advance, step=step, fine=True))
        if step == 1:
            loop(
                (blocks - blocks_fine) // 2,
                lambda pair: advance(pair + blocks_fine // 2, step=1, fine=False),
            )

    def keep(group):
        for index in range(12):
            mid_state[group, index : index + 1, :] = turn(table, group, index)

    loop(groups, keep)
    first = me * own_count
    low, count = meta[0], meta[1]
    result[...] = jnp.zeros_like(result)

    @pl.loop(0, (count + 7) // 8)
    def _(block):
        name = jnp.full((8, lanes), -1, jnp.int32)
        for row in range(8):
            at = block * 8 + row
            star = every[jnp.minimum(low + at, count_all - 1)]
            name = jnp.where((sub == row) & (at < count), star, name)
        own_hit = [name == lane + (first + half * lanes) for half in range(2)]
        coarse = [own_hit[half] & (level[half : half + 1, :] == 1) for half in range(2)]
        mid_hit = [name == mid_names[group, 0:1, :] for group in range(groups)]

        def find(part, component):
            total = jnp.zeros((8, lanes), jnp.float32)
            for half in range(2):
                at = 4 * half + component
                total = total + jnp.where(coarse[half], own[part, at : at + 1, :], 0.0)
            for group in range(groups):
                at = 3 * part + component
                total = total + jnp.where(mid_hit[group], mid_state[group, at : at + 1, :], 0.0)
            return lane_total(total)

        total = jnp.zeros((8, lanes), jnp.float32)
        for half in range(2):
            total = total + jnp.where(coarse[half], 4 * unit, 0.0)
        for group in range(groups):
            fine = lane + group * lanes < count_fine
            total = total + jnp.where(mid_hit[group], jnp.where(fine, unit, 2 * unit), 0.0)
        elapse = lane_total(total)

        state = [[find(part, index) for index in range(3)] for part in range(4)]
        pairs = [predict(*[state[part][index] for part in range(4)], elapse) for index in range(3)]
        target = [pair[0] for pair in pairs] + [pair[1] for pair in pairs]
        total = force(3, [target])[0]
        for index in range(3):
            moved, sped = correct(
                *[state[part][index] for part in range(4)], total[index], total[3 + index], elapse
            )
            for part, value in enumerate((moved, sped, total[index], total[3 + index])):
                for half in range(2):
                    result[part, half, index] += jnp.where(own_hit[half], value, 0.0)

    for part, ref in enumerate((out_place, out_motion, out_pull, out_change)):
        for half in range(2):
            changed = level[half : half + 1, :] >= 1
            for index in range(3):
                value = jnp.sum(result[part, half, index], axis=0, keepdims=True)
                at = 4 * half + index
                ref[index : index + 1, half * lanes : (half + 1) * lanes] = jnp.where(
                    changed, value, own[part, at : at + 1, :]
                )


def body(devices, place, motion, pull, change, masses, star_level, fine, mid, every):
    own_count = place.shape[1]
    count_mid = mid.shape[0]
    groups = -(-count_mid // lanes)
    mass = masses.reshape(2, lanes)
    level = star_level.reshape(2, lanes)
    own = pl.pallas_call(
        pack_kernel,
        out_shape=jax.ShapeDtypeStruct((4, 8, lanes), jnp.float32),
        in_specs=[vmem] * 6,
        out_specs=vmem,
        name="pack",
    )(place, motion, pull, change, mass, level)
    whole = gather(own.reshape(32, lanes), devices)
    order, meta = pl.pallas_call(
        functools.partial(plan_kernel, own_count),
        out_shape=(
            jax.ShapeDtypeStruct((count_mid + 8,), jnp.int32),
            jax.ShapeDtypeStruct((2,), jnp.int32),
        ),
        in_specs=[smem] * 3,
        out_specs=(smem, smem),
        name="plan",
    )(fine, mid, every)
    sizes = (fine.shape[0], count_mid, every.shape[0])
    result = jax.ShapeDtypeStruct((3, own_count), jnp.float32)
    return pl.pallas_call(
        functools.partial(main_kernel, devices, own_count, sizes),
        out_shape=(result,) * 4,
        in_specs=[smem] * 3 + [vmem] * 3,
        out_specs=(vmem,) * 4,
        scratch_shapes=[
            pltpu.VMEM((4, devices, 2, 8, lanes), jnp.float32),
            pltpu.VMEM((4, 32, lanes), jnp.float32),
            pltpu.VMEM((13, count_mid, lanes), jnp.float32),
            pltpu.VMEM((count_mid, lanes), jnp.int32),
            pltpu.VMEM((6, count_mid, lanes), jnp.float32),
            pltpu.VMEM((groups, 8, lanes), jnp.float32),
            pltpu.VMEM((groups, 16, lanes), jnp.float32),
            pltpu.VMEM((groups, 8, lanes), jnp.int32),
            pltpu.VMEM((4, 2, 3, 8, lanes), jnp.float32),
        ],
        compiler_params=pltpu.CompilerParams(vmem_limit_bytes=56 * 1024 * 1024),
        name="steps",
    )(order, every, meta, whole, own, level)


def solution(mesh):
    split = P(None, "stars")
    return jax.shard_map(
        functools.partial(body, mesh.shape["stars"]),
        mesh=mesh,
        in_specs=(split,) * 4 + (P("stars"),) * 2 + (P(),) * 3,
        out_specs=(split,) * 4,
        check_vma=False,
    )
```

```python
import functools

import jax
import jax.numpy as jnp
from jax import lax
from jax.experimental import pallas as pl
from jax.experimental.pallas import tpu as pltpu
from jax.sharding import PartitionSpec as P

softening = 0.0001
unit = 1.0 / 128.0
lanes = 128
vmem = pl.BlockSpec(memory_space=pltpu.VMEM)
smem = pl.BlockSpec(memory_space=pltpu.SMEM)


def predict(place, motion, pull, change, elapse):
    moved = place + elapse * (motion + elapse * (0.5 * pull + elapse * change * (1.0 / 6.0)))
    sped = motion + elapse * (pull + 0.5 * elapse * change)
    return moved, sped


def correct(place, motion, pull, change, pull_new, change_new, elapse):
    square = elapse * elapse * (1.0 / 12.0)
    sped = motion + 0.5 * elapse * (pull + pull_new) + square * (change - change_new)
    moved = place + 0.5 * elapse * (motion + sped) + square * (pull - pull_new)
    return moved, sped


def pack_kernel(place, motion, pull, change, mass, level, out):
    for part, ref in enumerate((place, motion, pull, change)):
        for half in range(2):
            out[part, 4 * half : 4 * half + 3, :] = ref[:, half * lanes : (half + 1) * lanes]
    for half in range(2):
        row = slice(half, half + 1)
        spare = slice(4 * half + 3, 4 * half + 4)
        out[0, spare, :] = jnp.where(level[row, :] <= 1, mass[row, :], 0.0)
        out[1, spare, :] = mass[row, :]
        out[2, spare, :] = jnp.zeros((1, lanes), jnp.float32)
        out[3, spare, :] = jnp.zeros((1, lanes), jnp.float32)


def plan_kernel(own, fine, mid, every, order, meta):
    first = lax.axis_index("stars") * own
    count_fine, count_mid, count_all = fine.shape[0], mid.shape[0], every.shape[0]
    for index in range(count_mid, order.shape[0]):
        order[index] = 0

    def merge(index, seen):
        star = mid[index]
        order[count_fine + index - seen] = star
        same = star == fine[jnp.minimum(seen, count_fine - 1)]
        return seen + same.astype(jnp.int32)

    lax.fori_loop(0, count_mid, merge, jnp.int32(0))
    for index in range(count_fine) if count_fine <= 16 else ():
        order[index] = fine[index]
    if count_fine > 16:

        @pl.loop(0, count_fine)
        def _(index):
            order[index] = fine[index]

    def tally(index, pair):
        star = every[index]
        return (
            pair[0] + (star < first).astype(jnp.int32),
            pair[1] + (star < first + own).astype(jnp.int32),
        )

    low, high = lax.fori_loop(0, count_all, tally, (jnp.int32(0), jnp.int32(0)), unroll=8)
    meta[0] = low
    meta[1] = high - low


def pair_terms(target, field, total):
    apart = [field[index] - target[index] for index in range(3)]
    closing = [field[3 + index] - target[3 + index] for index in range(3)]
    distance = apart[0] * apart[0] + apart[1] * apart[1] + (apart[2] * apart[2] + softening)
    inverse = lax.rsqrt(distance)
    square = inverse * inverse
    weight = field[6] * inverse * square
    dot = apart[0] * closing[0] + apart[1] * closing[1] + apart[2] * closing[2]
    rate = 3.0 * dot * square
    pulled = [weight * apart[index] for index in range(3)]
    return [total[index] + pulled[index] for index in range(3)] + [
        total[3 + index] + (weight * closing[index] - rate * pulled[index]) for index in range(3)
    ]


def rounds_of(devices):
    bits = devices.bit_length() - 1
    assert devices == 1 << bits
    return [(1 << bit, 2) for bit in reversed(range(bits))]


def gather(block, devices, beside):
    for place, (stride, radix) in enumerate(rounds_of(devices)):
        parts = [block]
        for turn in range(1, radix):
            pairs = [(device, device ^ (turn * stride)) for device in range(devices)]
            parts.append(lax.ppermute(block, "stars", pairs))
        block = jnp.concatenate(parts, axis=0)
        if place == 0:
            block, beside = lax.optimization_barrier((block, beside))
    return block, beside


def slot_of(apart, devices):
    slot, held = 0, 1
    for stride, radix in rounds_of(devices):
        slot = slot + ((apart // stride) % radix) * held
        held *= radix
    return slot


def main_kernel(
    devices,
    own_count,
    sizes,
    order,
    every,
    meta,
    field,
    own,
    level,
    out_place,
    out_motion,
    out_pull,
    out_change,
    ahead,
    slab,
    table,
    names,
    guess,
    mid_field,
    mid_state,
    mid_names,
    result,
):
    count_fine, count_mid, count_all = sizes
    blocks, blocks_fine = count_mid // 8, count_fine // 8
    groups = mid_field.shape[0]
    sub = lax.broadcasted_iota(jnp.int32, (8, lanes), 0)
    lane = lax.broadcasted_iota(jnp.int32, (8, lanes), 1)

    def spread(column):
        return jnp.broadcast_to(column, (8, lanes))

    def lane_total(value):
        return spread(jnp.sum(value, axis=1, keepdims=True))

    def loop(count, body):
        if count <= 4:
            for index in range(count):
                body(index)
        else:
            pl.loop(0, count)(body)

    def rows8(index):
        return pl.ds(index * 8 if isinstance(index, int) else pl.multiple_of(index * 8, 8), 8)

    def look_ahead(index):
        place, motion, pull, change = [field[pl.ds(index * 32 + 8 * part, 8), :] for part in range(4)]
        for step in range(4):
            moved, sped = predict(place, motion, pull, change, (step + 1) * unit)
            ahead[step, index, 0] = moved
            ahead[step, index, 1] = sped

    @pl.loop(0, devices // 4)
    def _(index):
        for inner in range(4):
            look_ahead(index * 4 + inner)

    me = lax.axis_index("stars")

    def fetch(block):
        name = jnp.zeros((8, lanes), jnp.int32)
        for row in range(8):
            star = order[block * 8 + row]
            base = slot_of((star // own_count) ^ me, devices) * 32 + ((star % own_count) // lanes) * 4
            for part in range(4):
                slab[part, 4 * row : 4 * row + 4, :] = field[pl.ds(base + 8 * part, 4), :]
            name = jnp.where(sub == row, star, name)
        names[rows8(block), :] = name
        hit = (name % lanes) == lane
        for part in range(4):
            for component in range(3):
                value = slab[part, pl.ds(component, 8, stride=4), :]
                table[3 * part + component, rows8(block), :] = lane_total(jnp.where(hit, value, 0.0))
        mass = slab[1, pl.ds(3, 8, stride=4), :]
        table[12, rows8(block), :] = lane_total(jnp.where(hit, mass, 0.0))

    loop(blocks, fetch)

    def turn(ref, group, *at):
        total = jnp.zeros((8, lanes), ref.dtype)
        for inner in range(min(16, blocks)):
            value = ref[(*at, rows8(group * 16 + inner), slice(None))]
            total = total + jnp.where(lane == sub + inner * 8, value, jnp.zeros_like(value))
        return jnp.sum(total, axis=0, keepdims=True)

    def fixed(group):
        mid_field[group, 6:7, :] = turn(table, group, 12)
        found = turn(names, group)
        if blocks * 8 < lanes:
            found = jnp.where(lane[0:1, :] < blocks * 8, found, -1)
        mid_names[group, 0:1, :] = found

    loop(groups, fixed)

    def elapse_of(step, fine):
        return unit * (1 if fine or step % 2 == 0 else 2)

    def guess_block(step, fine, block):
        state = [table[index, rows8(block), :] for index in range(12)]
        elapse = elapse_of(step, fine)
        for index in range(3):
            moved, sped = predict(
                state[index], state[3 + index], state[6 + index], state[9 + index], elapse
            )
            guess[index, rows8(block), :] = moved
            guess[3 + index, rows8(block), :] = sped

    def place_mid(group):
        for index in range(6):
            mid_field[group, index : index + 1, :] = turn(guess, group, index)

    def force(step, targets):
        def add(totals, row):
            return [pair_terms(target, row, total) for target, total in zip(targets, totals)]

        def one(index, totals):
            for half in range(2):
                base = 4 * half
                row = [ahead[step, index, 0, base + k : base + k + 1, :] for k in range(3)]
                row += [ahead[step, index, 1, base + k : base + k + 1, :] for k in range(3)]
                row += [field[pl.ds(index * 32 + base + 3, 1), :]]
                totals = add(totals, row)
            return totals

        def some(index, totals):
            for inner in range(4):
                totals = one(index * 4 + inner, totals)
            return totals

        zero = jnp.zeros((8, lanes), jnp.float32)
        totals = [[zero] * 6 for _ in targets]
        for group in range(groups):
            totals = add(totals, [mid_field[group, k : k + 1, :] for k in range(7)])
        totals = lax.fori_loop(0, devices // 4, some, totals)
        return [[lane_total(value) for value in total] for total in totals]

    for step in range(4):
        loop(blocks_fine, functools.partial(guess_block, step, True))
        loop(blocks - blocks_fine, lambda block: guess_block(step, False, block + blocks_fine))
        loop(groups, place_mid)
        if step == 3:
            break

        def advance(pair, step, fine):
            targets = [
                [guess[index, rows8(2 * pair + side), :] for index in range(6)] for side in range(2)
            ]
            elapse = elapse_of(step, fine)
            for side, total in enumerate(force(step, targets)):
                rows = rows8(2 * pair + side)
                for index in range(3):
                    moved, sped = correct(
                        *[table[3 * part + index, rows, :] for part in range(4)],
                        total[index],
                        total[3 + index],
                        elapse,
                    )
                    table[index, rows, :] = moved
                    table[3 + index, rows, :] = sped
                    table[6 + index, rows, :] = total[index]
                    table[9 + index, rows, :] = total[3 + index]

        loop(blocks_fine // 2, functools.partial(advance, step=step, fine=True))
        if step == 1:
            loop(
                (blocks - blocks_fine) // 2,
                lambda pair: advance(pair + blocks_fine // 2, step=1, fine=False),
            )

    def keep(group):
        for index in range(12):
            mid_state[group, index : index + 1, :] = turn(table, group, index)

    loop(groups, keep)
    first = me * own_count
    low, count = meta[0], meta[1]
    result[...] = jnp.zeros_like(result)

    @pl.loop(0, (count + 7) // 8)
    def _(block):
        name = jnp.full((8, lanes), -1, jnp.int32)
        for row in range(8):
            at = block * 8 + row
            star = every[jnp.minimum(low + at, count_all - 1)]
            name = jnp.where((sub == row) & (at < count), star, name)
        own_hit = [name == lane + (first + half * lanes) for half in range(2)]
        coarse = [own_hit[half] & (level[half : half + 1, :] == 1) for half in range(2)]
        mid_hit = [name == mid_names[group, 0:1, :] for group in range(groups)]

        def find(part, component):
            total = jnp.zeros((8, lanes), jnp.float32)
            for half in range(2):
                at = 4 * half + component
                total = total + jnp.where(coarse[half], own[part, at : at + 1, :], 0.0)
            for group in range(groups):
                at = 3 * part + component
                total = total + jnp.where(mid_hit[group], mid_state[group, at : at + 1, :], 0.0)
            return lane_total(total)

        total = jnp.zeros((8, lanes), jnp.float32)
        for half in range(2):
            total = total + jnp.where(coarse[half], 4 * unit, 0.0)
        for group in range(groups):
            fine = lane + group * lanes < count_fine
            total = total + jnp.where(mid_hit[group], jnp.where(fine, unit, 2 * unit), 0.0)
        elapse = lane_total(total)

        state = [[find(part, index) for index in range(3)] for part in range(4)]
        pairs = [predict(*[state[part][index] for part in range(4)], elapse) for index in range(3)]
        target = [pair[0] for pair in pairs] + [pair[1] for pair in pairs]
        total = force(3, [target])[0]
        for index in range(3):
            moved, sped = correct(
                *[state[part][index] for part in range(4)], total[index], total[3 + index], elapse
            )
            for part, value in enumerate((moved, sped, total[index], total[3 + index])):
                for half in range(2):
                    result[part, half, index] += jnp.where(own_hit[half], value, 0.0)

    for part, ref in enumerate((out_place, out_motion, out_pull, out_change)):
        for half in range(2):
            changed = level[half : half + 1, :] >= 1
            for index in range(3):
                value = jnp.sum(result[part, half, index], axis=0, keepdims=True)
                at = 4 * half + index
                ref[index : index + 1, half * lanes : (half + 1) * lanes] = jnp.where(
                    changed, value, own[part, at : at + 1, :]
                )


def body(devices, place, motion, pull, change, masses, star_level, fine, mid, every):
    own_count = place.shape[1]
    count_mid = mid.shape[0]
    groups = -(-count_mid // lanes)
    mass = masses.reshape(2, lanes)
    level = star_level.reshape(2, lanes)
    own = pl.pallas_call(
        pack_kernel,
        out_shape=jax.ShapeDtypeStruct((4, 8, lanes), jnp.float32),
        in_specs=[vmem] * 6,
        out_specs=vmem,
        name="pack",
    )(place, motion, pull, change, mass, level)
    order, meta = pl.pallas_call(
        functools.partial(plan_kernel, own_count),
        out_shape=(
            jax.ShapeDtypeStruct((count_mid + 8,), jnp.int32),
            jax.ShapeDtypeStruct((2,), jnp.int32),
        ),
        in_specs=[smem] * 3,
        out_specs=(smem, smem),
        name="plan",
    )(fine, mid, every)
    whole, (order, meta) = gather(own.reshape(32, lanes), devices, (order, meta))
    sizes = (fine.shape[0], count_mid, every.shape[0])
    room = devices * 56 * 1024 + count_mid * 16 * 1024 + 4 * 1024 * 1024
    result = jax.ShapeDtypeStruct((3, own_count), jnp.float32)
    return pl.pallas_call(
        functools.partial(main_kernel, devices, own_count, sizes),
        out_shape=(result,) * 4,
        in_specs=[smem] * 3 + [vmem] * 3,
        out_specs=(vmem,) * 4,
        scratch_shapes=[
            pltpu.VMEM((4, devices, 2, 8, lanes), jnp.float32),
            pltpu.VMEM((4, 32, lanes), jnp.float32),
            pltpu.VMEM((13, count_mid, lanes), jnp.float32),
            pltpu.VMEM((count_mid, lanes), jnp.int32),
            pltpu.VMEM((6, count_mid, lanes), jnp.float32),
            pltpu.VMEM((groups, 8, lanes), jnp.float32),
            pltpu.VMEM((groups, 16, lanes), jnp.float32),
            pltpu.VMEM((groups, 8, lanes), jnp.int32),
            pltpu.VMEM((4, 2, 3, 8, lanes), jnp.float32),
        ],
        compiler_params=pltpu.CompilerParams(vmem_limit_bytes=room),
        name="steps",
    )(order, every, meta, whole, own, level)


def solution(mesh):
    split = P(None, "stars")
    return jax.shard_map(
        functools.partial(body, mesh.shape["stars"]),
        mesh=mesh,
        in_specs=(split,) * 4 + (P("stars"),) * 2 + (P(),) * 3,
        out_specs=(split,) * 4,
        check_vma=False,
    )
```

```python
import functools

import jax
import jax.numpy as jnp
from jax import lax
from jax.experimental import pallas as pl
from jax.experimental.pallas import tpu as pltpu
from jax.sharding import PartitionSpec as P

softening = 0.0001
unit = 1.0 / 128.0
lanes = 128
vmem = pl.BlockSpec(memory_space=pltpu.VMEM)
smem = pl.BlockSpec(memory_space=pltpu.SMEM)


def predict(place, motion, pull, change, elapse):
    moved = place + elapse * (motion + elapse * (0.5 * pull + elapse * change * (1.0 / 6.0)))
    sped = motion + elapse * (pull + 0.5 * elapse * change)
    return moved, sped


def correct(place, motion, pull, change, pull_new, change_new, elapse):
    square = elapse * elapse * (1.0 / 12.0)
    sped = motion + 0.5 * elapse * (pull + pull_new) + square * (change - change_new)
    moved = place + 0.5 * elapse * (motion + sped) + square * (pull - pull_new)
    return moved, sped


def pack_kernel(place, motion, pull, change, mass, level, out):
    for part, ref in enumerate((place, motion, pull, change)):
        for half in range(2):
            out[part, 4 * half : 4 * half + 3, :] = ref[:, half * lanes : (half + 1) * lanes]
    for half in range(2):
        row = slice(half, half + 1)
        spare = slice(4 * half + 3, 4 * half + 4)
        out[0, spare, :] = jnp.where(level[row, :] <= 1, mass[row, :], 0.0)
        out[1, spare, :] = mass[row, :]
        out[2, spare, :] = jnp.zeros((1, lanes), jnp.float32)
        out[3, spare, :] = jnp.zeros((1, lanes), jnp.float32)


def plan_kernel(own, fine, mid, every, order, meta):
    first = lax.axis_index("stars") * own
    count_fine, count_mid, count_all = fine.shape[0], mid.shape[0], every.shape[0]
    for index in range(count_mid, order.shape[0]):
        order[index] = 0

    def merge(index, seen):
        star = mid[index]
        order[count_fine + index - seen] = star
        same = star == fine[jnp.minimum(seen, count_fine - 1)]
        return seen + same.astype(jnp.int32)

    lax.fori_loop(0, count_mid, merge, jnp.int32(0))
    for index in range(count_fine) if count_fine <= 16 else ():
        order[index] = fine[index]
    if count_fine > 16:

        @pl.loop(0, count_fine)
        def _(index):
            order[index] = fine[index]

    def tally(index, pair):
        star = every[index]
        return (
            pair[0] + (star < first).astype(jnp.int32),
            pair[1] + (star < first + own).astype(jnp.int32),
        )

    low, high = lax.fori_loop(0, count_all, tally, (jnp.int32(0), jnp.int32(0)), unroll=8)
    meta[0] = low
    meta[1] = high - low


def pair_terms(target, field, total):
    apart = [field[index] - target[index] for index in range(3)]
    closing = [field[3 + index] - target[3 + index] for index in range(3)]
    distance = apart[0] * apart[0] + apart[1] * apart[1] + (apart[2] * apart[2] + softening)
    inverse = lax.rsqrt(distance)
    square = inverse * inverse
    weight = field[6] * inverse * square
    dot = apart[0] * closing[0] + apart[1] * closing[1] + apart[2] * closing[2]
    rate = 3.0 * dot * square
    pulled = [weight * apart[index] for index in range(3)]
    return [total[index] + pulled[index] for index in range(3)] + [
        total[3 + index] + (weight * closing[index] - rate * pulled[index]) for index in range(3)
    ]


def rounds_of(devices):
    bits = devices.bit_length() - 1
    assert devices == 1 << bits
    rounds = []
    high = bits
    while high > 1:
        width = 1 if (high - 1) % 2 else 2
        high -= width
        rounds.append((1 << high, 1 << width))
    if high == 1:
        rounds.append((1, 2))
    return rounds


def gather(block, devices, beside):
    for place, (stride, radix) in enumerate(rounds_of(devices)):
        if stride == 1:
            pairs = [(device, device ^ 1) for device in range(devices)]
            block = jnp.concatenate([block, lax.ppermute(block, "stars", pairs)], axis=0)
        else:
            groups = [
                [base + step * stride for step in range(radix)]
                for base in range(devices)
                if (base // stride) % radix == 0
            ]
            copies = jnp.broadcast_to(block, (radix,) + block.shape)
            block = lax.all_to_all(copies, "stars", 0, 0, axis_index_groups=groups)
            block = block.reshape(-1, lanes)
        if place == 0:
            block, beside = lax.optimization_barrier((block, beside))
    return block, beside


def slot_of(device, me, devices):
    slot, held = 0, 1
    for stride, radix in rounds_of(devices):
        digit = ((device ^ me) if stride == 1 else device) // stride % radix
        slot = slot + digit * held
        held *= radix
    return slot


def main_kernel(
    devices,
    own_count,
    sizes,
    order,
    every,
    meta,
    field,
    level,
    out_place,
    out_motion,
    out_pull,
    out_change,
    ahead,
    slab,
    table,
    names,
    guess,
    mid_field,
    mid_state,
    mid_names,
    result,
):
    count_fine, count_mid, count_all = sizes
    blocks, blocks_fine = count_mid // 8, count_fine // 8
    groups = mid_field.shape[0]
    sub = lax.broadcasted_iota(jnp.int32, (8, lanes), 0)
    lane = lax.broadcasted_iota(jnp.int32, (8, lanes), 1)

    def spread(column):
        return jnp.broadcast_to(column, (8, lanes))

    def lane_total(value):
        return spread(jnp.sum(value, axis=1, keepdims=True))

    def loop(count, body):
        if count <= 4:
            for index in range(count):
                body(index)
        else:
            pl.loop(0, count)(body)

    def rows8(index):
        return pl.ds(index * 8 if isinstance(index, int) else pl.multiple_of(index * 8, 8), 8)

    def look_ahead(index):
        place, motion, pull, change = [field[pl.ds(index * 32 + 8 * part, 8), :] for part in range(4)]
        for step in range(4):
            moved, sped = predict(place, motion, pull, change, (step + 1) * unit)
            ahead[step, index, 0] = moved
            ahead[step, index, 1] = sped

    @pl.loop(0, devices // 4)
    def _(index):
        for inner in range(4):
            look_ahead(index * 4 + inner)

    me = lax.axis_index("stars")
    mine = slot_of(me, me, devices) * 32

    def own(part, at):
        return field[pl.ds(mine + (8 * part + at), 1), :]

    def fetch(block):
        name = jnp.zeros((8, lanes), jnp.int32)
        for row in range(8):
            star = order[block * 8 + row]
            base = slot_of(star // own_count, me, devices) * 32 + ((star % own_count) // lanes) * 4
            for part in range(4):
                slab[part, 4 * row : 4 * row + 4, :] = field[pl.ds(base + 8 * part, 4), :]
            name = jnp.where(sub == row, star, name)
        names[rows8(block), :] = name
        hit = (name % lanes) == lane
        for part in range(4):
            for component in range(3):
                value = slab[part, pl.ds(component, 8, stride=4), :]
                table[3 * part + component, rows8(block), :] = lane_total(jnp.where(hit, value, 0.0))
        mass = slab[1, pl.ds(3, 8, stride=4), :]
        table[12, rows8(block), :] = lane_total(jnp.where(hit, mass, 0.0))

    loop(blocks, fetch)

    def turn(ref, group, *at):
        total = jnp.zeros((8, lanes), ref.dtype)
        for inner in range(min(16, blocks)):
            value = ref[(*at, rows8(group * 16 + inner), slice(None))]
            total = total + jnp.where(lane == sub + inner * 8, value, jnp.zeros_like(value))
        return jnp.sum(total, axis=0, keepdims=True)

    def fixed(group):
        mid_field[group, 6:7, :] = turn(table, group, 12)
        found = turn(names, group)
        if blocks * 8 < lanes:
            found = jnp.where(lane[0:1, :] < blocks * 8, found, -1)
        mid_names[group, 0:1, :] = found

    loop(groups, fixed)

    def elapse_of(step, fine):
        return unit * (1 if fine or step % 2 == 0 else 2)

    def guess_block(step, fine, block):
        state = [table[index, rows8(block), :] for index in range(12)]
        elapse = elapse_of(step, fine)
        for index in range(3):
            moved, sped = predict(
                state[index], state[3 + index], state[6 + index], state[9 + index], elapse
            )
            guess[index, rows8(block), :] = moved
            guess[3 + index, rows8(block), :] = sped

    def place_mid(group):
        for index in range(6):
            mid_field[group, index : index + 1, :] = turn(guess, group, index)

    def force(step, targets):
        def add(totals, row):
            return [pair_terms(target, row, total) for target, total in zip(targets, totals)]

        def one(index, totals):
            for half in range(2):
                base = 4 * half
                row = [ahead[step, index, 0, base + k : base + k + 1, :] for k in range(3)]
                row += [ahead[step, index, 1, base + k : base + k + 1, :] for k in range(3)]
                row += [field[pl.ds(index * 32 + base + 3, 1), :]]
                totals = add(totals, row)
            return totals

        def some(index, totals):
            for inner in range(4):
                totals = one(index * 4 + inner, totals)
            return totals

        zero = jnp.zeros((8, lanes), jnp.float32)
        totals = [[zero] * 6 for _ in targets]
        for group in range(groups):
            totals = add(totals, [mid_field[group, k : k + 1, :] for k in range(7)])
        totals = lax.fori_loop(0, devices // 4, some, totals)
        return [[lane_total(value) for value in total] for total in totals]

    for step in range(4):
        loop(blocks_fine, functools.partial(guess_block, step, True))
        loop(blocks - blocks_fine, lambda block: guess_block(step, False, block + blocks_fine))
        loop(groups, place_mid)
        if step == 3:
            break

        def advance(pair, step, fine):
            targets = [
                [guess[index, rows8(2 * pair + side), :] for index in range(6)] for side in range(2)
            ]
            elapse = elapse_of(step, fine)
            for side, total in enumerate(force(step, targets)):
                rows = rows8(2 * pair + side)
                for index in range(3):
                    moved, sped = correct(
                        *[table[3 * part + index, rows, :] for part in range(4)],
                        total[index],
                        total[3 + index],
                        elapse,
                    )
                    table[index, rows, :] = moved
                    table[3 + index, rows, :] = sped
                    table[6 + index, rows, :] = total[index]
                    table[9 + index, rows, :] = total[3 + index]

        loop(blocks_fine // 2, functools.partial(advance, step=step, fine=True))
        if step == 1:
            loop(
                (blocks - blocks_fine) // 2,
                lambda pair: advance(pair + blocks_fine // 2, step=1, fine=False),
            )

    def keep(group):
        for index in range(12):
            mid_state[group, index : index + 1, :] = turn(table, group, index)

    loop(groups, keep)
    first = me * own_count
    low, count = meta[0], meta[1]
    result[...] = jnp.zeros_like(result)

    @pl.loop(0, (count + 7) // 8)
    def _(block):
        name = jnp.full((8, lanes), -1, jnp.int32)
        for row in range(8):
            at = block * 8 + row
            star = every[jnp.minimum(low + at, count_all - 1)]
            name = jnp.where((sub == row) & (at < count), star, name)
        own_hit = [name == lane + (first + half * lanes) for half in range(2)]
        coarse = [own_hit[half] & (level[half : half + 1, :] == 1) for half in range(2)]
        mid_hit = [name == mid_names[group, 0:1, :] for group in range(groups)]

        def find(part, component):
            total = jnp.zeros((8, lanes), jnp.float32)
            for half in range(2):
                at = 4 * half + component
                total = total + jnp.where(coarse[half], own(part, at), 0.0)
            for group in range(groups):
                at = 3 * part + component
                total = total + jnp.where(mid_hit[group], mid_state[group, at : at + 1, :], 0.0)
            return lane_total(total)

        total = jnp.zeros((8, lanes), jnp.float32)
        for half in range(2):
            total = total + jnp.where(coarse[half], 4 * unit, 0.0)
        for group in range(groups):
            fine = lane + group * lanes < count_fine
            total = total + jnp.where(mid_hit[group], jnp.where(fine, unit, 2 * unit), 0.0)
        elapse = lane_total(total)

        state = [[find(part, index) for index in range(3)] for part in range(4)]
        pairs = [predict(*[state[part][index] for part in range(4)], elapse) for index in range(3)]
        target = [pair[0] for pair in pairs] + [pair[1] for pair in pairs]
        total = force(3, [target])[0]
        for index in range(3):
            moved, sped = correct(
                *[state[part][index] for part in range(4)], total[index], total[3 + index], elapse
            )
            for part, value in enumerate((moved, sped, total[index], total[3 + index])):
                for half in range(2):
                    result[part, half, index] += jnp.where(own_hit[half], value, 0.0)

    for part, ref in enumerate((out_place, out_motion, out_pull, out_change)):
        for half in range(2):
            changed = level[half : half + 1, :] >= 1
            for index in range(3):
                value = jnp.sum(result[part, half, index], axis=0, keepdims=True)
                at = 4 * half + index
                ref[index : index + 1, half * lanes : (half + 1) * lanes] = jnp.where(
                    changed, value, own(part, at)
                )


def body(devices, place, motion, pull, change, masses, star_level, fine, mid, every):
    own_count = place.shape[1]
    count_mid = mid.shape[0]
    groups = -(-count_mid // lanes)
    mass = masses.reshape(2, lanes)
    level = star_level.reshape(2, lanes)
    own = pl.pallas_call(
        pack_kernel,
        out_shape=jax.ShapeDtypeStruct((4, 8, lanes), jnp.float32),
        in_specs=[vmem] * 6,
        out_specs=vmem,
        name="pack",
    )(place, motion, pull, change, mass, level)
    order, meta = pl.pallas_call(
        functools.partial(plan_kernel, own_count),
        out_shape=(
            jax.ShapeDtypeStruct((count_mid + 8,), jnp.int32),
            jax.ShapeDtypeStruct((2,), jnp.int32),
        ),
        in_specs=[smem] * 3,
        out_specs=(smem, smem),
        name="plan",
    )(fine, mid, every)
    whole, (order, meta) = gather(own.reshape(32, lanes), devices, (order, meta))
    sizes = (fine.shape[0], count_mid, every.shape[0])
    room = devices * 56 * 1024 + count_mid * 16 * 1024 + 4 * 1024 * 1024
    result = jax.ShapeDtypeStruct((3, own_count), jnp.float32)
    return pl.pallas_call(
        functools.partial(main_kernel, devices, own_count, sizes),
        out_shape=(result,) * 4,
        in_specs=[smem] * 3 + [vmem] * 2,
        out_specs=(vmem,) * 4,
        scratch_shapes=[
            pltpu.VMEM((4, devices, 2, 8, lanes), jnp.float32),
            pltpu.VMEM((4, 32, lanes), jnp.float32),
            pltpu.VMEM((13, count_mid, lanes), jnp.float32),
            pltpu.VMEM((count_mid, lanes), jnp.int32),
            pltpu.VMEM((6, count_mid, lanes), jnp.float32),
            pltpu.VMEM((groups, 8, lanes), jnp.float32),
            pltpu.VMEM((groups, 16, lanes), jnp.float32),
            pltpu.VMEM((groups, 8, lanes), jnp.int32),
            pltpu.VMEM((4, 2, 3, 8, lanes), jnp.float32),
        ],
        compiler_params=pltpu.CompilerParams(vmem_limit_bytes=room),
        name="steps",
    )(order, every, meta, whole, level)


def solution(mesh):
    split = P(None, "stars")
    return jax.shard_map(
        functools.partial(body, mesh.shape["stars"]),
        mesh=mesh,
        in_specs=(split,) * 4 + (P("stars"),) * 2 + (P(),) * 3,
        out_specs=(split,) * 4,
        check_vma=False,
    )
```

```python
import functools

import jax
import jax.numpy as jnp
from jax import lax
from jax.experimental import pallas as pl
from jax.experimental.pallas import tpu as pltpu
from jax.sharding import PartitionSpec as P

softening = 0.0001
unit = 1.0 / 128.0
lanes = 128
vmem = pl.BlockSpec(memory_space=pltpu.VMEM)
smem = pl.BlockSpec(memory_space=pltpu.SMEM)


def predict(place, motion, pull, change, elapse):
    moved = place + elapse * (motion + elapse * (0.5 * pull + elapse * change * (1.0 / 6.0)))
    sped = motion + elapse * (pull + 0.5 * elapse * change)
    return moved, sped


def correct(place, motion, pull, change, pull_new, change_new, elapse):
    square = elapse * elapse * (1.0 / 12.0)
    sped = motion + 0.5 * elapse * (pull + pull_new) + square * (change - change_new)
    moved = place + 0.5 * elapse * (motion + sped) + square * (pull - pull_new)
    return moved, sped


def pack(place, motion, pull, change, masses, star_level):
    mass = masses.reshape(1, -1)
    slow = jnp.where(star_level.reshape(1, -1) <= 1, mass, 0.0)
    none = jnp.zeros_like(mass)
    return jnp.concatenate([place, slow, motion, mass, pull, none, change, none], axis=0)


def rounds_of(devices):
    bits = devices.bit_length() - 1
    assert devices == 1 << bits
    rounds = []
    high = bits
    while high > 1:
        width = 1 if high == 2 else 2
        high -= width
        rounds.append((1 << high, 1 << width))
    return rounds


def gather(block, devices):
    everyone = range(devices)
    odd = lax.axis_index("stars") % 2 == 1

    def swap(value):
        return lax.ppermute(value, "stars", [(device, device ^ 1) for device in everyone])

    other = swap(block)
    block = jnp.concatenate([jnp.where(odd, other, block), jnp.where(odd, block, other)], axis=0)
    for stride, radix in rounds_of(devices):
        if radix == 2:
            got = lax.ppermute(block, "stars", [(device, device ^ stride) for device in everyone])
            block = jnp.concatenate([block, got], axis=0)
            continue
        pairs = [(device, device ^ (stride * (1 if device % 2 else 3))) for device in everyone]
        one = lax.ppermute(block, "stars", pairs)
        pairs = [(device, device ^ (2 * stride)) for device in everyone if device % 2]
        two = lax.ppermute(block, "stars", pairs)
        one_other = swap(one)
        pairs = [(device, device ^ 1) for device in everyone if device % 2]
        two_other = lax.ppermute(two, "stars", pairs)
        parts = [
            block,
            jnp.where(odd, one, one_other),
            jnp.where(odd, two, two_other),
            jnp.where(odd, one_other, one),
        ]
        block = jnp.concatenate(parts, axis=0)
    return block


def slot_of(device, me, devices):
    slot, held = device % 2, 2
    for stride, radix in rounds_of(devices):
        slot = slot + (device ^ me) // stride % radix * held
        held *= radix
    return slot


def pair_terms(target, field, total):
    apart = [field[index] - target[index] for index in range(3)]
    closing = [field[3 + index] - target[3 + index] for index in range(3)]
    distance = apart[0] * apart[0] + apart[1] * apart[1] + (apart[2] * apart[2] + softening)
    inverse = lax.rsqrt(distance)
    square = inverse * inverse
    weight = field[6] * inverse * square
    dot = apart[0] * closing[0] + apart[1] * closing[1] + apart[2] * closing[2]
    rate = 3.0 * dot * square
    pulled = [weight * apart[index] for index in range(3)]
    return [total[index] + pulled[index] for index in range(3)] + [
        total[3 + index] + (weight * closing[index] - rate * pulled[index]) for index in range(3)
    ]


def main_kernel(
    devices,
    own_count,
    sizes,
    listed_fine,
    listed_mid,
    every,
    field,
    level,
    out_place,
    out_motion,
    out_pull,
    out_change,
    ahead,
    slab,
    table,
    names,
    guess,
    mid_field,
    mid_state,
    mid_names,
    result,
    order,
):
    count_fine, count_mid, count_all = sizes
    blocks, blocks_fine = count_mid // 8, count_fine // 8
    groups = mid_field.shape[0]
    sub = lax.broadcasted_iota(jnp.int32, (8, lanes), 0)
    lane = lax.broadcasted_iota(jnp.int32, (8, lanes), 1)

    def spread(column):
        return jnp.broadcast_to(column, (8, lanes))

    def lane_total(value):
        return spread(jnp.sum(value, axis=1, keepdims=True))

    def loop(count, body):
        if count <= 4:
            for index in range(count):
                body(index)
        else:
            pl.loop(0, count)(body)

    def rows8(index):
        return pl.ds(index * 8 if isinstance(index, int) else pl.multiple_of(index * 8, 8), 8)

    halves = [slice(0, lanes), slice(lanes, 2 * lanes)]
    me = lax.axis_index("stars")
    first = me * own_count

    def look_ahead(index):
        for half in range(2):
            upper = field[pl.ds(pl.multiple_of(index * 16, 16), 8), halves[half]]
            lower = field[pl.ds(pl.multiple_of(index * 16 + 8, 8), 8), halves[half]]
            turned = pltpu.roll(lower, 4, 0)
            slope = jnp.where(sub < 4, pltpu.roll(upper, 4, 0), turned)
            bend = 0.5 * lower
            twist = jnp.where(sub < 4, turned * (1.0 / 6.0), 0.0)
            for step in range(4):
                time = (step + 1) * unit
                moved = upper + time * (slope + time * (bend + time * twist))
                ahead[step, index * 2 + half] = jnp.where(sub == 3, upper, moved)

    turns = devices // 4 if devices >= 4 else 1
    per_mid, per_all, per_fine = -(-count_mid // turns), -(-count_all // turns), -(-count_fine // turns)

    def prepare(index, carry):
        seen, low, high = carry
        for inner in range(devices // turns):
            look_ahead(index * (devices // turns) + inner)
        for inner in range(per_mid):
            at = index * per_mid + inner
            star = listed_mid[jnp.minimum(at, count_mid - 1)]
            order[count_fine + at - seen] = star
            same = star == listed_fine[jnp.minimum(seen, count_fine - 1)]
            seen = seen + same.astype(jnp.int32)
        for inner in range(per_all):
            at = index * per_all + inner
            star = every[jnp.minimum(at, count_all - 1)]
            low = low + ((star < first) & (at < count_all)).astype(jnp.int32)
            high = high + ((star < first + own_count) & (at < count_all)).astype(jnp.int32)
        return seen, low, high

    none = jnp.int32(0)
    _, low, high = lax.fori_loop(0, turns, prepare, (none, none, none))
    count = high - low

    mine = pl.multiple_of(slot_of(me, me, devices) * 16, 16)

    def own(part, component, half):
        tile = field[pl.ds(pl.multiple_of(mine + part // 2 * 8, 8), 8), halves[half]]
        at = part % 2 * 4 + component
        return tile[at : at + 1, :]

    def fetch(block, source):
        name = jnp.zeros((8, lanes), jnp.int32)
        for row in range(8):
            star = source[block * 8 + row]
            base = pl.multiple_of(slot_of(star // own_count, me, devices) * 16, 16)
            side = pl.multiple_of(star % own_count // lanes * lanes, lanes)
            slab[16 * row : 16 * row + 16, :] = field[pl.ds(base, 16), pl.ds(side, lanes)]
            name = jnp.where(sub == row, star, name)
        names[rows8(block), :] = name
        hit = (name % lanes) == lane
        for part in range(4):
            for component in range(3):
                value = slab[pl.ds(4 * part + component, 8, stride=16), :]
                table[3 * part + component, rows8(block), :] = lane_total(jnp.where(hit, value, 0.0))
        mass = slab[pl.ds(7, 8, stride=16), :]
        table[12, rows8(block), :] = lane_total(jnp.where(hit, mass, 0.0))

    loop(blocks_fine, lambda block: fetch(block, listed_fine))
    loop(blocks - blocks_fine, lambda block: fetch(block + blocks_fine, order))

    def turn(ref, group, *at):
        total = jnp.zeros((8, lanes), ref.dtype)
        for inner in range(min(16, blocks)):
            value = ref[(*at, rows8(group * 16 + inner), slice(None))]
            total = total + jnp.where(lane == sub + inner * 8, value, jnp.zeros_like(value))
        return jnp.sum(total, axis=0, keepdims=True)

    def fixed(group):
        mid_field[group, 6:7, :] = turn(table, group, 12)
        found = turn(names, group)
        if blocks * 8 < lanes:
            found = jnp.where(lane[0:1, :] < blocks * 8, found, -1)
        mid_names[group, 0:1, :] = found

    loop(groups, fixed)

    def elapse_of(step, fine):
        return unit * (1 if fine or step % 2 == 0 else 2)

    def guess_block(step, fine, block):
        state = [table[index, rows8(block), :] for index in range(12)]
        elapse = elapse_of(step, fine)
        for index in range(3):
            moved, sped = predict(
                state[index], state[3 + index], state[6 + index], state[9 + index], elapse
            )
            guess[index, rows8(block), :] = moved
            guess[3 + index, rows8(block), :] = sped

    def place_mid(group):
        for index in range(6):
            mid_field[group, index : index + 1, :] = turn(guess, group, index)

    def force(step, targets):
        def add(totals, row):
            return [pair_terms(target, row, total) for target, total in zip(targets, totals)]

        def one(index, totals):
            for half in range(2):
                row = [ahead[step, index * 2 + half, k : k + 1, :] for k in (0, 1, 2, 4, 5, 6, 3)]
                totals = add(totals, row)
            return totals

        def some(index, totals):
            for inner in range(4):
                totals = one(index * 4 + inner, totals)
            return totals

        zero = jnp.zeros((8, lanes), jnp.float32)
        totals = [[zero] * 6 for _ in targets]
        for group in range(groups):
            totals = add(totals, [mid_field[group, k : k + 1, :] for k in range(7)])
        totals = lax.fori_loop(0, devices // 4, some, totals)
        return [[lane_total(value) for value in total] for total in totals]

    for step in range(4):
        loop(blocks_fine, functools.partial(guess_block, step, True))
        loop(blocks - blocks_fine, lambda block: guess_block(step, False, block + blocks_fine))
        loop(groups, place_mid)
        if step == 3:
            break

        def advance(pair, step, fine):
            targets = [
                [guess[index, rows8(2 * pair + side), :] for index in range(6)] for side in range(2)
            ]
            elapse = elapse_of(step, fine)
            for side, total in enumerate(force(step, targets)):
                rows = rows8(2 * pair + side)
                for index in range(3):
                    moved, sped = correct(
                        *[table[3 * part + index, rows, :] for part in range(4)],
                        total[index],
                        total[3 + index],
                        elapse,
                    )
                    table[index, rows, :] = moved
                    table[3 + index, rows, :] = sped
                    table[6 + index, rows, :] = total[index]
                    table[9 + index, rows, :] = total[3 + index]

        loop(blocks_fine // 2, functools.partial(advance, step=step, fine=True))
        if step == 1:
            loop(
                (blocks - blocks_fine) // 2,
                lambda pair: advance(pair + blocks_fine // 2, step=1, fine=False),
            )

    def keep(group):
        for index in range(12):
            mid_state[group, index : index + 1, :] = turn(table, group, index)

    loop(groups, keep)
    result[...] = jnp.zeros_like(result)
    wide = 3

    @pl.loop(0, (count + (8 * wide - 1)) // (8 * wide))
    def _(turn_at):
        hits, states, elapses, targets = [], [], [], []
        for side in range(wide):
            name = jnp.full((8, lanes), -1, jnp.int32)
            for row in range(8):
                at = (turn_at * wide + side) * 8 + row
                star = every[jnp.minimum(low + at, count_all - 1)]
                name = jnp.where((sub == row) & (at < count), star, name)
            own_hit = [name == lane + (first + half * lanes) for half in range(2)]
            coarse = [own_hit[half] & (level[half : half + 1, :] == 1) for half in range(2)]
            mid_hit = [name == mid_names[group, 0:1, :] for group in range(groups)]

            def find(part, component):
                total = jnp.zeros((8, lanes), jnp.float32)
                for half in range(2):
                    total = jnp.where(coarse[half], own(part, component, half), total)
                for group in range(groups):
                    at = 3 * part + component
                    total = jnp.where(mid_hit[group], mid_state[group, at : at + 1, :], total)
                return lane_total(total)

            total = jnp.zeros((8, lanes), jnp.float32)
            for half in range(2):
                total = jnp.where(coarse[half], 4 * unit, total)
            for group in range(groups):
                fine = jnp.where(lane + group * lanes < count_fine, unit, 2 * unit)
                total = jnp.where(mid_hit[group], fine, total)
            elapse = lane_total(total)
            state = [[find(part, index) for index in range(3)] for part in range(4)]
            pairs = [
                predict(*[state[part][index] for part in range(4)], elapse) for index in range(3)
            ]
            hits.append(own_hit)
            states.append(state)
            elapses.append(elapse)
            targets.append([pair[0] for pair in pairs] + [pair[1] for pair in pairs])
        for side, total in enumerate(force(3, targets)):
            for index in range(3):
                moved, sped = correct(
                    *[states[side][part][index] for part in range(4)],
                    total[index],
                    total[3 + index],
                    elapses[side],
                )
                for part, value in enumerate((moved, sped, total[index], total[3 + index])):
                    for half in range(2):
                        result[part, half, index] += jnp.where(hits[side][half], value, 0.0)

    for part, ref in enumerate((out_place, out_motion, out_pull, out_change)):
        for half in range(2):
            changed = level[half : half + 1, :] >= 1
            for index in range(3):
                value = jnp.sum(result[part, half, index], axis=0, keepdims=True)
                ref[index : index + 1, halves[half]] = jnp.where(
                    changed, value, own(part, index, half)
                )


def body(devices, place, motion, pull, change, masses, star_level, fine, mid, every):
    own_count = place.shape[1]
    sizes = (fine.shape[0], mid.shape[0], every.shape[0])
    groups = -(-sizes[1] // lanes)
    block = pack(place, motion, pull, change, masses, star_level)
    whole = gather(block, devices)
    room = devices * 52 * 1024 + sizes[1] * 12 * 1024 + 3 * 1024 * 1024
    result = jax.ShapeDtypeStruct((3, own_count), jnp.float32)
    return pl.pallas_call(
        functools.partial(main_kernel, devices, own_count, sizes),
        out_shape=(result,) * 4,
        in_specs=[smem] * 3 + [vmem] * 2,
        out_specs=(vmem,) * 4,
        scratch_shapes=[
            pltpu.VMEM((4, devices * 2, 8, lanes), jnp.float32),
            pltpu.VMEM((8 * 16, lanes), jnp.float32),
            pltpu.VMEM((13, sizes[1], lanes), jnp.float32),
            pltpu.VMEM((sizes[1], lanes), jnp.int32),
            pltpu.VMEM((6, sizes[1], lanes), jnp.float32),
            pltpu.VMEM((groups, 8, lanes), jnp.float32),
            pltpu.VMEM((groups, 16, lanes), jnp.float32),
            pltpu.VMEM((groups, 8, lanes), jnp.int32),
            pltpu.VMEM((4, 2, 3, 8, lanes), jnp.float32),
            pltpu.SMEM((2 * sizes[1] + devices,), jnp.int32),
        ],
        compiler_params=pltpu.CompilerParams(vmem_limit_bytes=room),
        name="steps",
    )(fine, mid, every, whole, star_level.reshape(2, lanes))


def solution(mesh):
    split = P(None, "stars")
    return jax.shard_map(
        functools.partial(body, mesh.shape["stars"]),
        mesh=mesh,
        in_specs=(split,) * 4 + (P("stars"),) * 2 + (P(),) * 3,
        out_specs=(split,) * 4,
        check_vma=False,
    )
```

```python
import functools

import jax
import jax.numpy as jnp
from jax import lax
from jax.experimental import pallas as pl
from jax.experimental.pallas import tpu as pltpu
from jax.sharding import PartitionSpec as P

softening = 0.0001
unit = 1.0 / 128.0
lanes = 128
vmem = pl.BlockSpec(memory_space=pltpu.VMEM)
smem = pl.BlockSpec(memory_space=pltpu.SMEM)


def predict(place, motion, pull, change, elapse):
    moved = place + elapse * (motion + elapse * (0.5 * pull + elapse * change * (1.0 / 6.0)))
    sped = motion + elapse * (pull + 0.5 * elapse * change)
    return moved, sped


def correct(place, motion, pull, change, pull_new, change_new, elapse):
    square = elapse * elapse * (1.0 / 12.0)
    sped = motion + 0.5 * elapse * (pull + pull_new) + square * (change - change_new)
    moved = place + 0.5 * elapse * (motion + sped) + square * (pull - pull_new)
    return moved, sped


def pack_kernel(place, motion, pull, change, mass, level, out, *held):
    place_at, motion_at, pull_at, change_at, mass_at, level_at, arrived = held
    sources = (place, motion, pull, change, mass, level)
    copies = [
        pltpu.make_async_copy(source, target, arrived.at[index])
        for index, (source, target) in enumerate(zip(sources, held))
    ]
    for copy in copies:
        copy.start()
    for copy in copies:
        copy.wait()
    out[15:16, :] = jnp.zeros((1, out.shape[1]), jnp.float32)
    for part, ref in enumerate((place_at, motion_at, pull_at, change_at)):
        out[4 * part : 4 * part + 3, :] = ref[...]
    for half in range(2):
        row = slice(half, half + 1)
        at = slice(half * lanes, (half + 1) * lanes)
        out[3:4, at] = jnp.where(level_at[row, :] <= 1, mass_at[row, :], 0.0)
        out[7:8, at] = mass_at[row, :]
        out[11:12, at] = level_at[row, :].astype(jnp.float32)


def plan_kernel(own, fine, mid, every, order, meta):
    first = lax.axis_index("stars") * own
    count_fine, count_mid, count_all = fine.shape[0], mid.shape[0], every.shape[0]

    def merge(index, seen):
        star = mid[index]
        order[count_fine + index - seen] = star
        same = star == fine[jnp.minimum(seen, count_fine - 1)]
        return seen + same.astype(jnp.int32)

    lax.fori_loop(0, count_mid, merge, jnp.int32(0), unroll=8)

    def keep(index, carry):
        order[index] = fine[index]
        return carry

    lax.fori_loop(0, count_fine, keep, 0, unroll=8)

    def below(bound):
        found = jnp.int32(0)
        for bit in reversed(range(count_all.bit_length())):
            at = found + (1 << bit)
            less = (at <= count_all) & (every[jnp.minimum(at, count_all) - 1] < bound)
            found = jnp.where(less, at, found)
        return found

    low = below(first)
    meta[0] = low
    meta[1] = below(first + own) - low


def rounds_of(devices):
    bits = devices.bit_length() - 1
    assert devices == 1 << bits
    rounds = []
    high = bits
    while high > 1:
        width = 1 if high == 2 else 2
        high -= width
        rounds.append((1 << high, 1 << width))
    return rounds


def settle(value):
    return pl.pallas_call(
        lambda source, target: None,
        out_shape=jax.ShapeDtypeStruct(value.shape, value.dtype),
        in_specs=[pl.BlockSpec(memory_space=pl.ANY)],
        out_specs=pl.BlockSpec(memory_space=pl.ANY),
        input_output_aliases={0: 0},
        cost_estimate=pl.CostEstimate(flops=10**11, bytes_accessed=10**8, transcendentals=0),
        name="settle",
    )(value)


def gather(block, devices, lists, plan):
    everyone = range(devices)
    odd = lax.axis_index("stars") % 2 == 1

    def fetch(value, even_by, odd_by):
        pairs = [(device, device ^ (odd_by if device % 2 else even_by)) for device in everyone]
        return lax.ppermute(value, "stars", pairs)

    other = fetch(block, 1, 1)
    block = jnp.concatenate([jnp.where(odd, other, block), jnp.where(odd, block, other)], axis=0)
    rounds = rounds_of(devices)
    planned = None if rounds else plan(lists)
    for stride, radix in rounds:
        if stride == rounds[-1][0]:
            block, lists = lax.optimization_barrier((block, lists))
        if radix == 2:
            parts = [block, fetch(block, stride, stride)]
        else:
            one = fetch(block, stride, 3 * stride)
            two = settle(fetch(block, 2 * stride, 2 * stride))
            swapped = fetch(one, 1, 1)
            parts = [block, jnp.where(odd, swapped, one), two, jnp.where(odd, one, swapped)]
        if stride == rounds[-1][0]:
            planned = plan(lists)
        block = jnp.concatenate(parts, axis=0)
    return block, planned


def slot_of(device, me, devices):
    slot, held = device % 2, 2
    for stride, radix in rounds_of(devices):
        slot = slot + (device ^ me) // stride % radix * held
        held *= radix
    return slot


def pair_terms(target, field, total):
    apart = [field[index] - target[index] for index in range(3)]
    closing = [field[3 + index] - target[3 + index] for index in range(3)]
    distance = apart[0] * apart[0] + apart[1] * apart[1] + (apart[2] * apart[2] + softening)
    inverse = lax.rsqrt(distance)
    square = inverse * inverse
    weight = field[6] * inverse * square
    dot = apart[0] * closing[0] + apart[1] * closing[1] + apart[2] * closing[2]
    rate = 3.0 * dot * square
    pulled = [weight * apart[index] for index in range(3)]
    return [total[index] + pulled[index] for index in range(3)] + [
        total[3 + index] + (weight * closing[index] - rate * pulled[index]) for index in range(3)
    ]


def main_kernel(
    devices,
    own_count,
    sizes,
    order,
    every,
    meta,
    field,
    out_place,
    out_motion,
    out_pull,
    out_change,
    ahead,
    slab,
    table,
    names,
    guess,
    mid_field,
    mid_state,
    mid_names,
    result,
):
    count_fine, count_mid, count_all = sizes
    blocks, blocks_fine = count_mid // 8, count_fine // 8
    groups = mid_field.shape[0]
    sub = lax.broadcasted_iota(jnp.int32, (8, lanes), 0)
    lane = lax.broadcasted_iota(jnp.int32, (8, lanes), 1)

    def spread(column):
        return jnp.broadcast_to(column, (8, lanes))

    def lane_total(value):
        return spread(jnp.sum(value, axis=1, keepdims=True))

    def loop(count, body):
        if count <= 4:
            for index in range(count):
                body(index)
        else:
            pl.loop(0, count)(body)

    def rows8(index):
        return pl.ds(index * 8 if isinstance(index, int) else pl.multiple_of(index * 8, 8), 8)

    halves = [slice(0, lanes), slice(lanes, 2 * lanes)]
    me = lax.axis_index("stars")
    first = me * own_count

    def look_ahead(index):
        for half in range(2):
            upper = field[pl.ds(pl.multiple_of(index * 16, 16), 8), halves[half]]
            lower = field[pl.ds(pl.multiple_of(index * 16 + 8, 8), 8), halves[half]]
            turned = pltpu.roll(lower, 4, 0)
            slope = jnp.where(sub < 4, pltpu.roll(upper, 4, 0), turned)
            bend = 0.5 * lower
            twist = jnp.where(sub < 4, turned * (1.0 / 6.0), 0.0)
            for step in range(4):
                time = (step + 1) * unit
                moved = upper + time * (slope + time * (bend + time * twist))
                ahead[step, index * 2 + half] = jnp.where(sub == 3, upper, moved)

    together = min(4, devices)

    @pl.loop(0, devices // together)
    def _(index):
        for inner in range(together):
            look_ahead(index * together + inner)

    low, count = meta[0], meta[1]

    mine = pl.multiple_of(slot_of(me, me, devices) * 16, 16)

    def own(part, component, half):
        tile = field[pl.ds(pl.multiple_of(mine + part // 2 * 8, 8), 8), halves[half]]
        at = part % 2 * 4 + component
        return tile[at : at + 1, :]

    def fetch(block):
        name = jnp.zeros((8, lanes), jnp.int32)
        for row in range(8):
            star = order[block * 8 + row]
            base = pl.multiple_of(slot_of(star // own_count, me, devices) * 16, 16)
            side = pl.multiple_of(star % own_count // lanes * lanes, lanes)
            slab[16 * row : 16 * row + 16, :] = field[pl.ds(base, 16), pl.ds(side, lanes)]
            name = jnp.where(sub == row, star, name)
        names[rows8(block), :] = name
        hit = (name % lanes) == lane
        for part in range(4):
            for component in range(3):
                value = slab[pl.ds(4 * part + component, 8, stride=16), :]
                table[3 * part + component, rows8(block), :] = lane_total(jnp.where(hit, value, 0.0))
        mass = slab[pl.ds(7, 8, stride=16), :]
        table[12, rows8(block), :] = lane_total(jnp.where(hit, mass, 0.0))

    loop(blocks, fetch)
    level = [own(2, 3, half) for half in range(2)]

    def turn(ref, group, *at):
        total = jnp.zeros((8, lanes), ref.dtype)
        for inner in range(min(16, blocks)):
            value = ref[(*at, rows8(group * 16 + inner), slice(None))]
            total = total + jnp.where(lane == sub + inner * 8, value, jnp.zeros_like(value))
        return jnp.sum(total, axis=0, keepdims=True)

    def fixed(group):
        mid_field[group, 6:7, :] = turn(table, group, 12)
        found = turn(names, group)
        if blocks * 8 < lanes:
            found = jnp.where(lane[0:1, :] < blocks * 8, found, -1)
        mid_names[group, 0:1, :] = found

    loop(groups, fixed)

    def elapse_of(step, fine):
        return unit * (1 if fine or step % 2 == 0 else 2)

    def guess_block(step, fine, block):
        state = [table[index, rows8(block), :] for index in range(12)]
        elapse = elapse_of(step, fine)
        for index in range(3):
            moved, sped = predict(
                state[index], state[3 + index], state[6 + index], state[9 + index], elapse
            )
            guess[index, rows8(block), :] = moved
            guess[3 + index, rows8(block), :] = sped

    def place_mid(group):
        for index in range(6):
            mid_field[group, index : index + 1, :] = turn(guess, group, index)

    def force(step, targets):
        def add(totals, row):
            return [pair_terms(target, row, total) for target, total in zip(targets, totals)]

        def one(index, totals):
            for half in range(2):
                row = [ahead[step, index * 2 + half, k : k + 1, :] for k in (0, 1, 2, 4, 5, 6, 3)]
                totals = add(totals, row)
            return totals

        together = min(8, devices)

        def some(index, totals):
            for inner in range(together):
                totals = one(index * together + inner, totals)
            return totals

        zero = jnp.zeros((8, lanes), jnp.float32)
        totals = [[zero] * 6 for _ in targets]
        for group in range(groups):
            totals = add(totals, [mid_field[group, k : k + 1, :] for k in range(7)])
        totals = lax.fori_loop(0, devices // together, some, totals)
        return [[lane_total(value) for value in total] for total in totals]

    for step in range(4):
        loop(blocks_fine, functools.partial(guess_block, step, True))
        loop(blocks - blocks_fine, lambda block: guess_block(step, False, block + blocks_fine))
        loop(groups, place_mid)
        if step == 3:
            break

        def advance(pair, step, fine):
            targets = [
                [guess[index, rows8(2 * pair + side), :] for index in range(6)] for side in range(2)
            ]
            elapse = elapse_of(step, fine)
            for side, total in enumerate(force(step, targets)):
                rows = rows8(2 * pair + side)
                for index in range(3):
                    moved, sped = correct(
                        *[table[3 * part + index, rows, :] for part in range(4)],
                        total[index],
                        total[3 + index],
                        elapse,
                    )
                    table[index, rows, :] = moved
                    table[3 + index, rows, :] = sped
                    table[6 + index, rows, :] = total[index]
                    table[9 + index, rows, :] = total[3 + index]

        loop(blocks_fine // 2, functools.partial(advance, step=step, fine=True))
        if step == 1:
            loop(
                (blocks - blocks_fine) // 2,
                lambda pair: advance(pair + blocks_fine // 2, step=1, fine=False),
            )

    def keep(group):
        for index in range(12):
            mid_state[group, index : index + 1, :] = turn(table, group, index)

    loop(groups, keep)
    result[...] = jnp.zeros_like(result)

    def finish(wide, turn_at):
        hits, states, elapses, targets = [], [], [], []
        for side in range(wide):
            name = jnp.full((8, lanes), -1, jnp.int32)
            for row in range(8):
                at = (turn_at * wide + side) * 8 + row
                star = every[jnp.minimum(low + at, count_all - 1)]
                name = jnp.where((sub == row) & (at < count), star, name)
            own_hit = [name == lane + (first + half * lanes) for half in range(2)]
            coarse = [own_hit[half] & (level[half] == 1.0) for half in range(2)]
            mid_hit = [name == mid_names[group, 0:1, :] for group in range(groups)]

            def find(part, component):
                total = jnp.zeros((8, lanes), jnp.float32)
                for half in range(2):
                    total = jnp.where(coarse[half], own(part, component, half), total)
                for group in range(groups):
                    at = 3 * part + component
                    total = jnp.where(mid_hit[group], mid_state[group, at : at + 1, :], total)
                return lane_total(total)

            total = jnp.zeros((8, lanes), jnp.float32)
            for half in range(2):
                total = jnp.where(coarse[half], 4 * unit, total)
            for group in range(groups):
                fine = jnp.where(lane + group * lanes < count_fine, unit, 2 * unit)
                total = jnp.where(mid_hit[group], fine, total)
            elapse = lane_total(total)
            state = [[find(part, index) for index in range(3)] for part in range(4)]
            pairs = [
                predict(*[state[part][index] for part in range(4)], elapse) for index in range(3)
            ]
            hits.append(own_hit)
            states.append(state)
            elapses.append(elapse)
            targets.append([pair[0] for pair in pairs] + [pair[1] for pair in pairs])
        for side, total in enumerate(force(3, targets)):
            for index in range(3):
                moved, sped = correct(
                    *[states[side][part][index] for part in range(4)],
                    total[index],
                    total[3 + index],
                    elapses[side],
                )
                for part, value in enumerate((moved, sped, total[index], total[3 + index])):
                    for half in range(2):
                        result[part, half, index] += jnp.where(hits[side][half], value, 0.0)

    @pl.when((count > 0) & (count <= 16))
    def _():
        finish(2, 0)

    @pl.when(count > 16)
    def _():
        pl.loop(0, (count + 23) // 24)(functools.partial(finish, 3))

    for part, ref in enumerate((out_place, out_motion, out_pull, out_change)):
        for half in range(2):
            changed = level[half] >= 1.0
            for index in range(3):
                value = jnp.sum(result[part, half, index], axis=0, keepdims=True)
                ref[index : index + 1, halves[half]] = jnp.where(
                    changed, value, own(part, index, half)
                )


def body(devices, place, motion, pull, change, masses, star_level, fine, mid, every):
    own_count = place.shape[1]
    sizes = (fine.shape[0], mid.shape[0], every.shape[0])
    groups = -(-sizes[1] // lanes)
    held = [pltpu.VMEM((3, own_count), jnp.float32)] * 4
    held += [pltpu.VMEM((2, lanes), jnp.float32), pltpu.VMEM((2, lanes), jnp.int32)]
    block = pl.pallas_call(
        pack_kernel,
        out_shape=jax.ShapeDtypeStruct((16, own_count), jnp.float32),
        in_specs=[pl.BlockSpec(memory_space=pl.ANY)] * 6,
        out_specs=vmem,
        scratch_shapes=held + [pltpu.SemaphoreType.DMA((6,))],
        name="pack",
    )(place, motion, pull, change, masses.reshape(2, lanes), star_level.reshape(2, lanes))

    def plan(lists):
        return pl.pallas_call(
            functools.partial(plan_kernel, own_count),
            out_shape=(
                jax.ShapeDtypeStruct((sizes[1] + 8,), jnp.int32),
                jax.ShapeDtypeStruct((2,), jnp.int32),
            ),
            in_specs=[smem] * 3,
            out_specs=(smem, smem),
            name="plan",
        )(*lists)

    whole, (order, meta) = gather(block, devices, (fine, mid, every), plan)
    room = devices * 52 * 1024 + sizes[1] * 12 * 1024 + 3 * 1024 * 1024
    result = jax.ShapeDtypeStruct((3, own_count), jnp.float32)
    return pl.pallas_call(
        functools.partial(main_kernel, devices, own_count, sizes),
        out_shape=(result,) * 4,
        in_specs=[smem] * 3 + [vmem],
        out_specs=(vmem,) * 4,
        scratch_shapes=[
            pltpu.VMEM((4, devices * 2, 8, lanes), jnp.float32),
            pltpu.VMEM((8 * 16, lanes), jnp.float32),
            pltpu.VMEM((13, sizes[1], lanes), jnp.float32),
            pltpu.VMEM((sizes[1], lanes), jnp.int32),
            pltpu.VMEM((6, sizes[1], lanes), jnp.float32),
            pltpu.VMEM((groups, 8, lanes), jnp.float32),
            pltpu.VMEM((groups, 16, lanes), jnp.float32),
            pltpu.VMEM((groups, 8, lanes), jnp.int32),
            pltpu.VMEM((4, 2, 3, 8, lanes), jnp.float32),
        ],
        compiler_params=pltpu.CompilerParams(vmem_limit_bytes=room),
        name="steps",
    )(order, every, meta, whole)


def solution(mesh):
    split = P(None, "stars")
    return jax.shard_map(
        functools.partial(body, mesh.shape["stars"]),
        mesh=mesh,
        in_specs=(split,) * 4 + (P("stars"),) * 2 + (P(),) * 3,
        out_specs=(split,) * 4,
        check_vma=False,
    )
```

```python
import functools

import jax
import jax.numpy as jnp
from jax import lax
from jax.experimental import pallas as pl
from jax.experimental.pallas import tpu as pltpu
from jax.sharding import PartitionSpec as P

softening = 0.0001
unit = 1.0 / 128.0
lanes = 128
vmem = pl.BlockSpec(memory_space=pltpu.VMEM)
smem = pl.BlockSpec(memory_space=pltpu.SMEM)


def predict(place, motion, pull, change, elapse):
    moved = place + elapse * (motion + elapse * (0.5 * pull + elapse * change * (1.0 / 6.0)))
    sped = motion + elapse * (pull + 0.5 * elapse * change)
    return moved, sped


def correct(place, motion, pull, change, pull_new, change_new, elapse):
    square = elapse * elapse * (1.0 / 12.0)
    sped = motion + 0.5 * elapse * (pull + pull_new) + square * (change - change_new)
    moved = place + 0.5 * elapse * (motion + sped) + square * (pull - pull_new)
    return moved, sped


def pack_kernel(place, motion, pull, change, mass, level, out, *held):
    place_at, motion_at, pull_at, change_at, mass_at, level_at, arrived = held
    sources = (place, motion, pull, change, mass, level)
    copies = [
        pltpu.make_async_copy(source, target, arrived.at[index])
        for index, (source, target) in enumerate(zip(sources, held))
    ]
    for copy in copies:
        copy.start()
    for copy in copies:
        copy.wait()
    out[15:16, :] = jnp.zeros((1, out.shape[1]), jnp.float32)
    for part, ref in enumerate((place_at, motion_at, pull_at, change_at)):
        out[4 * part : 4 * part + 3, :] = ref[...]
    for half in range(2):
        row = slice(half, half + 1)
        at = slice(half * lanes, (half + 1) * lanes)
        out[3:4, at] = jnp.where(level_at[row, :] <= 1, mass_at[row, :], 0.0)
        out[7:8, at] = mass_at[row, :]
        out[11:12, at] = level_at[row, :].astype(jnp.float32)


def plan_kernel(own, fine, mid, every, listed):
    first = lax.axis_index("stars") * own
    count_fine, count_mid, count_all = fine.shape[0], mid.shape[0], every.shape[0]
    order = 2 + count_all

    def merge(index, seen):
        star = mid[index]
        listed[order + count_fine + index - seen] = star
        same = star == fine[jnp.minimum(seen, count_fine - 1)]
        return seen + same.astype(jnp.int32)

    lax.fori_loop(0, count_mid, merge, jnp.int32(0), unroll=8)

    def keep(source, start):
        def one(index, carry):
            listed[start + index] = source[index]
            return carry

        lax.fori_loop(0, source.shape[0], one, 0, unroll=8)

    keep(fine, order)
    keep(every, 2)

    def below(bound):
        found = jnp.int32(0)
        for bit in reversed(range(count_all.bit_length())):
            at = found + (1 << bit)
            less = (at <= count_all) & (every[jnp.minimum(at, count_all) - 1] < bound)
            found = jnp.where(less, at, found)
        return found

    low = below(first)
    listed[0] = low
    listed[1] = below(first + own) - low


def rounds_of(devices):
    bits = devices.bit_length() - 1
    assert devices == 1 << bits
    rounds = []
    high = bits
    while high > 1:
        width = 1 if high == 2 else 2
        high -= width
        rounds.append((1 << high, 1 << width))
    return rounds


def settle(value):
    return pl.pallas_call(
        lambda source, target: None,
        out_shape=jax.ShapeDtypeStruct(value.shape, value.dtype),
        in_specs=[pl.BlockSpec(memory_space=pl.ANY)],
        out_specs=pl.BlockSpec(memory_space=pl.ANY),
        input_output_aliases={0: 0},
        cost_estimate=pl.CostEstimate(flops=10**11, bytes_accessed=10**8, transcendentals=0),
        compiler_params=pltpu.CompilerParams(vmem_limit_bytes=1024 * 1024),
        name="settle",
    )(value)


def gather(block, devices, lists, plan):
    everyone = range(devices)
    odd = lax.axis_index("stars") % 2 == 1

    def fetch(value, even_by, odd_by):
        pairs = [(device, device ^ (odd_by if device % 2 else even_by)) for device in everyone]
        return lax.ppermute(value, "stars", pairs)

    def both(mine, other):
        return [jnp.where(odd, other, mine), jnp.where(odd, mine, other)]

    block = jnp.concatenate(both(block, fetch(block, 1, 1)), axis=0)
    rounds = rounds_of(devices)
    planned = None if rounds else plan(lists)
    for stride, radix in rounds:
        last = stride == rounds[-1][0]
        if last:
            block, lists = lax.optimization_barrier((block, lists))
            planned = plan(lists)
        if radix == 2:
            parts = [block, fetch(block, stride, stride)]
        elif last:
            half = block.shape[0] // 2
            one = fetch(block, stride, 2 * stride)
            two = jnp.where(odd, block[half:], block[:half])
            two = settle(fetch(two, 3 * stride, 3 * stride))
            parts = [block] + both(one, fetch(one, 1, 1)) + both(two, fetch(two, 1, 1))
        else:
            one = fetch(block, stride, 3 * stride)
            two = settle(fetch(block, 2 * stride, 2 * stride))
            near, far = both(one, fetch(one, 1, 1))
            parts = [block, near, two, far]
        block = jnp.concatenate(parts, axis=0)
    return block, planned


def slot_of(device, me, devices):
    slot, held = device % 2, 2
    for stride, radix in rounds_of(devices):
        slot = slot + (device ^ me) // stride % radix * held
        held *= radix
    return slot


def pair_terms(target, field, total):
    apart = [field[index] - target[index] for index in range(3)]
    closing = [field[3 + index] - target[3 + index] for index in range(3)]
    distance = apart[0] * apart[0] + apart[1] * apart[1] + (apart[2] * apart[2] + softening)
    inverse = lax.rsqrt(distance)
    square = inverse * inverse
    weight = field[6] * inverse * square
    dot = apart[0] * closing[0] + apart[1] * closing[1] + apart[2] * closing[2]
    rate = 3.0 * dot * square
    pulled = [weight * apart[index] for index in range(3)]
    return [total[index] + pulled[index] for index in range(3)] + [
        total[3 + index] + (weight * closing[index] - rate * pulled[index]) for index in range(3)
    ]


def main_kernel(
    devices,
    own_count,
    sizes,
    listed,
    field,
    out_place,
    out_motion,
    out_pull,
    out_change,
    ahead,
    slab,
    table,
    names,
    guess,
    mid_field,
    mid_state,
    mid_names,
    result,
):
    count_fine, count_mid, count_all = sizes
    blocks, blocks_fine = count_mid // 8, count_fine // 8
    groups = mid_field.shape[0]
    sub = lax.broadcasted_iota(jnp.int32, (8, lanes), 0)
    lane = lax.broadcasted_iota(jnp.int32, (8, lanes), 1)

    def spread(column):
        return jnp.broadcast_to(column, (8, lanes))

    def lane_total(value):
        return spread(jnp.sum(value, axis=1, keepdims=True))

    def loop(count, body):
        if count <= 4:
            for index in range(count):
                body(index)
        else:
            pl.loop(0, count)(body)

    def rows8(index):
        return pl.ds(index * 8 if isinstance(index, int) else pl.multiple_of(index * 8, 8), 8)

    halves = [slice(0, lanes), slice(lanes, 2 * lanes)]
    me = lax.axis_index("stars")
    first = me * own_count

    def look_ahead(index):
        for half in range(2):
            upper = field[pl.ds(pl.multiple_of(index * 16, 16), 8), halves[half]]
            lower = field[pl.ds(pl.multiple_of(index * 16 + 8, 8), 8), halves[half]]
            turned = pltpu.roll(lower, 4, 0)
            slope = jnp.where(sub < 4, pltpu.roll(upper, 4, 0), turned)
            bend = 0.5 * lower
            twist = jnp.where(sub < 4, turned * (1.0 / 6.0), 0.0)
            for step in range(4):
                time = (step + 1) * unit
                moved = upper + time * (slope + time * (bend + time * twist))
                ahead[step, index * 2 + half] = jnp.where(sub == 3, upper, moved)

    together = min(4, devices)

    @pl.loop(0, devices // together)
    def _(index):
        for inner in range(together):
            look_ahead(index * together + inner)

    low, count = listed[0], listed[1]

    mine = pl.multiple_of(slot_of(me, me, devices) * 16, 16)

    def own(part, component, half):
        tile = field[pl.ds(pl.multiple_of(mine + part // 2 * 8, 8), 8), halves[half]]
        at = part % 2 * 4 + component
        return tile[at : at + 1, :]

    def fetch(block):
        name = jnp.zeros((8, lanes), jnp.int32)
        for row in range(8):
            star = listed[2 + count_all + block * 8 + row]
            base = pl.multiple_of(slot_of(star // own_count, me, devices) * 16, 16)
            side = pl.multiple_of(star % own_count // lanes * lanes, lanes)
            slab[16 * row : 16 * row + 16, :] = field[pl.ds(base, 16), pl.ds(side, lanes)]
            name = jnp.where(sub == row, star, name)
        names[rows8(block), :] = name
        hit = (name % lanes) == lane
        for part in range(4):
            for component in range(3):
                value = slab[pl.ds(4 * part + component, 8, stride=16), :]
                table[3 * part + component, rows8(block), :] = lane_total(jnp.where(hit, value, 0.0))
        mass = slab[pl.ds(7, 8, stride=16), :]
        table[12, rows8(block), :] = lane_total(jnp.where(hit, mass, 0.0))

    loop(blocks, fetch)
    level = [own(2, 3, half) for half in range(2)]

    def turn(ref, group, *at):
        total = jnp.zeros((8, lanes), ref.dtype)
        for inner in range(min(16, blocks)):
            value = ref[(*at, rows8(group * 16 + inner), slice(None))]
            total = total + jnp.where(lane == sub + inner * 8, value, jnp.zeros_like(value))
        return jnp.sum(total, axis=0, keepdims=True)

    def fixed(group):
        mid_field[group, 6:7, :] = turn(table, group, 12)
        found = turn(names, group)
        if blocks * 8 < lanes:
            found = jnp.where(lane[0:1, :] < blocks * 8, found, -1)
        mid_names[group, 0:1, :] = found

    loop(groups, fixed)

    def elapse_of(step, fine):
        return unit * (1 if fine or step % 2 == 0 else 2)

    def guess_block(step, fine, block):
        state = [table[index, rows8(block), :] for index in range(12)]
        elapse = elapse_of(step, fine)
        for index in range(3):
            moved, sped = predict(
                state[index], state[3 + index], state[6 + index], state[9 + index], elapse
            )
            guess[index, rows8(block), :] = moved
            guess[3 + index, rows8(block), :] = sped

    def place_mid(group):
        for index in range(6):
            mid_field[group, index : index + 1, :] = turn(guess, group, index)

    def force(step, targets):
        def add(totals, row):
            return [pair_terms(target, row, total) for target, total in zip(targets, totals)]

        def one(index, totals):
            for half in range(2):
                row = [ahead[step, index * 2 + half, k : k + 1, :] for k in (0, 1, 2, 4, 5, 6, 3)]
                totals = add(totals, row)
            return totals

        together = min(8, devices)

        def some(index, totals):
            for inner in range(together):
                totals = one(index * together + inner, totals)
            return totals

        zero = jnp.zeros((8, lanes), jnp.float32)
        totals = [[zero] * 6 for _ in targets]
        for group in range(groups):
            totals = add(totals, [mid_field[group, k : k + 1, :] for k in range(7)])
        totals = lax.fori_loop(0, devices // together, some, totals)
        return [[lane_total(value) for value in total] for total in totals]

    for step in range(4):
        loop(blocks_fine, functools.partial(guess_block, step, True))
        loop(blocks - blocks_fine, lambda block: guess_block(step, False, block + blocks_fine))
        loop(groups, place_mid)
        if step == 3:
            break

        def advance(pair, step, fine):
            targets = [
                [guess[index, rows8(2 * pair + side), :] for index in range(6)] for side in range(2)
            ]
            elapse = elapse_of(step, fine)
            for side, total in enumerate(force(step, targets)):
                rows = rows8(2 * pair + side)
                for index in range(3):
                    moved, sped = correct(
                        *[table[3 * part + index, rows, :] for part in range(4)],
                        total[index],
                        total[3 + index],
                        elapse,
                    )
                    table[index, rows, :] = moved
                    table[3 + index, rows, :] = sped
                    table[6 + index, rows, :] = total[index]
                    table[9 + index, rows, :] = total[3 + index]

        loop(blocks_fine // 2, functools.partial(advance, step=step, fine=True))
        if step == 1:
            loop(
                (blocks - blocks_fine) // 2,
                lambda pair: advance(pair + blocks_fine // 2, step=1, fine=False),
            )

    def keep(group):
        for index in range(12):
            mid_state[group, index : index + 1, :] = turn(table, group, index)

    loop(groups, keep)
    result[...] = jnp.zeros_like(result)

    def finish(wide, turn_at):
        hits, states, elapses, targets = [], [], [], []
        for side in range(wide):
            name = jnp.full((8, lanes), -1, jnp.int32)
            for row in range(8):
                at = (turn_at * wide + side) * 8 + row
                star = listed[2 + jnp.minimum(low + at, count_all - 1)]
                name = jnp.where((sub == row) & (at < count), star, name)
            own_hit = [name == lane + (first + half * lanes) for half in range(2)]
            coarse = [own_hit[half] & (level[half] == 1.0) for half in range(2)]
            mid_hit = [name == mid_names[group, 0:1, :] for group in range(groups)]

            def find(part, component):
                total = jnp.zeros((8, lanes), jnp.float32)
                for half in range(2):
                    total = jnp.where(coarse[half], own(part, component, half), total)
                for group in range(groups):
                    at = 3 * part + component
                    total = jnp.where(mid_hit[group], mid_state[group, at : at + 1, :], total)
                return lane_total(total)

            total = jnp.zeros((8, lanes), jnp.float32)
            for half in range(2):
                total = jnp.where(coarse[half], 4 * unit, total)
            for group in range(groups):
                fine = jnp.where(lane + group * lanes < count_fine, unit, 2 * unit)
                total = jnp.where(mid_hit[group], fine, total)
            elapse = lane_total(total)
            state = [[find(part, index) for index in range(3)] for part in range(4)]
            pairs = [
                predict(*[state[part][index] for part in range(4)], elapse) for index in range(3)
            ]
            hits.append(own_hit)
            states.append(state)
            elapses.append(elapse)
            targets.append([pair[0] for pair in pairs] + [pair[1] for pair in pairs])
        for side, total in enumerate(force(3, targets)):
            for index in range(3):
                moved, sped = correct(
                    *[states[side][part][index] for part in range(4)],
                    total[index],
                    total[3 + index],
                    elapses[side],
                )
                for part, value in enumerate((moved, sped, total[index], total[3 + index])):
                    for half in range(2):
                        result[part, half, index] += jnp.where(hits[side][half], value, 0.0)

    @pl.when((count > 0) & (count <= 16))
    def _():
        finish(2, 0)

    @pl.when(count > 16)
    def _():
        pl.loop(0, (count + 23) // 24)(functools.partial(finish, 3))

    for part, ref in enumerate((out_place, out_motion, out_pull, out_change)):
        for half in range(2):
            changed = level[half] >= 1.0
            for index in range(3):
                value = jnp.sum(result[part, half, index], axis=0, keepdims=True)
                ref[index : index + 1, halves[half]] = jnp.where(
                    changed, value, own(part, index, half)
                )


def body(devices, place, motion, pull, change, masses, star_level, fine, mid, every):
    own_count = place.shape[1]
    sizes = (fine.shape[0], mid.shape[0], every.shape[0])
    groups = -(-sizes[1] // lanes)
    held = [pltpu.VMEM((3, own_count), jnp.float32)] * 4
    held += [pltpu.VMEM((2, lanes), jnp.float32), pltpu.VMEM((2, lanes), jnp.int32)]
    block = pl.pallas_call(
        pack_kernel,
        out_shape=jax.ShapeDtypeStruct((16, own_count), jnp.float32),
        in_specs=[pl.BlockSpec(memory_space=pl.ANY)] * 6,
        out_specs=vmem,
        scratch_shapes=held + [pltpu.SemaphoreType.DMA((6,))],
        name="pack",
    )(place, motion, pull, change, masses.reshape(2, lanes), star_level.reshape(2, lanes))

    def plan(lists):
        return pl.pallas_call(
            functools.partial(plan_kernel, own_count),
            out_shape=jax.ShapeDtypeStruct((2 + sizes[2] + sizes[1] + 6,), jnp.int32),
            in_specs=[smem] * 3,
            out_specs=smem,
            compiler_params=pltpu.CompilerParams(vmem_limit_bytes=1024 * 1024),
            name="plan",
        )(*lists)

    whole, listed = gather(block, devices, (fine, mid, every), plan)
    room = devices * 52 * 1024 + sizes[1] * 12 * 1024 + 3 * 1024 * 1024
    result = jax.ShapeDtypeStruct((3, own_count), jnp.float32)
    return pl.pallas_call(
        functools.partial(main_kernel, devices, own_count, sizes),
        out_shape=(result,) * 4,
        in_specs=[smem, vmem],
        out_specs=(vmem,) * 4,
        scratch_shapes=[
            pltpu.VMEM((4, devices * 2, 8, lanes), jnp.float32),
            pltpu.VMEM((8 * 16, lanes), jnp.float32),
            pltpu.VMEM((13, sizes[1], lanes), jnp.float32),
            pltpu.VMEM((sizes[1], lanes), jnp.int32),
            pltpu.VMEM((6, sizes[1], lanes), jnp.float32),
            pltpu.VMEM((groups, 8, lanes), jnp.float32),
            pltpu.VMEM((groups, 16, lanes), jnp.float32),
            pltpu.VMEM((groups, 8, lanes), jnp.int32),
            pltpu.VMEM((4, 2, 3, 8, lanes), jnp.float32),
        ],
        compiler_params=pltpu.CompilerParams(vmem_limit_bytes=room),
        name="steps",
    )(listed, whole)


def solution(mesh):
    split = P(None, "stars")
    return jax.shard_map(
        functools.partial(body, mesh.shape["stars"]),
        mesh=mesh,
        in_specs=(split,) * 4 + (P("stars"),) * 2 + (P(),) * 3,
        out_specs=(split,) * 4,
        check_vma=False,
    )
```

```python
import functools

import jax
import jax.numpy as jnp
from jax import lax
from jax.experimental import pallas as pl
from jax.experimental.pallas import tpu as pltpu
from jax.sharding import PartitionSpec as P

softening = 0.0001
unit = 1.0 / 128.0
lanes = 128
vmem = pl.BlockSpec(memory_space=pltpu.VMEM)
smem = pl.BlockSpec(memory_space=pltpu.SMEM)


def predict(place, motion, pull, change, elapse):
    moved = place + elapse * (motion + elapse * (0.5 * pull + elapse * change * (1.0 / 6.0)))
    sped = motion + elapse * (pull + 0.5 * elapse * change)
    return moved, sped


def correct(place, motion, pull, change, pull_new, change_new, elapse):
    square = elapse * elapse * (1.0 / 12.0)
    sped = motion + 0.5 * elapse * (pull + pull_new) + square * (change - change_new)
    moved = place + 0.5 * elapse * (motion + sped) + square * (pull - pull_new)
    return moved, sped


def pack_kernel(place, motion, pull, change, mass, level, out, *held):
    place_at, motion_at, pull_at, change_at, mass_at, level_at, arrived = held
    sources = (place, motion, pull, change, mass, level)
    copies = [
        pltpu.make_async_copy(source, target, arrived.at[index])
        for index, (source, target) in enumerate(zip(sources, held))
    ]
    for copy in copies:
        copy.start()
    for copy in copies:
        copy.wait()
    out[15:16, :] = jnp.zeros((1, out.shape[1]), jnp.float32)
    for part, ref in enumerate((place_at, motion_at, pull_at, change_at)):
        out[4 * part : 4 * part + 3, :] = ref[...]
    for half in range(2):
        row = slice(half, half + 1)
        at = slice(half * lanes, (half + 1) * lanes)
        out[3:4, at] = jnp.where(level_at[row, :] <= 1, mass_at[row, :], 0.0)
        out[7:8, at] = mass_at[row, :]
        out[11:12, at] = level_at[row, :].astype(jnp.float32)


def plan_kernel(own, fine, mid, every, listed):
    first = lax.axis_index("stars") * own
    count_fine, count_mid, count_all = fine.shape[0], mid.shape[0], every.shape[0]
    order = 2 + count_all

    def merge(index, seen):
        star = mid[index]
        listed[order + count_fine + index - seen] = star
        same = star == fine[jnp.minimum(seen, count_fine - 1)]
        return seen + same.astype(jnp.int32)

    lax.fori_loop(0, count_mid, merge, jnp.int32(0), unroll=8)

    def keep(source, start):
        def one(index, carry):
            listed[start + index] = source[index]
            return carry

        lax.fori_loop(0, source.shape[0], one, 0, unroll=8)

    keep(fine, order)
    keep(every, 2)

    def below(bound):
        found = jnp.int32(0)
        for bit in reversed(range(count_all.bit_length())):
            at = found + (1 << bit)
            less = (at <= count_all) & (every[jnp.minimum(at, count_all) - 1] < bound)
            found = jnp.where(less, at, found)
        return found

    low = below(first)
    listed[0] = low
    listed[1] = below(first + own) - low


def rounds_of(devices):
    bits = devices.bit_length() - 1
    assert devices == 1 << bits
    rounds = []
    high = bits
    while high > 1:
        width = 1 if high == 2 else 2
        high -= width
        rounds.append((1 << high, 1 << width))
    return rounds


def settle(value):
    return pl.pallas_call(
        lambda source, target: None,
        out_shape=jax.ShapeDtypeStruct(value.shape, value.dtype),
        in_specs=[pl.BlockSpec(memory_space=pl.ANY)],
        out_specs=pl.BlockSpec(memory_space=pl.ANY),
        input_output_aliases={0: 0},
        cost_estimate=pl.CostEstimate(flops=10**11, bytes_accessed=10**8, transcendentals=0),
        compiler_params=pltpu.CompilerParams(vmem_limit_bytes=1024 * 1024),
        name="settle",
    )(value)


def gather(block, devices, lists, plan):
    everyone = range(devices)
    odd = lax.axis_index("stars") % 2 == 1

    def fetch(value, even_by, odd_by):
        pairs = [(device, device ^ (odd_by if device % 2 else even_by)) for device in everyone]
        return lax.ppermute(value, "stars", pairs)

    def both(mine, other):
        return [jnp.where(odd, other, mine), jnp.where(odd, mine, other)]

    block = jnp.concatenate(both(block, fetch(block, 1, 1)), axis=0)
    rounds = rounds_of(devices)
    planned = None if rounds else plan(lists)
    for stride, radix in rounds:
        last = stride == rounds[-1][0]
        if last:
            block, lists = lax.optimization_barrier((block, lists))
            planned = plan(lists)
        if radix == 2:
            parts = [block, fetch(block, stride, stride)]
        elif last:
            half = block.shape[0] // 2
            one = fetch(block, stride, 2 * stride)
            two = jnp.where(odd, block[half:], block[:half])
            two = settle(fetch(two, 3 * stride, 3 * stride))
            parts = [block] + both(one, fetch(one, 1, 1)) + both(two, fetch(two, 1, 1))
        else:
            one = fetch(block, 2 * stride, 3 * stride)
            near = settle(fetch(block, stride, stride))
            parts = [block, near] + both(one, fetch(one, 1, 1))
        block = jnp.concatenate(parts, axis=0)
    return block, planned


def slot_of(device, me, devices):
    slot, held = device % 2, 2
    for stride, radix in rounds_of(devices):
        slot = slot + (device ^ me) // stride % radix * held
        held *= radix
    return slot


def pair_terms(target, field, total):
    apart = [field[index] - target[index] for index in range(3)]
    closing = [field[3 + index] - target[3 + index] for index in range(3)]
    distance = apart[0] * apart[0] + apart[1] * apart[1] + (apart[2] * apart[2] + softening)
    inverse = lax.rsqrt(distance)
    square = inverse * inverse
    weight = field[6] * inverse * square
    dot = apart[0] * closing[0] + apart[1] * closing[1] + apart[2] * closing[2]
    rate = 3.0 * dot * square
    pulled = [weight * apart[index] for index in range(3)]
    return [total[index] + pulled[index] for index in range(3)] + [
        total[3 + index] + (weight * closing[index] - rate * pulled[index]) for index in range(3)
    ]


def main_kernel(
    devices,
    own_count,
    sizes,
    listed,
    field,
    out_place,
    out_motion,
    out_pull,
    out_change,
    ahead,
    slab,
    table,
    names,
    guess,
    mid_field,
    mid_state,
    mid_names,
    result,
):
    count_fine, count_mid, count_all = sizes
    blocks, blocks_fine = count_mid // 8, count_fine // 8
    groups = mid_field.shape[0]
    sub = lax.broadcasted_iota(jnp.int32, (8, lanes), 0)
    lane = lax.broadcasted_iota(jnp.int32, (8, lanes), 1)

    def spread(column):
        return jnp.broadcast_to(column, (8, lanes))

    def lane_total(value):
        return spread(jnp.sum(value, axis=1, keepdims=True))

    def loop(count, body):
        if count <= 4:
            for index in range(count):
                body(index)
        else:
            pl.loop(0, count)(body)

    def rows8(index):
        return pl.ds(index * 8 if isinstance(index, int) else pl.multiple_of(index * 8, 8), 8)

    halves = [slice(0, lanes), slice(lanes, 2 * lanes)]
    me = lax.axis_index("stars")
    first = me * own_count

    def look_ahead(index):
        for half in range(2):
            upper = field[pl.ds(pl.multiple_of(index * 16, 16), 8), halves[half]]
            lower = field[pl.ds(pl.multiple_of(index * 16 + 8, 8), 8), halves[half]]
            turned = pltpu.roll(lower, 4, 0)
            slope = jnp.where(sub < 4, pltpu.roll(upper, 4, 0), turned)
            bend = 0.5 * lower
            twist = jnp.where(sub < 4, turned * (1.0 / 6.0), 0.0)
            for step in range(4):
                time = (step + 1) * unit
                moved = upper + time * (slope + time * (bend + time * twist))
                ahead[step, index * 2 + half] = jnp.where(sub == 3, upper, moved)

    together = min(4, devices)

    @pl.loop(0, devices // together)
    def _(index):
        for inner in range(together):
            look_ahead(index * together + inner)

    low, count = listed[0], listed[1]

    mine = pl.multiple_of(slot_of(me, me, devices) * 16, 16)

    def own(part, component, half):
        tile = field[pl.ds(pl.multiple_of(mine + part // 2 * 8, 8), 8), halves[half]]
        at = part % 2 * 4 + component
        return tile[at : at + 1, :]

    def fetch(block):
        name = jnp.zeros((8, lanes), jnp.int32)
        for row in range(8):
            star = listed[2 + count_all + block * 8 + row]
            base = pl.multiple_of(slot_of(star // own_count, me, devices) * 16, 16)
            side = pl.multiple_of(star % own_count // lanes * lanes, lanes)
            slab[16 * row : 16 * row + 16, :] = field[pl.ds(base, 16), pl.ds(side, lanes)]
            name = jnp.where(sub == row, star, name)
        names[rows8(block), :] = name
        hit = (name % lanes) == lane
        for part in range(4):
            for component in range(3):
                value = slab[pl.ds(4 * part + component, 8, stride=16), :]
                table[3 * part + component, rows8(block), :] = lane_total(jnp.where(hit, value, 0.0))
        mass = slab[pl.ds(7, 8, stride=16), :]
        table[12, rows8(block), :] = lane_total(jnp.where(hit, mass, 0.0))

    loop(blocks, fetch)
    level = [own(2, 3, half) for half in range(2)]

    def turn(ref, group, *at):
        total = jnp.zeros((8, lanes), ref.dtype)
        for inner in range(min(16, blocks)):
            value = ref[(*at, rows8(group * 16 + inner), slice(None))]
            total = total + jnp.where(lane == sub + inner * 8, value, jnp.zeros_like(value))
        return jnp.sum(total, axis=0, keepdims=True)

    def fixed(group):
        mid_field[group, 6:7, :] = turn(table, group, 12)
        found = turn(names, group)
        if blocks * 8 < lanes:
            found = jnp.where(lane[0:1, :] < blocks * 8, found, -1)
        mid_names[group, 0:1, :] = found

    loop(groups, fixed)

    def elapse_of(step, fine):
        return unit * (1 if fine or step % 2 == 0 else 2)

    def guess_block(step, fine, block):
        state = [table[index, rows8(block), :] for index in range(12)]
        elapse = elapse_of(step, fine)
        for index in range(3):
            moved, sped = predict(
                state[index], state[3 + index], state[6 + index], state[9 + index], elapse
            )
            guess[index, rows8(block), :] = moved
            guess[3 + index, rows8(block), :] = sped

    def place_mid(group):
        for index in range(6):
            mid_field[group, index : index + 1, :] = turn(guess, group, index)

    def force(step, targets):
        def add(totals, row):
            return [pair_terms(target, row, total) for target, total in zip(targets, totals)]

        def one(index, totals):
            for half in range(2):
                row = [ahead[step, index * 2 + half, k : k + 1, :] for k in (0, 1, 2, 4, 5, 6, 3)]
                totals = add(totals, row)
            return totals

        together = min(8, devices)

        def some(index, totals):
            for inner in range(together):
                totals = one(index * together + inner, totals)
            return totals

        zero = jnp.zeros((8, lanes), jnp.float32)
        totals = [[zero] * 6 for _ in targets]
        for group in range(groups):
            totals = add(totals, [mid_field[group, k : k + 1, :] for k in range(7)])
        totals = lax.fori_loop(0, devices // together, some, totals)
        return [[lane_total(value) for value in total] for total in totals]

    for step in range(4):
        loop(blocks_fine, functools.partial(guess_block, step, True))
        loop(blocks - blocks_fine, lambda block: guess_block(step, False, block + blocks_fine))
        loop(groups, place_mid)
        if step == 3:
            break

        def advance(pair, step, fine):
            targets = [
                [guess[index, rows8(2 * pair + side), :] for index in range(6)] for side in range(2)
            ]
            elapse = elapse_of(step, fine)
            for side, total in enumerate(force(step, targets)):
                rows = rows8(2 * pair + side)
                for index in range(3):
                    moved, sped = correct(
                        *[table[3 * part + index, rows, :] for part in range(4)],
                        total[index],
                        total[3 + index],
                        elapse,
                    )
                    table[index, rows, :] = moved
                    table[3 + index, rows, :] = sped
                    table[6 + index, rows, :] = total[index]
                    table[9 + index, rows, :] = total[3 + index]

        loop(blocks_fine // 2, functools.partial(advance, step=step, fine=True))
        if step == 1:
            loop(
                (blocks - blocks_fine) // 2,
                lambda pair: advance(pair + blocks_fine // 2, step=1, fine=False),
            )

    def keep(group):
        for index in range(12):
            mid_state[group, index : index + 1, :] = turn(table, group, index)

    loop(groups, keep)
    result[...] = jnp.zeros_like(result)

    def finish(wide, turn_at):
        hits, states, elapses, targets = [], [], [], []
        for side in range(wide):
            name = jnp.full((8, lanes), -1, jnp.int32)
            for row in range(8):
                at = (turn_at * wide + side) * 8 + row
                star = listed[2 + jnp.minimum(low + at, count_all - 1)]
                name = jnp.where((sub == row) & (at < count), star, name)
            own_hit = [name == lane + (first + half * lanes) for half in range(2)]
            coarse = [own_hit[half] & (level[half] == 1.0) for half in range(2)]
            mid_hit = [name == mid_names[group, 0:1, :] for group in range(groups)]

            def find(part, component):
                total = jnp.zeros((8, lanes), jnp.float32)
                for half in range(2):
                    total = jnp.where(coarse[half], own(part, component, half), total)
                for group in range(groups):
                    at = 3 * part + component
                    total = jnp.where(mid_hit[group], mid_state[group, at : at + 1, :], total)
                return lane_total(total)

            total = jnp.zeros((8, lanes), jnp.float32)
            for half in range(2):
                total = jnp.where(coarse[half], 4 * unit, total)
            for group in range(groups):
                fine = jnp.where(lane + group * lanes < count_fine, unit, 2 * unit)
                total = jnp.where(mid_hit[group], fine, total)
            elapse = lane_total(total)
            state = [[find(part, index) for index in range(3)] for part in range(4)]
            pairs = [
                predict(*[state[part][index] for part in range(4)], elapse) for index in range(3)
            ]
            hits.append(own_hit)
            states.append(state)
            elapses.append(elapse)
            targets.append([pair[0] for pair in pairs] + [pair[1] for pair in pairs])
        for side, total in enumerate(force(3, targets)):
            for index in range(3):
                moved, sped = correct(
                    *[states[side][part][index] for part in range(4)],
                    total[index],
                    total[3 + index],
                    elapses[side],
                )
                for part, value in enumerate((moved, sped, total[index], total[3 + index])):
                    for half in range(2):
                        result[part, half, index] += jnp.where(hits[side][half], value, 0.0)

    @pl.when((count > 0) & (count <= 16))
    def _():
        finish(2, 0)

    @pl.when(count > 16)
    def _():
        pl.loop(0, (count + 23) // 24)(functools.partial(finish, 3))

    for part, ref in enumerate((out_place, out_motion, out_pull, out_change)):
        for half in range(2):
            changed = level[half] >= 1.0
            for index in range(3):
                value = jnp.sum(result[part, half, index], axis=0, keepdims=True)
                ref[index : index + 1, halves[half]] = jnp.where(
                    changed, value, own(part, index, half)
                )


def body(devices, place, motion, pull, change, masses, star_level, fine, mid, every):
    own_count = place.shape[1]
    sizes = (fine.shape[0], mid.shape[0], every.shape[0])
    groups = -(-sizes[1] // lanes)
    held = [pltpu.VMEM((3, own_count), jnp.float32)] * 4
    held += [pltpu.VMEM((2, lanes), jnp.float32), pltpu.VMEM((2, lanes), jnp.int32)]
    block = pl.pallas_call(
        pack_kernel,
        out_shape=jax.ShapeDtypeStruct((16, own_count), jnp.float32),
        in_specs=[pl.BlockSpec(memory_space=pl.ANY)] * 6,
        out_specs=vmem,
        scratch_shapes=held + [pltpu.SemaphoreType.DMA((6,))],
        name="pack",
    )(place, motion, pull, change, masses.reshape(2, lanes), star_level.reshape(2, lanes))

    def plan(lists):
        return pl.pallas_call(
            functools.partial(plan_kernel, own_count),
            out_shape=jax.ShapeDtypeStruct((2 + sizes[2] + sizes[1] + 6,), jnp.int32),
            in_specs=[smem] * 3,
            out_specs=smem,
            compiler_params=pltpu.CompilerParams(vmem_limit_bytes=1024 * 1024),
            name="plan",
        )(*lists)

    whole, listed = gather(block, devices, (fine, mid, every), plan)
    room = devices * 52 * 1024 + sizes[1] * 12 * 1024 + 3 * 1024 * 1024
    result = jax.ShapeDtypeStruct((3, own_count), jnp.float32)
    return pl.pallas_call(
        functools.partial(main_kernel, devices, own_count, sizes),
        out_shape=(result,) * 4,
        in_specs=[smem, vmem],
        out_specs=(vmem,) * 4,
        scratch_shapes=[
            pltpu.VMEM((4, devices * 2, 8, lanes), jnp.float32),
            pltpu.VMEM((8 * 16, lanes), jnp.float32),
            pltpu.VMEM((13, sizes[1], lanes), jnp.float32),
            pltpu.VMEM((sizes[1], lanes), jnp.int32),
            pltpu.VMEM((6, sizes[1], lanes), jnp.float32),
            pltpu.VMEM((groups, 8, lanes), jnp.float32),
            pltpu.VMEM((groups, 16, lanes), jnp.float32),
            pltpu.VMEM((groups, 8, lanes), jnp.int32),
            pltpu.VMEM((4, 2, 3, 8, lanes), jnp.float32),
        ],
        compiler_params=pltpu.CompilerParams(vmem_limit_bytes=room),
        name="steps",
    )(listed, whole)


def solution(mesh):
    split = P(None, "stars")
    return jax.shard_map(
        functools.partial(body, mesh.shape["stars"]),
        mesh=mesh,
        in_specs=(split,) * 4 + (P("stars"),) * 2 + (P(),) * 3,
        out_specs=(split,) * 4,
        check_vma=False,
    )
```

```python
import functools

import jax
import jax.numpy as jnp
from jax import lax
from jax.experimental import pallas as pl
from jax.experimental.pallas import tpu as pltpu
from jax.sharding import PartitionSpec as P

softening = 0.0001
unit = 1.0 / 128.0
lanes = 128
vmem = pl.BlockSpec(memory_space=pltpu.VMEM)
smem = pl.BlockSpec(memory_space=pltpu.SMEM)


def predict(place, motion, pull, change, elapse):
    moved = place + elapse * (motion + elapse * (0.5 * pull + elapse * change * (1.0 / 6.0)))
    sped = motion + elapse * (pull + 0.5 * elapse * change)
    return moved, sped


def correct(place, motion, pull, change, pull_new, change_new, elapse):
    square = elapse * elapse * (1.0 / 12.0)
    sped = motion + 0.5 * elapse * (pull + pull_new) + square * (change - change_new)
    moved = place + 0.5 * elapse * (motion + sped) + square * (pull - pull_new)
    return moved, sped


def pack_kernel(place, motion, pull, change, mass, level, out, *held):
    place_at, motion_at, pull_at, change_at, mass_at, level_at, arrived = held
    sources = (place, motion, pull, change, mass, level)
    copies = [
        pltpu.make_async_copy(source, target, arrived.at[index])
        for index, (source, target) in enumerate(zip(sources, held))
    ]
    for copy in copies:
        copy.start()
    for copy in copies:
        copy.wait()
    out[15:16, :] = jnp.zeros((1, out.shape[1]), jnp.float32)
    for part, ref in enumerate((place_at, motion_at, pull_at, change_at)):
        out[4 * part : 4 * part + 3, :] = ref[...]
    for half in range(2):
        row = slice(half, half + 1)
        at = slice(half * lanes, (half + 1) * lanes)
        out[3:4, at] = jnp.where(level_at[row, :] <= 1, mass_at[row, :], 0.0)
        out[7:8, at] = mass_at[row, :]
        out[11:12, at] = level_at[row, :].astype(jnp.float32)


def plan_kernel(own, fine, mid, every, listed):
    first = lax.axis_index("stars") * own
    count_fine, count_mid, count_all = fine.shape[0], mid.shape[0], every.shape[0]
    order = 2 + count_all

    def merge(index, seen):
        star = mid[index]
        listed[order + count_fine + index - seen] = star
        same = star == fine[jnp.minimum(seen, count_fine - 1)]
        return seen + same.astype(jnp.int32)

    lax.fori_loop(0, count_mid, merge, jnp.int32(0), unroll=8)

    def keep(source, start):
        def one(index, carry):
            listed[start + index] = source[index]
            return carry

        lax.fori_loop(0, source.shape[0], one, 0, unroll=8)

    keep(fine, order)
    keep(every, 2)

    def below(bound):
        found = jnp.int32(0)
        for bit in reversed(range(count_all.bit_length())):
            at = found + (1 << bit)
            less = (at <= count_all) & (every[jnp.minimum(at, count_all) - 1] < bound)
            found = jnp.where(less, at, found)
        return found

    low = below(first)
    listed[0] = low
    listed[1] = below(first + own) - low


def rounds_of(devices):
    bits = devices.bit_length() - 1
    assert devices == 1 << bits
    rounds = []
    high = bits
    while high > 1:
        width = 1 if high == 2 else 2
        high -= width
        rounds.append((1 << high, 1 << width))
    return rounds


def settle(value):
    return pl.pallas_call(
        lambda source, target: None,
        out_shape=jax.ShapeDtypeStruct(value.shape, value.dtype),
        in_specs=[pl.BlockSpec(memory_space=pl.ANY)],
        out_specs=pl.BlockSpec(memory_space=pl.ANY),
        input_output_aliases={0: 0},
        cost_estimate=pl.CostEstimate(flops=10**11, bytes_accessed=10**8, transcendentals=0),
        compiler_params=pltpu.CompilerParams(vmem_limit_bytes=1024 * 1024),
        name="settle",
    )(value)


def gather(block, devices, lists, plan):
    everyone = range(devices)
    odd = lax.axis_index("stars") % 2 == 1

    def fetch(value, even_by, odd_by):
        pairs = [(device, device ^ (odd_by if device % 2 else even_by)) for device in everyone]
        return lax.ppermute(value, "stars", pairs)

    def both(mine, other):
        return [jnp.where(odd, other, mine), jnp.where(odd, mine, other)]

    block = jnp.concatenate(both(block, fetch(block, 1, 1)), axis=0)
    rounds = rounds_of(devices)
    planned = None if rounds else plan(lists)
    for stride, radix in rounds:
        last = stride == rounds[-1][0]
        if last:
            block, lists = lax.optimization_barrier((block, lists))
            planned = plan(lists)
        if radix == 2:
            parts = [block, fetch(block, stride, stride)]
        elif last:
            half = block.shape[0] // 2
            one = fetch(block, stride, 3 * stride)
            two = jnp.where(odd, block[half:], block[:half])
            two = settle(fetch(two, 2 * stride, 2 * stride))
            parts = [block] + both(one, fetch(one, 1, 1)) + both(two, fetch(two, 1, 1))
        else:
            one = fetch(block, 2 * stride, 3 * stride)
            near = settle(fetch(block, stride, stride))
            second, third = both(one, fetch(one, 1, 1))
            parts = [block, second, near, third]
        block = jnp.concatenate(parts, axis=0)
    return block, planned


def slot_of(device, me, devices):
    slot, held = device % 2, 2
    rounds = rounds_of(devices)
    for stride, radix in rounds:
        digit = (device ^ me) // stride % radix
        if radix == 4:
            last = stride == rounds[-1][0]
            digit = digit ^ (digit // 2) if last else digit // 2 + digit % 2 * 2
        slot = slot + digit * held
        held *= radix
    return slot


def pair_terms(target, field, total):
    apart = [field[index] - target[index] for index in range(3)]
    closing = [field[3 + index] - target[3 + index] for index in range(3)]
    distance = apart[0] * apart[0] + apart[1] * apart[1] + (apart[2] * apart[2] + softening)
    inverse = lax.rsqrt(distance)
    square = inverse * inverse
    weight = field[6] * inverse * square
    dot = apart[0] * closing[0] + apart[1] * closing[1] + apart[2] * closing[2]
    rate = 3.0 * dot * square
    pulled = [weight * apart[index] for index in range(3)]
    return [total[index] + pulled[index] for index in range(3)] + [
        total[3 + index] + (weight * closing[index] - rate * pulled[index]) for index in range(3)
    ]


def main_kernel(
    devices,
    own_count,
    sizes,
    listed,
    field,
    out_place,
    out_motion,
    out_pull,
    out_change,
    ahead,
    slab,
    table,
    names,
    guess,
    mid_field,
    mid_state,
    mid_names,
    result,
):
    count_fine, count_mid, count_all = sizes
    blocks, blocks_fine = count_mid // 8, count_fine // 8
    groups = mid_field.shape[0]
    sub = lax.broadcasted_iota(jnp.int32, (8, lanes), 0)
    lane = lax.broadcasted_iota(jnp.int32, (8, lanes), 1)

    def spread(column):
        return jnp.broadcast_to(column, (8, lanes))

    def lane_total(value):
        return spread(jnp.sum(value, axis=1, keepdims=True))

    def loop(count, body):
        if count <= 4:
            for index in range(count):
                body(index)
        else:
            pl.loop(0, count)(body)

    def rows8(index):
        return pl.ds(index * 8 if isinstance(index, int) else pl.multiple_of(index * 8, 8), 8)

    halves = [slice(0, lanes), slice(lanes, 2 * lanes)]
    me = lax.axis_index("stars")
    first = me * own_count

    def look_ahead(index):
        for half in range(2):
            upper = field[pl.ds(pl.multiple_of(index * 16, 16), 8), halves[half]]
            lower = field[pl.ds(pl.multiple_of(index * 16 + 8, 8), 8), halves[half]]
            turned = pltpu.roll(lower, 4, 0)
            slope = jnp.where(sub < 4, pltpu.roll(upper, 4, 0), turned)
            bend = 0.5 * lower
            twist = jnp.where(sub < 4, turned * (1.0 / 6.0), 0.0)
            for step in range(4):
                time = (step + 1) * unit
                moved = upper + time * (slope + time * (bend + time * twist))
                ahead[step, index * 2 + half] = jnp.where(sub == 3, upper, moved)

    together = min(4, devices)

    @pl.loop(0, devices // together)
    def _(index):
        for inner in range(together):
            look_ahead(index * together + inner)

    low, count = listed[0], listed[1]

    mine = pl.multiple_of(slot_of(me, me, devices) * 16, 16)

    def own(part, component, half):
        tile = field[pl.ds(pl.multiple_of(mine + part // 2 * 8, 8), 8), halves[half]]
        at = part % 2 * 4 + component
        return tile[at : at + 1, :]

    def fetch(block):
        name = jnp.zeros((8, lanes), jnp.int32)
        for row in range(8):
            star = listed[2 + count_all + block * 8 + row]
            base = pl.multiple_of(slot_of(star // own_count, me, devices) * 16, 16)
            side = pl.multiple_of(star % own_count // lanes * lanes, lanes)
            slab[16 * row : 16 * row + 16, :] = field[pl.ds(base, 16), pl.ds(side, lanes)]
            name = jnp.where(sub == row, star, name)
        names[rows8(block), :] = name
        hit = (name % lanes) == lane
        for part in range(4):
            for component in range(3):
                value = slab[pl.ds(4 * part + component, 8, stride=16), :]
                table[3 * part + component, rows8(block), :] = lane_total(jnp.where(hit, value, 0.0))
        mass = slab[pl.ds(7, 8, stride=16), :]
        table[12, rows8(block), :] = lane_total(jnp.where(hit, mass, 0.0))

    loop(blocks, fetch)
    level = [own(2, 3, half) for half in range(2)]

    def turn(ref, group, *at):
        total = jnp.zeros((8, lanes), ref.dtype)
        for inner in range(min(16, blocks)):
            value = ref[(*at, rows8(group * 16 + inner), slice(None))]
            total = total + jnp.where(lane == sub + inner * 8, value, jnp.zeros_like(value))
        return jnp.sum(total, axis=0, keepdims=True)

    def fixed(group):
        mid_field[group, 6:7, :] = turn(table, group, 12)
        found = turn(names, group)
        if blocks * 8 < lanes:
            found = jnp.where(lane[0:1, :] < blocks * 8, found, -1)
        mid_names[group, 0:1, :] = found

    loop(groups, fixed)

    def elapse_of(step, fine):
        return unit * (1 if fine or step % 2 == 0 else 2)

    def guess_block(step, fine, block):
        state = [table[index, rows8(block), :] for index in range(12)]
        elapse = elapse_of(step, fine)
        for index in range(3):
            moved, sped = predict(
                state[index], state[3 + index], state[6 + index], state[9 + index], elapse
            )
            guess[index, rows8(block), :] = moved
            guess[3 + index, rows8(block), :] = sped

    def place_mid(group):
        for index in range(6):
            mid_field[group, index : index + 1, :] = turn(guess, group, index)

    def force(step, targets):
        def add(totals, row):
            return [pair_terms(target, row, total) for target, total in zip(targets, totals)]

        def one(index, totals):
            for half in range(2):
                row = [ahead[step, index * 2 + half, k : k + 1, :] for k in (0, 1, 2, 4, 5, 6, 3)]
                totals = add(totals, row)
            return totals

        together = min(8, devices)

        def some(index, totals):
            for inner in range(together):
                totals = one(index * together + inner, totals)
            return totals

        zero = jnp.zeros((8, lanes), jnp.float32)
        totals = [[zero] * 6 for _ in targets]
        for group in range(groups):
            totals = add(totals, [mid_field[group, k : k + 1, :] for k in range(7)])
        totals = lax.fori_loop(0, devices // together, some, totals)
        return [[lane_total(value) for value in total] for total in totals]

    for step in range(4):
        loop(blocks_fine, functools.partial(guess_block, step, True))
        loop(blocks - blocks_fine, lambda block: guess_block(step, False, block + blocks_fine))
        loop(groups, place_mid)
        if step == 3:
            break

        def advance(pair, step, fine):
            targets = [
                [guess[index, rows8(2 * pair + side), :] for index in range(6)] for side in range(2)
            ]
            elapse = elapse_of(step, fine)
            for side, total in enumerate(force(step, targets)):
                rows = rows8(2 * pair + side)
                for index in range(3):
                    moved, sped = correct(
                        *[table[3 * part + index, rows, :] for part in range(4)],
                        total[index],
                        total[3 + index],
                        elapse,
                    )
                    table[index, rows, :] = moved
                    table[3 + index, rows, :] = sped
                    table[6 + index, rows, :] = total[index]
                    table[9 + index, rows, :] = total[3 + index]

        loop(blocks_fine // 2, functools.partial(advance, step=step, fine=True))
        if step == 1:
            loop(
                (blocks - blocks_fine) // 2,
                lambda pair: advance(pair + blocks_fine // 2, step=1, fine=False),
            )

    def keep(group):
        for index in range(12):
            mid_state[group, index : index + 1, :] = turn(table, group, index)

    loop(groups, keep)
    result[...] = jnp.zeros_like(result)

    def finish(wide, turn_at):
        hits, states, elapses, targets = [], [], [], []
        for side in range(wide):
            name = jnp.full((8, lanes), -1, jnp.int32)
            for row in range(8):
                at = (turn_at * wide + side) * 8 + row
                star = listed[2 + jnp.minimum(low + at, count_all - 1)]
                name = jnp.where((sub == row) & (at < count), star, name)
            own_hit = [name == lane + (first + half * lanes) for half in range(2)]
            coarse = [own_hit[half] & (level[half] == 1.0) for half in range(2)]
            mid_hit = [name == mid_names[group, 0:1, :] for group in range(groups)]

            def find(part, component):
                total = jnp.zeros((8, lanes), jnp.float32)
                for half in range(2):
                    total = jnp.where(coarse[half], own(part, component, half), total)
                for group in range(groups):
                    at = 3 * part + component
                    total = jnp.where(mid_hit[group], mid_state[group, at : at + 1, :], total)
                return lane_total(total)

            total = jnp.zeros((8, lanes), jnp.float32)
            for half in range(2):
                total = jnp.where(coarse[half], 4 * unit, total)
            for group in range(groups):
                fine = jnp.where(lane + group * lanes < count_fine, unit, 2 * unit)
                total = jnp.where(mid_hit[group], fine, total)
            elapse = lane_total(total)
            state = [[find(part, index) for index in range(3)] for part in range(4)]
            pairs = [
                predict(*[state[part][index] for part in range(4)], elapse) for index in range(3)
            ]
            hits.append(own_hit)
            states.append(state)
            elapses.append(elapse)
            targets.append([pair[0] for pair in pairs] + [pair[1] for pair in pairs])
        for side, total in enumerate(force(3, targets)):
            for index in range(3):
                moved, sped = correct(
                    *[states[side][part][index] for part in range(4)],
                    total[index],
                    total[3 + index],
                    elapses[side],
                )
                for part, value in enumerate((moved, sped, total[index], total[3 + index])):
                    for half in range(2):
                        result[part, half, index] += jnp.where(hits[side][half], value, 0.0)

    @pl.when((count > 0) & (count <= 16))
    def _():
        finish(2, 0)

    @pl.when(count > 16)
    def _():
        pl.loop(0, (count + 23) // 24)(functools.partial(finish, 3))

    for part, ref in enumerate((out_place, out_motion, out_pull, out_change)):
        for half in range(2):
            changed = level[half] >= 1.0
            for index in range(3):
                value = jnp.sum(result[part, half, index], axis=0, keepdims=True)
                ref[index : index + 1, halves[half]] = jnp.where(
                    changed, value, own(part, index, half)
                )


def body(devices, place, motion, pull, change, masses, star_level, fine, mid, every):
    own_count = place.shape[1]
    sizes = (fine.shape[0], mid.shape[0], every.shape[0])
    groups = -(-sizes[1] // lanes)
    held = [pltpu.VMEM((3, own_count), jnp.float32)] * 4
    held += [pltpu.VMEM((2, lanes), jnp.float32), pltpu.VMEM((2, lanes), jnp.int32)]
    block = pl.pallas_call(
        pack_kernel,
        out_shape=jax.ShapeDtypeStruct((16, own_count), jnp.float32),
        in_specs=[pl.BlockSpec(memory_space=pl.ANY)] * 6,
        out_specs=vmem,
        scratch_shapes=held + [pltpu.SemaphoreType.DMA((6,))],
        name="pack",
    )(place, motion, pull, change, masses.reshape(2, lanes), star_level.reshape(2, lanes))

    def plan(lists):
        return pl.pallas_call(
            functools.partial(plan_kernel, own_count),
            out_shape=jax.ShapeDtypeStruct((2 + sizes[2] + sizes[1] + 6,), jnp.int32),
            in_specs=[smem] * 3,
            out_specs=smem,
            compiler_params=pltpu.CompilerParams(vmem_limit_bytes=1024 * 1024),
            name="plan",
        )(*lists)

    whole, listed = gather(block, devices, (fine, mid, every), plan)
    room = devices * 52 * 1024 + sizes[1] * 12 * 1024 + 3 * 1024 * 1024
    result = jax.ShapeDtypeStruct((3, own_count), jnp.float32)
    return pl.pallas_call(
        functools.partial(main_kernel, devices, own_count, sizes),
        out_shape=(result,) * 4,
        in_specs=[smem, vmem],
        out_specs=(vmem,) * 4,
        scratch_shapes=[
            pltpu.VMEM((4, devices * 2, 8, lanes), jnp.float32),
            pltpu.VMEM((8 * 16, lanes), jnp.float32),
            pltpu.VMEM((13, sizes[1], lanes), jnp.float32),
            pltpu.VMEM((sizes[1], lanes), jnp.int32),
            pltpu.VMEM((6, sizes[1], lanes), jnp.float32),
            pltpu.VMEM((groups, 8, lanes), jnp.float32),
            pltpu.VMEM((groups, 16, lanes), jnp.float32),
            pltpu.VMEM((groups, 8, lanes), jnp.int32),
            pltpu.VMEM((4, 2, 3, 8, lanes), jnp.float32),
        ],
        compiler_params=pltpu.CompilerParams(vmem_limit_bytes=room),
        name="steps",
    )(listed, whole)


def solution(mesh):
    split = P(None, "stars")
    return jax.shard_map(
        functools.partial(body, mesh.shape["stars"]),
        mesh=mesh,
        in_specs=(split,) * 4 + (P("stars"),) * 2 + (P(),) * 3,
        out_specs=(split,) * 4,
        check_vma=False,
    )
```

```python
import functools

import jax
import jax.numpy as jnp
from jax import lax
from jax.experimental import pallas as pl
from jax.experimental.pallas import tpu as pltpu
from jax.sharding import PartitionSpec as P

softening = 0.0001
unit = 1.0 / 128.0
lanes = 128
vmem = pl.BlockSpec(memory_space=pltpu.VMEM)
smem = pl.BlockSpec(memory_space=pltpu.SMEM)


def predict(place, motion, pull, change, elapse):
    moved = place + elapse * (motion + elapse * (0.5 * pull + elapse * change * (1.0 / 6.0)))
    sped = motion + elapse * (pull + 0.5 * elapse * change)
    return moved, sped


def correct(place, motion, pull, change, pull_new, change_new, elapse):
    square = elapse * elapse * (1.0 / 12.0)
    sped = motion + 0.5 * elapse * (pull + pull_new) + square * (change - change_new)
    moved = place + 0.5 * elapse * (motion + sped) + square * (pull - pull_new)
    return moved, sped


def pack_kernel(place, motion, pull, change, mass, level, out, *held):
    place_at, motion_at, pull_at, change_at, mass_at, level_at, arrived = held
    sources = (place, motion, pull, change, mass, level)
    copies = [
        pltpu.make_async_copy(source, target, arrived.at[index])
        for index, (source, target) in enumerate(zip(sources, held))
    ]
    for copy in copies:
        copy.start()
    for copy in copies:
        copy.wait()
    out[15:16, :] = jnp.zeros((1, out.shape[1]), jnp.float32)
    for part, ref in enumerate((place_at, motion_at, pull_at, change_at)):
        out[4 * part : 4 * part + 3, :] = ref[...]
    for half in range(2):
        row = slice(half, half + 1)
        at = slice(half * lanes, (half + 1) * lanes)
        out[3:4, at] = jnp.where(level_at[row, :] <= 1, mass_at[row, :], 0.0)
        out[7:8, at] = mass_at[row, :]
        out[11:12, at] = level_at[row, :].astype(jnp.float32)


def plan_kernel(devices, own, fine, mid, every, listed):
    me = lax.axis_index("stars")
    first = me * own
    count_fine, count_mid, count_all = fine.shape[0], mid.shape[0], every.shape[0]
    order = 2 + count_all

    def merge(index, seen):
        star = mid[index]
        listed[order + count_fine + index - seen] = star
        same = star == fine[jnp.minimum(seen, count_fine - 1)]
        return seen + same.astype(jnp.int32)

    lax.fori_loop(0, count_mid, merge, jnp.int32(0), unroll=8)

    def keep(source, start):
        def one(index, carry):
            listed[start + index] = source[index]
            return carry

        lax.fori_loop(0, source.shape[0], one, 0, unroll=8)

    keep(fine, order)
    keep(every, 2)

    def locate(index, carry):
        star = listed[order + index]
        device = star >> (own.bit_length() - 1)
        listed[order + count_mid + index] = slot_of(device, me, devices) * 16
        listed[order + 2 * count_mid + index] = star & lanes
        return carry

    lax.fori_loop(0, count_mid, locate, 0, unroll=8)

    def below(bound):
        found = jnp.int32(0)
        for bit in reversed(range(count_all.bit_length())):
            at = found + (1 << bit)
            less = (at <= count_all) & (every[jnp.minimum(at, count_all) - 1] < bound)
            found = jnp.where(less, at, found)
        return found

    low = below(first)
    listed[0] = low
    listed[1] = below(first + own) - low


def rounds_of(devices):
    bits = devices.bit_length() - 1
    assert devices == 1 << bits
    rounds = []
    high = bits
    while high > 1:
        width = 1 if high == 2 else 2
        high -= width
        rounds.append((1 << high, 1 << width))
    return rounds


def settle(value):
    return pl.pallas_call(
        lambda source, target: None,
        out_shape=jax.ShapeDtypeStruct(value.shape, value.dtype),
        in_specs=[pl.BlockSpec(memory_space=pl.ANY)],
        out_specs=pl.BlockSpec(memory_space=pl.ANY),
        input_output_aliases={0: 0},
        cost_estimate=pl.CostEstimate(flops=10**11, bytes_accessed=10**8, transcendentals=0),
        compiler_params=pltpu.CompilerParams(vmem_limit_bytes=1024 * 1024),
        name="settle",
    )(value)


def gather(block, devices, lists, plan):
    everyone = range(devices)
    odd = lax.axis_index("stars") % 2 == 1

    def fetch(value, even_by, odd_by):
        pairs = [(device, device ^ (odd_by if device % 2 else even_by)) for device in everyone]
        return lax.ppermute(value, "stars", pairs)

    def both(mine, other):
        return [jnp.where(odd, other, mine), jnp.where(odd, mine, other)]

    block = jnp.concatenate(both(block, fetch(block, 1, 1)), axis=0)
    rounds = rounds_of(devices)
    planned = None if rounds else plan(lists)
    for stride, radix in rounds:
        last = stride == rounds[-1][0]
        if last:
            block, lists = lax.optimization_barrier((block, lists))
            planned = plan(lists)
        if radix == 2:
            parts = [block, fetch(block, stride, stride)]
        elif last:
            half = block.shape[0] // 2
            one = fetch(block, stride, 3 * stride)
            two = jnp.where(odd, block[half:], block[:half])
            two = settle(fetch(two, 2 * stride, 2 * stride))
            parts = [block] + both(one, fetch(one, 1, 1)) + both(two, fetch(two, 1, 1))
        else:
            one = fetch(block, 2 * stride, 3 * stride)
            near = settle(fetch(block, stride, stride))
            second, third = both(one, fetch(one, 1, 1))
            parts = [block, second, near, third]
        block = jnp.concatenate(parts, axis=0)
    return block, planned


def slot_of(device, me, devices):
    slot, shift = device & 1, 1
    rounds = rounds_of(devices)
    for stride, radix in rounds:
        digit = ((device ^ me) >> (stride.bit_length() - 1)) & (radix - 1)
        if radix == 4:
            last = stride == rounds[-1][0]
            digit = digit ^ (digit >> 1) if last else (digit >> 1) | ((digit & 1) << 1)
        slot = slot | (digit << shift)
        shift += radix.bit_length() - 1
    return slot


def pair_terms(target, field, total):
    apart = [field[index] - target[index] for index in range(3)]
    closing = [field[3 + index] - target[3 + index] for index in range(3)]
    distance = apart[0] * apart[0] + apart[1] * apart[1] + (apart[2] * apart[2] + softening)
    inverse = lax.rsqrt(distance)
    square = inverse * inverse
    weight = field[6] * inverse * square
    dot = apart[0] * closing[0] + apart[1] * closing[1] + apart[2] * closing[2]
    rate = 3.0 * dot * square
    pulled = [weight * apart[index] for index in range(3)]
    return [total[index] + pulled[index] for index in range(3)] + [
        total[3 + index] + (weight * closing[index] - rate * pulled[index]) for index in range(3)
    ]


def main_kernel(
    devices,
    own_count,
    sizes,
    listed_from,
    field,
    out_place,
    out_motion,
    out_pull,
    out_change,
    ahead,
    slab,
    table,
    names,
    guess,
    mid_field,
    mid_state,
    mid_names,
    result,
    listed,
    arrived,
):
    count_fine, count_mid, count_all = sizes
    blocks, blocks_fine = count_mid // 8, count_fine // 8
    groups = mid_field.shape[0]
    sub = lax.broadcasted_iota(jnp.int32, (8, lanes), 0)
    lane = lax.broadcasted_iota(jnp.int32, (8, lanes), 1)

    def spread(column):
        return jnp.broadcast_to(column, (8, lanes))

    def lane_total(value):
        return spread(jnp.sum(value, axis=1, keepdims=True))

    def loop(count, body):
        if count <= 4:
            for index in range(count):
                body(index)
        else:
            pl.loop(0, count)(body)

    def rows8(index):
        return pl.ds(index * 8 if isinstance(index, int) else pl.multiple_of(index * 8, 8), 8)

    halves = [slice(0, lanes), slice(lanes, 2 * lanes)]
    me = lax.axis_index("stars")
    first = me * own_count

    copy = pltpu.make_async_copy(listed_from, listed, arrived)
    copy.start()

    def look_ahead(index):
        for half in range(2):
            upper = field[pl.ds(pl.multiple_of(index * 16, 16), 8), halves[half]]
            lower = field[pl.ds(pl.multiple_of(index * 16 + 8, 8), 8), halves[half]]
            turned = pltpu.roll(lower, 4, 0)
            slope = jnp.where(sub < 4, pltpu.roll(upper, 4, 0), turned)
            bend = 0.5 * lower
            twist = jnp.where(sub < 4, turned * (1.0 / 6.0), 0.0)
            for step in range(4):
                time = (step + 1) * unit
                moved = upper + time * (slope + time * (bend + time * twist))
                ahead[step, index * 2 + half] = jnp.where(sub == 3, upper, moved)

    together = min(4, devices)

    @pl.loop(0, devices // together)
    def _(index):
        for inner in range(together):
            look_ahead(index * together + inner)

    copy.wait()
    low, count = listed[0], listed[1]

    mine = pl.multiple_of(slot_of(me, me, devices) * 16, 16)

    def own(part, component, half):
        tile = field[pl.ds(pl.multiple_of(mine + part // 2 * 8, 8), 8), halves[half]]
        at = part % 2 * 4 + component
        return tile[at : at + 1, :]

    def fetch(block):
        name = jnp.zeros((8, lanes), jnp.int32)
        for row in range(8):
            at = 2 + count_all + block * 8 + row
            star = listed[at]
            base = pl.multiple_of(listed[at + count_mid], 16)
            side = pl.multiple_of(listed[at + 2 * count_mid], lanes)
            slab[16 * row : 16 * row + 16, :] = field[pl.ds(base, 16), pl.ds(side, lanes)]
            name = jnp.where(sub == row, star, name)
        names[rows8(block), :] = name
        hit = (name & (lanes - 1)) == lane
        for part in range(4):
            for component in range(3):
                value = slab[pl.ds(4 * part + component, 8, stride=16), :]
                table[3 * part + component, rows8(block), :] = lane_total(jnp.where(hit, value, 0.0))
        mass = slab[pl.ds(7, 8, stride=16), :]
        table[12, rows8(block), :] = lane_total(jnp.where(hit, mass, 0.0))

    loop(blocks, fetch)
    level = [own(2, 3, half) for half in range(2)]

    def turn(ref, group, *at):
        total = jnp.zeros((8, lanes), ref.dtype)
        for inner in range(min(16, blocks)):
            value = ref[(*at, rows8(group * 16 + inner), slice(None))]
            total = total + jnp.where(lane == sub + inner * 8, value, jnp.zeros_like(value))
        return jnp.sum(total, axis=0, keepdims=True)

    def fixed(group):
        mid_field[group, 6:7, :] = turn(table, group, 12)
        found = turn(names, group)
        if blocks * 8 < lanes:
            found = jnp.where(lane[0:1, :] < blocks * 8, found, -1)
        mid_names[group, 0:1, :] = found

    loop(groups, fixed)

    def elapse_of(step, fine):
        return unit * (1 if fine or step % 2 == 0 else 2)

    def guess_block(step, fine, block):
        state = [table[index, rows8(block), :] for index in range(12)]
        elapse = elapse_of(step, fine)
        for index in range(3):
            moved, sped = predict(
                state[index], state[3 + index], state[6 + index], state[9 + index], elapse
            )
            guess[index, rows8(block), :] = moved
            guess[3 + index, rows8(block), :] = sped

    def place_mid(group):
        for index in range(6):
            mid_field[group, index : index + 1, :] = turn(guess, group, index)

    def force(step, targets):
        def add(totals, row):
            return [pair_terms(target, row, total) for target, total in zip(targets, totals)]

        def one(index, totals):
            for half in range(2):
                row = [ahead[step, index * 2 + half, k : k + 1, :] for k in (0, 1, 2, 4, 5, 6, 3)]
                totals = add(totals, row)
            return totals

        together = min(8, devices)

        def some(index, totals):
            for inner in range(together):
                totals = one(index * together + inner, totals)
            return totals

        zero = jnp.zeros((8, lanes), jnp.float32)
        totals = [[zero] * 6 for _ in targets]
        for group in range(groups):
            totals = add(totals, [mid_field[group, k : k + 1, :] for k in range(7)])
        totals = lax.fori_loop(0, devices // together, some, totals)
        return [[lane_total(value) for value in total] for total in totals]

    for step in range(4):
        loop(blocks_fine, functools.partial(guess_block, step, True))
        loop(blocks - blocks_fine, lambda block: guess_block(step, False, block + blocks_fine))
        loop(groups, place_mid)
        if step == 3:
            break

        def advance(pair, step, fine):
            targets = [
                [guess[index, rows8(2 * pair + side), :] for index in range(6)] for side in range(2)
            ]
            elapse = elapse_of(step, fine)
            for side, total in enumerate(force(step, targets)):
                rows = rows8(2 * pair + side)
                for index in range(3):
                    moved, sped = correct(
                        *[table[3 * part + index, rows, :] for part in range(4)],
                        total[index],
                        total[3 + index],
                        elapse,
                    )
                    table[index, rows, :] = moved
                    table[3 + index, rows, :] = sped
                    table[6 + index, rows, :] = total[index]
                    table[9 + index, rows, :] = total[3 + index]

        loop(blocks_fine // 2, functools.partial(advance, step=step, fine=True))
        if step == 1:
            loop(
                (blocks - blocks_fine) // 2,
                lambda pair: advance(pair + blocks_fine // 2, step=1, fine=False),
            )

    def keep(group):
        for index in range(12):
            mid_state[group, index : index + 1, :] = turn(table, group, index)

    loop(groups, keep)
    result[...] = jnp.zeros_like(result)

    def finish(wide, turn_at):
        hits, states, elapses, targets = [], [], [], []
        for side in range(wide):
            name = jnp.full((8, lanes), -1, jnp.int32)
            for row in range(8):
                at = (turn_at * wide + side) * 8 + row
                star = listed[2 + jnp.minimum(low + at, count_all - 1)]
                name = jnp.where((sub == row) & (at < count), star, name)
            own_hit = [name == lane + (first + half * lanes) for half in range(2)]
            coarse = [own_hit[half] & (level[half] == 1.0) for half in range(2)]
            mid_hit = [name == mid_names[group, 0:1, :] for group in range(groups)]

            def find(part, component):
                total = jnp.zeros((8, lanes), jnp.float32)
                for half in range(2):
                    total = jnp.where(coarse[half], own(part, component, half), total)
                for group in range(groups):
                    at = 3 * part + component
                    total = jnp.where(mid_hit[group], mid_state[group, at : at + 1, :], total)
                return lane_total(total)

            total = jnp.zeros((8, lanes), jnp.float32)
            for half in range(2):
                total = jnp.where(coarse[half], 4 * unit, total)
            for group in range(groups):
                fine = jnp.where(lane + group * lanes < count_fine, unit, 2 * unit)
                total = jnp.where(mid_hit[group], fine, total)
            elapse = lane_total(total)
            state = [[find(part, index) for index in range(3)] for part in range(4)]
            pairs = [
                predict(*[state[part][index] for part in range(4)], elapse) for index in range(3)
            ]
            hits.append(own_hit)
            states.append(state)
            elapses.append(elapse)
            targets.append([pair[0] for pair in pairs] + [pair[1] for pair in pairs])
        for side, total in enumerate(force(3, targets)):
            for index in range(3):
                moved, sped = correct(
                    *[states[side][part][index] for part in range(4)],
                    total[index],
                    total[3 + index],
                    elapses[side],
                )
                for part, value in enumerate((moved, sped, total[index], total[3 + index])):
                    for half in range(2):
                        result[part, half, index] += jnp.where(hits[side][half], value, 0.0)

    @pl.when((count > 0) & (count <= 16))
    def _():
        finish(2, 0)

    @pl.when(count > 16)
    def _():
        pl.loop(0, (count + 23) // 24)(functools.partial(finish, 3))

    for part, ref in enumerate((out_place, out_motion, out_pull, out_change)):
        for half in range(2):
            changed = level[half] >= 1.0
            for index in range(3):
                value = jnp.sum(result[part, half, index], axis=0, keepdims=True)
                ref[index : index + 1, halves[half]] = jnp.where(
                    changed, value, own(part, index, half)
                )


def body(devices, place, motion, pull, change, masses, star_level, fine, mid, every):
    own_count = place.shape[1]
    assert own_count == 2 * lanes
    sizes = (fine.shape[0], mid.shape[0], every.shape[0])
    groups = -(-sizes[1] // lanes)
    held = [pltpu.VMEM((3, own_count), jnp.float32)] * 4
    held += [pltpu.VMEM((2, lanes), jnp.float32), pltpu.VMEM((2, lanes), jnp.int32)]
    block = pl.pallas_call(
        pack_kernel,
        out_shape=jax.ShapeDtypeStruct((16, own_count), jnp.float32),
        in_specs=[pl.BlockSpec(memory_space=pl.ANY)] * 6,
        out_specs=vmem,
        scratch_shapes=held + [pltpu.SemaphoreType.DMA((6,))],
        name="pack",
    )(place, motion, pull, change, masses.reshape(2, lanes), star_level.reshape(2, lanes))

    listed_shape = (2 + sizes[2] + 3 * sizes[1],)

    def plan(lists):
        return pl.pallas_call(
            functools.partial(plan_kernel, devices, own_count),
            out_shape=jax.ShapeDtypeStruct(listed_shape, jnp.int32),
            in_specs=[smem] * 3,
            out_specs=smem,
            compiler_params=pltpu.CompilerParams(vmem_limit_bytes=1024 * 1024),
            name="plan",
        )(*lists)

    whole, listed = gather(block, devices, (fine, mid, every), plan)
    room = devices * 52 * 1024 + sizes[1] * 12 * 1024 + 3 * 1024 * 1024
    result = jax.ShapeDtypeStruct((3, own_count), jnp.float32)
    return pl.pallas_call(
        functools.partial(main_kernel, devices, own_count, sizes),
        out_shape=(result,) * 4,
        in_specs=[pl.BlockSpec(memory_space=pl.ANY), vmem],
        out_specs=(vmem,) * 4,
        scratch_shapes=[
            pltpu.VMEM((4, devices * 2, 8, lanes), jnp.float32),
            pltpu.VMEM((8 * 16, lanes), jnp.float32),
            pltpu.VMEM((13, sizes[1], lanes), jnp.float32),
            pltpu.VMEM((sizes[1], lanes), jnp.int32),
            pltpu.VMEM((6, sizes[1], lanes), jnp.float32),
            pltpu.VMEM((groups, 8, lanes), jnp.float32),
            pltpu.VMEM((groups, 16, lanes), jnp.float32),
            pltpu.VMEM((groups, 8, lanes), jnp.int32),
            pltpu.VMEM((4, 2, 3, 8, lanes), jnp.float32),
            pltpu.SMEM(listed_shape, jnp.int32),
            pltpu.SemaphoreType.DMA,
        ],
        compiler_params=pltpu.CompilerParams(vmem_limit_bytes=room),
        name="steps",
    )(listed, whole)


def solution(mesh):
    split = P(None, "stars")
    return jax.shard_map(
        functools.partial(body, mesh.shape["stars"]),
        mesh=mesh,
        in_specs=(split,) * 4 + (P("stars"),) * 2 + (P(),) * 3,
        out_specs=(split,) * 4,
        check_vma=False,
    )
```

```python
import functools

import jax
import jax.numpy as jnp
from jax import lax
from jax.experimental import pallas as pl
from jax.experimental.pallas import tpu as pltpu
from jax.sharding import PartitionSpec as P

softening = 0.0001
unit = 1.0 / 128.0
lanes = 128
vmem = pl.BlockSpec(memory_space=pltpu.VMEM)
smem = pl.BlockSpec(memory_space=pltpu.SMEM)


def predict(place, motion, pull, change, elapse):
    moved = place + elapse * (motion + elapse * (0.5 * pull + elapse * change * (1.0 / 6.0)))
    sped = motion + elapse * (pull + 0.5 * elapse * change)
    return moved, sped


def correct(place, motion, pull, change, pull_new, change_new, elapse):
    square = elapse * elapse * (1.0 / 12.0)
    sped = motion + 0.5 * elapse * (pull + pull_new) + square * (change - change_new)
    moved = place + 0.5 * elapse * (motion + sped) + square * (pull - pull_new)
    return moved, sped


def pack_kernel(place, motion, pull, change, mass, level, out, *held):
    place_at, motion_at, pull_at, change_at, mass_at, level_at, arrived = held
    sources = (place, motion, pull, change, mass, level)
    copies = [
        pltpu.make_async_copy(source, target, arrived.at[index])
        for index, (source, target) in enumerate(zip(sources, held))
    ]
    for copy in copies:
        copy.start()
    for copy in copies:
        copy.wait()
    out[7:8, :] = jnp.zeros((1, out.shape[1]), jnp.float32)
    out[11:12, :] = jnp.zeros((1, out.shape[1]), jnp.float32)
    for part, ref in enumerate((place_at, motion_at, pull_at, change_at)):
        out[4 * part : 4 * part + 3, :] = ref[...]
    for half in range(2):
        row = slice(half, half + 1)
        at = slice(half * lanes, (half + 1) * lanes)
        rank, heavy = level_at[row, :], mass_at[row, :]
        out[3:4, at] = jnp.where(rank <= 1, heavy, 0.0)
        out[15:16, at] = jnp.where(rank == 0, heavy, -heavy)


def padded(count_all, own):
    return -(-min(count_all, own) // 24) * 24


def plan_kernel(devices, own, fine, mid, every, listed):
    me = lax.axis_index("stars")
    first = me * own
    count_fine, count_mid, count_all = fine.shape[0], mid.shape[0], every.shape[0]
    room = padded(count_all, own)
    order = 1 + room

    def merge(index, seen):
        star = mid[index]
        listed[order + count_fine + index - seen] = star
        same = star == fine[jnp.minimum(seen, count_fine - 1)]
        return seen + same.astype(jnp.int32)

    lax.fori_loop(0, count_mid, merge, jnp.int32(0), unroll=8)

    def keep(index, carry):
        listed[order + index] = fine[index]
        return carry

    lax.fori_loop(0, count_fine, keep, 0, unroll=8)

    def locate(index, carry):
        star = listed[order + index]
        device = star >> (own.bit_length() - 1)
        listed[order + count_mid + index] = slot_of(device, me, devices) * 16
        listed[order + 2 * count_mid + index] = star & lanes
        return carry

    lax.fori_loop(0, count_mid, locate, 0, unroll=8)

    def below(bound):
        found = jnp.int32(0)
        for bit in reversed(range(count_all.bit_length())):
            at = found + (1 << bit)
            less = (at <= count_all) & (every[jnp.minimum(at, count_all) - 1] < bound)
            found = jnp.where(less, at, found)
        return found

    low = below(first)
    count = below(first + own) - low
    listed[0] = count

    def mine(index, carry):
        star = every[jnp.minimum(low + index, count_all - 1)]
        listed[1 + index] = jnp.where(index < count, star, -1)
        return carry

    lax.fori_loop(0, room, mine, 0, unroll=8)


def rounds_of(devices):
    bits = devices.bit_length() - 1
    assert devices == 1 << bits
    rounds = []
    high = bits
    while high > 1:
        width = 1 if high == 2 else 2
        high -= width
        rounds.append((1 << high, 1 << width))
    return rounds


def settle(value):
    return pl.pallas_call(
        lambda source, target: None,
        out_shape=jax.ShapeDtypeStruct(value.shape, value.dtype),
        in_specs=[pl.BlockSpec(memory_space=pl.ANY)],
        out_specs=pl.BlockSpec(memory_space=pl.ANY),
        input_output_aliases={0: 0},
        cost_estimate=pl.CostEstimate(flops=10**11, bytes_accessed=10**8, transcendentals=0),
        compiler_params=pltpu.CompilerParams(vmem_limit_bytes=1024 * 1024),
        name="settle",
    )(value)


def gather(block, devices, lists, plan):
    everyone = range(devices)
    odd = lax.axis_index("stars") % 2 == 1

    def fetch(value, even_by, odd_by):
        pairs = [(device, device ^ (odd_by if device % 2 else even_by)) for device in everyone]
        return lax.ppermute(value, "stars", pairs)

    def both(mine, other):
        return [jnp.where(odd, other, mine), jnp.where(odd, mine, other)]

    block = jnp.concatenate(both(block, fetch(block, 1, 1)), axis=0)
    rounds = rounds_of(devices)
    planned = None if rounds else plan(lists)
    for stride, radix in rounds:
        last = stride == rounds[-1][0]
        if last:
            block, lists = lax.optimization_barrier((block, lists))
            planned = plan(lists)
        if radix == 2:
            parts = [block, fetch(block, stride, stride)]
        elif last:
            half = block.shape[0] // 2
            one = fetch(block, stride, 3 * stride)
            two = jnp.where(odd, block[half:], block[:half])
            two = settle(fetch(two, 2 * stride, 2 * stride))
            parts = [block] + both(one, fetch(one, 1, 1)) + both(two, fetch(two, 1, 1))
        else:
            one = fetch(block, 2 * stride, 3 * stride)
            near = settle(fetch(block, stride, stride))
            second, third = both(one, fetch(one, 1, 1))
            parts = [block, second, near, third]
        block = jnp.concatenate(parts, axis=0)
    return block, planned


def slot_of(device, me, devices):
    slot, shift = device & 1, 1
    rounds = rounds_of(devices)
    for stride, radix in rounds:
        digit = ((device ^ me) >> (stride.bit_length() - 1)) & (radix - 1)
        if radix == 4:
            last = stride == rounds[-1][0]
            digit = digit ^ (digit >> 1) if last else (digit >> 1) | ((digit & 1) << 1)
        slot = slot | (digit << shift)
        shift += radix.bit_length() - 1
    return slot


def pair_terms(target, field, total):
    apart = [field[index] - target[index] for index in range(3)]
    closing = [field[3 + index] - target[3 + index] for index in range(3)]
    distance = apart[0] * apart[0] + apart[1] * apart[1] + (apart[2] * apart[2] + softening)
    inverse = lax.rsqrt(distance)
    square = inverse * inverse
    weight = field[6] * inverse * square
    dot = apart[0] * closing[0] + apart[1] * closing[1] + apart[2] * closing[2]
    rate = 3.0 * dot * square
    pulled = [weight * apart[index] for index in range(3)]
    return [total[index] + pulled[index] for index in range(3)] + [
        total[3 + index] + (weight * closing[index] - rate * pulled[index]) for index in range(3)
    ]


def main_kernel(
    devices,
    own_count,
    sizes,
    listed_from,
    field,
    out_place,
    out_motion,
    out_pull,
    out_change,
    ahead,
    slab,
    table,
    names,
    guess,
    mid_field,
    mid_state,
    mid_names,
    result,
    listed,
    arrived,
):
    count_fine, count_mid, count_all = sizes
    blocks, blocks_fine = count_mid // 8, count_fine // 8
    groups = mid_field.shape[0]
    sub = lax.broadcasted_iota(jnp.int32, (8, lanes), 0)
    lane = lax.broadcasted_iota(jnp.int32, (8, lanes), 1)

    def spread(column):
        return jnp.broadcast_to(column, (8, lanes))

    def lane_total(value):
        return spread(jnp.sum(value, axis=1, keepdims=True))

    def loop(count, body):
        if count <= 4:
            for index in range(count):
                body(index)
        else:
            pl.loop(0, count)(body)

    def rows8(index):
        return pl.ds(index * 8 if isinstance(index, int) else pl.multiple_of(index * 8, 8), 8)

    halves = [slice(0, lanes), slice(lanes, 2 * lanes)]
    me = lax.axis_index("stars")
    first = me * own_count

    copy = pltpu.make_async_copy(listed_from, listed, arrived)
    copy.start()

    def look_ahead(index):
        for half in range(2):
            upper = field[pl.ds(pl.multiple_of(index * 16, 16), 8), halves[half]]
            lower = field[pl.ds(pl.multiple_of(index * 16 + 8, 8), 8), halves[half]]
            turned = pltpu.roll(lower, 4, 0)
            slope = unit * jnp.where(sub < 4, pltpu.roll(upper, 4, 0), turned)
            bend = unit**2 * lower
            twist = jnp.where(sub < 3, unit**3 * turned, 0.0)
            way = slope + 0.5 * bend + twist * (1.0 / 6.0)
            change, second = way, bend + twist
            for step in range(4):
                ahead[step, index * 2 + half] = upper + way
                if step < 3:
                    change = change + second
                    second = second + twist
                    way = way + change

    together = min(4, devices)

    @pl.loop(0, devices // together)
    def _(index):
        for inner in range(together):
            look_ahead(index * together + inner)

    copy.wait()
    count = listed[0]

    mine = pl.multiple_of(slot_of(me, me, devices) * 16, 16)

    def own(part, component, half):
        tile = field[pl.ds(pl.multiple_of(mine + part // 2 * 8, 8), 8), halves[half]]
        at = part % 2 * 4 + component
        return tile[at : at + 1, :]

    def fetch(block):
        room = block if isinstance(block, int) else 0
        name = jnp.zeros((8, lanes), jnp.int32)
        for row in range(8):
            at = 1 + padded(count_all, own_count) + block * 8 + row
            star = listed[at]
            base = pl.multiple_of(listed[at + count_mid], 16)
            side = pl.multiple_of(listed[at + 2 * count_mid], lanes)
            slab[room, 16 * row : 16 * row + 16, :] = field[pl.ds(base, 16), pl.ds(side, lanes)]
            name = jnp.where(sub == row, star, name)
        names[rows8(block), :] = name
        hit = (name & (lanes - 1)) == lane
        for part in range(4):
            for component in range(3):
                value = slab[room, pl.ds(4 * part + component, 8, stride=16), :]
                table[3 * part + component, rows8(block), :] = lane_total(jnp.where(hit, value, 0.0))
        mass = slab[room, pl.ds(15, 8, stride=16), :]
        table[12, rows8(block), :] = -lane_total(jnp.where(hit, mass, 0.0))

    loop(blocks, fetch)
    slow = [own(0, 3, half) > 0.0 for half in range(2)]

    def turn(ref, group, *at):
        total = jnp.zeros((8, lanes), ref.dtype)
        for inner in range(min(16, blocks)):
            value = ref[(*at, rows8(group * 16 + inner), slice(None))]
            total = total + jnp.where(lane == sub + inner * 8, value, jnp.zeros_like(value))
        return jnp.sum(total, axis=0, keepdims=True)

    def fixed(group):
        mid_field[group, 6:7, :] = turn(table, group, 12)
        found = turn(names, group)
        if blocks * 8 < lanes:
            found = jnp.where(lane[0:1, :] < blocks * 8, found, -2)
        mid_names[group, 0:1, :] = found

    loop(groups, fixed)

    def elapse_of(step, fine):
        return unit * (1 if fine or step % 2 == 0 else 2)

    def guess_block(step, fine, block):
        state = [table[index, rows8(block), :] for index in range(12)]
        elapse = elapse_of(step, fine)
        for index in range(3):
            moved, sped = predict(
                state[index], state[3 + index], state[6 + index], state[9 + index], elapse
            )
            guess[index, rows8(block), :] = moved
            guess[3 + index, rows8(block), :] = sped

    def place_mid(group):
        for index in range(6):
            mid_field[group, index : index + 1, :] = turn(guess, group, index)

    def force(step, targets):
        def add(totals, row):
            return [pair_terms(target, row, total) for target, total in zip(targets, totals)]

        def one(index, totals):
            for half in range(2):
                row = [ahead[step, index * 2 + half, k : k + 1, :] for k in (0, 1, 2, 4, 5, 6, 3)]
                totals = add(totals, row)
            return totals

        together = min(8, devices)

        def some(index, totals):
            for inner in range(together):
                totals = one(index * together + inner, totals)
            return totals

        zero = jnp.zeros((8, lanes), jnp.float32)
        totals = [[zero] * 6 for _ in targets]
        for group in range(groups):
            totals = add(totals, [mid_field[group, k : k + 1, :] for k in range(7)])
        totals = lax.fori_loop(0, devices // together, some, totals)
        return [[lane_total(value) for value in total] for total in totals]

    for step in range(4):
        loop(blocks_fine, functools.partial(guess_block, step, True))
        loop(blocks - blocks_fine, lambda block: guess_block(step, False, block + blocks_fine))
        loop(groups, place_mid)
        if step == 3:
            break

        def advance(pair, step, fine):
            targets = [
                [guess[index, rows8(2 * pair + side), :] for index in range(6)] for side in range(2)
            ]
            elapse = elapse_of(step, fine)
            for side, total in enumerate(force(step, targets)):
                rows = rows8(2 * pair + side)
                for index in range(3):
                    moved, sped = correct(
                        *[table[3 * part + index, rows, :] for part in range(4)],
                        total[index],
                        total[3 + index],
                        elapse,
                    )
                    table[index, rows, :] = moved
                    table[3 + index, rows, :] = sped
                    table[6 + index, rows, :] = total[index]
                    table[9 + index, rows, :] = total[3 + index]

        loop(blocks_fine // 2, functools.partial(advance, step=step, fine=True))
        if step == 1:
            loop(
                (blocks - blocks_fine) // 2,
                lambda pair: advance(pair + blocks_fine // 2, step=1, fine=False),
            )

    def keep(group):
        for index in range(12):
            mid_state[group, index : index + 1, :] = turn(table, group, index)

    loop(groups, keep)
    result[...] = jnp.zeros_like(result)

    def finish(wide, turn_at):
        hits, states, elapses, targets = [], [], [], []
        for side in range(wide):
            name = jnp.zeros((8, lanes), jnp.int32)
            for row in range(8):
                star = listed[1 + (turn_at * wide + side) * 8 + row]
                name = jnp.where(sub == row, star, name)
            own_hit = [name == lane + (first + half * lanes) for half in range(2)]
            coarse = [own_hit[half] & slow[half] for half in range(2)]
            mid_hit = [name == mid_names[group, 0:1, :] for group in range(groups)]

            def find(part, component):
                total = jnp.zeros((8, lanes), jnp.float32)
                for half in range(2):
                    total = jnp.where(coarse[half], own(part, component, half), total)
                for group in range(groups):
                    at = 3 * part + component
                    total = jnp.where(mid_hit[group], mid_state[group, at : at + 1, :], total)
                return lane_total(total)

            total = jnp.zeros((8, lanes), jnp.float32)
            for half in range(2):
                total = jnp.where(coarse[half], 4 * unit, total)
            for group in range(groups):
                fine = jnp.where(lane + group * lanes < count_fine, unit, 2 * unit)
                total = jnp.where(mid_hit[group], fine, total)
            elapse = lane_total(total)
            state = [[find(part, index) for index in range(3)] for part in range(4)]
            pairs = [
                predict(*[state[part][index] for part in range(4)], elapse) for index in range(3)
            ]
            hits.append(own_hit)
            states.append(state)
            elapses.append(elapse)
            targets.append([pair[0] for pair in pairs] + [pair[1] for pair in pairs])
        for side, total in enumerate(force(3, targets)):
            for index in range(3):
                moved, sped = correct(
                    *[states[side][part][index] for part in range(4)],
                    total[index],
                    total[3 + index],
                    elapses[side],
                )
                for part, value in enumerate((moved, sped, total[index], total[3 + index])):
                    for half in range(2):
                        result[part, half, index] += jnp.where(hits[side][half], value, 0.0)

    @pl.when((count > 0) & (count <= 16))
    def _():
        finish(2, 0)

    @pl.when(count > 16)
    def _():
        pl.loop(0, (count + 23) // 24)(functools.partial(finish, 3))

    for part, ref in enumerate((out_place, out_motion, out_pull, out_change)):
        for half in range(2):
            changed = own(3, 3, half) < 0.0
            for index in range(3):
                value = jnp.sum(result[part, half, index], axis=0, keepdims=True)
                ref[index : index + 1, halves[half]] = jnp.where(
                    changed, value, own(part, index, half)
                )


def body(devices, place, motion, pull, change, masses, star_level, fine, mid, every):
    own_count = place.shape[1]
    assert own_count == 2 * lanes
    sizes = (fine.shape[0], mid.shape[0], every.shape[0])
    groups = -(-sizes[1] // lanes)
    held = [pltpu.VMEM((3, own_count), jnp.float32)] * 4
    held += [pltpu.VMEM((2, lanes), jnp.float32), pltpu.VMEM((2, lanes), jnp.int32)]
    block = pl.pallas_call(
        pack_kernel,
        out_shape=jax.ShapeDtypeStruct((16, own_count), jnp.float32),
        in_specs=[pl.BlockSpec(memory_space=pl.ANY)] * 6,
        out_specs=vmem,
        scratch_shapes=held + [pltpu.SemaphoreType.DMA((6,))],
        name="pack",
    )(place, motion, pull, change, masses.reshape(2, lanes), star_level.reshape(2, lanes))

    listed_shape = (1 + padded(sizes[2], own_count) + 3 * sizes[1],)

    def plan(lists):
        return pl.pallas_call(
            functools.partial(plan_kernel, devices, own_count),
            out_shape=jax.ShapeDtypeStruct(listed_shape, jnp.int32),
            in_specs=[smem] * 3,
            out_specs=smem,
            compiler_params=pltpu.CompilerParams(vmem_limit_bytes=1024 * 1024),
            name="plan",
        )(*lists)

    whole, listed = gather(block, devices, (fine, mid, every), plan)
    room = devices * 52 * 1024 + sizes[1] * 12 * 1024 + 3 * 1024 * 1024
    result = jax.ShapeDtypeStruct((3, own_count), jnp.float32)
    return pl.pallas_call(
        functools.partial(main_kernel, devices, own_count, sizes),
        out_shape=(result,) * 4,
        in_specs=[pl.BlockSpec(memory_space=pl.ANY), vmem],
        out_specs=(vmem,) * 4,
        scratch_shapes=[
            pltpu.VMEM((4, devices * 2, 8, lanes), jnp.float32),
            pltpu.VMEM((min(4, sizes[1] // 8), 8 * 16, lanes), jnp.float32),
            pltpu.VMEM((13, sizes[1], lanes), jnp.float32),
            pltpu.VMEM((sizes[1], lanes), jnp.int32),
            pltpu.VMEM((6, sizes[1], lanes), jnp.float32),
            pltpu.VMEM((groups, 8, lanes), jnp.float32),
            pltpu.VMEM((groups, 16, lanes), jnp.float32),
            pltpu.VMEM((groups, 8, lanes), jnp.int32),
            pltpu.VMEM((4, 2, 3, 8, lanes), jnp.float32),
            pltpu.SMEM(listed_shape, jnp.int32),
            pltpu.SemaphoreType.DMA,
        ],
        compiler_params=pltpu.CompilerParams(vmem_limit_bytes=room),
        name="steps",
    )(listed, whole)


def solution(mesh):
    split = P(None, "stars")
    return jax.shard_map(
        functools.partial(body, mesh.shape["stars"]),
        mesh=mesh,
        in_specs=(split,) * 4 + (P("stars"),) * 2 + (P(),) * 3,
        out_specs=(split,) * 4,
        check_vma=False,
    )
```

```python
import functools

import jax
import jax.numpy as jnp
from jax import lax
from jax.experimental import pallas as pl
from jax.experimental.pallas import tpu as pltpu
from jax.sharding import PartitionSpec as P

softening = 0.0001
unit = 1.0 / 128.0
lanes = 128
vmem = pl.BlockSpec(memory_space=pltpu.VMEM)
smem = pl.BlockSpec(memory_space=pltpu.SMEM)


def predict(place, motion, pull, change, elapse):
    moved = place + elapse * (motion + elapse * (0.5 * pull + elapse * change * (1.0 / 6.0)))
    sped = motion + elapse * (pull + 0.5 * elapse * change)
    return moved, sped


def correct(place, motion, pull, change, pull_new, change_new, elapse):
    square = elapse * elapse * (1.0 / 12.0)
    sped = motion + 0.5 * elapse * (pull + pull_new) + square * (change - change_new)
    moved = place + 0.5 * elapse * (motion + sped) + square * (pull - pull_new)
    return moved, sped


def pack_kernel(place, motion, pull, change, mass, level, out, *held):
    place_at, motion_at, pull_at, change_at, mass_at, level_at, arrived = held
    sources = (place, motion, pull, change, mass, level)
    copies = [
        pltpu.make_async_copy(source, target, arrived.at[index])
        for index, (source, target) in enumerate(zip(sources, held))
    ]
    for copy in copies:
        copy.start()
    for copy in copies:
        copy.wait()
    out[7:8, :] = jnp.zeros((1, out.shape[1]), jnp.float32)
    out[11:12, :] = jnp.zeros((1, out.shape[1]), jnp.float32)
    for part, ref in enumerate((place_at, motion_at, pull_at, change_at)):
        out[4 * part : 4 * part + 3, :] = ref[...]
    for half in range(2):
        row = slice(half, half + 1)
        at = slice(half * lanes, (half + 1) * lanes)
        rank, heavy = level_at[row, :], mass_at[row, :]
        out[3:4, at] = jnp.where(rank <= 1, heavy, 0.0)
        out[15:16, at] = jnp.where(rank == 0, heavy, -heavy)


def padded(count_all, own):
    return -(-min(count_all, own) // 24) * 24


def plan_kernel(devices, own, fine, mid, every, listed):
    me = lax.axis_index("stars")
    first = me * own
    count_fine, count_mid, count_all = fine.shape[0], mid.shape[0], every.shape[0]
    room = padded(count_all, own)
    order = 1 + room

    def merge(index, seen):
        star = mid[index]
        listed[order + count_fine + index - seen] = star
        same = star == fine[jnp.minimum(seen, count_fine - 1)]
        return seen + same.astype(jnp.int32)

    lax.fori_loop(0, count_mid, merge, jnp.int32(0), unroll=8)

    def keep(index, carry):
        listed[order + index] = fine[index]
        return carry

    lax.fori_loop(0, count_fine, keep, 0, unroll=8)

    def locate(index, carry):
        star = listed[order + index]
        device = star >> (own.bit_length() - 1)
        listed[order + count_mid + index] = slot_of(device, me, devices) * 16
        listed[order + 2 * count_mid + index] = star & lanes
        return carry

    lax.fori_loop(0, count_mid, locate, 0, unroll=8)

    def below(bound):
        found = jnp.int32(0)
        for bit in reversed(range(count_all.bit_length())):
            at = found + (1 << bit)
            less = (at <= count_all) & (every[jnp.minimum(at, count_all) - 1] < bound)
            found = jnp.where(less, at, found)
        return found

    low = below(first)
    count = below(first + own) - low
    listed[0] = count

    def mine(index, carry):
        star = every[jnp.minimum(low + index, count_all - 1)]
        listed[1 + index] = jnp.where(index < count, star, -1)
        return carry

    lax.fori_loop(0, room, mine, 0, unroll=8)


def rounds_of(devices):
    bits = devices.bit_length() - 1
    assert devices == 1 << bits
    rounds = []
    high = bits
    while high > 1:
        width = 1 if high == 2 else 2
        high -= width
        rounds.append((1 << high, 1 << width))
    return rounds


def settle(value):
    return pl.pallas_call(
        lambda source, target: None,
        out_shape=jax.ShapeDtypeStruct(value.shape, value.dtype),
        in_specs=[pl.BlockSpec(memory_space=pl.ANY)],
        out_specs=pl.BlockSpec(memory_space=pl.ANY),
        input_output_aliases={0: 0},
        cost_estimate=pl.CostEstimate(flops=10**11, bytes_accessed=10**8, transcendentals=0),
        compiler_params=pltpu.CompilerParams(vmem_limit_bytes=1024 * 1024),
        name="settle",
    )(value)


def gather(block, devices, lists, plan):
    everyone = range(devices)
    odd = lax.axis_index("stars") % 2 == 1

    def fetch(value, even_by, odd_by):
        pairs = [(device, device ^ (odd_by if device % 2 else even_by)) for device in everyone]
        return lax.ppermute(value, "stars", pairs)

    def both(mine, other):
        return [jnp.where(odd, other, mine), jnp.where(odd, mine, other)]

    block = jnp.concatenate(both(block, fetch(block, 1, 1)), axis=0)
    rounds = rounds_of(devices)
    planned = None if rounds else plan(lists)
    for stride, radix in rounds:
        last = stride == rounds[-1][0]
        if last:
            block, lists = lax.optimization_barrier((block, lists))
            planned = plan(lists)
        if radix == 2:
            parts = [block, fetch(block, stride, stride)]
        elif last:
            half = block.shape[0] // 2
            one = fetch(block, stride, 3 * stride)
            two = jnp.where(odd, block[half:], block[:half])
            two = settle(fetch(two, 2 * stride, 2 * stride))
            parts = [block] + both(one, fetch(one, 1, 1)) + both(two, fetch(two, 1, 1))
        else:
            one = fetch(block, 2 * stride, 3 * stride)
            near = settle(fetch(block, stride, stride))
            second, third = both(one, fetch(one, 1, 1))
            parts = [block, second, near, third]
        block = jnp.concatenate(parts, axis=0)
    return block, planned


def slot_of(device, me, devices):
    slot, shift = device & 1, 1
    rounds = rounds_of(devices)
    for stride, radix in rounds:
        digit = ((device ^ me) >> (stride.bit_length() - 1)) & (radix - 1)
        if radix == 4:
            last = stride == rounds[-1][0]
            digit = digit ^ (digit >> 1) if last else (digit >> 1) | ((digit & 1) << 1)
        slot = slot | (digit << shift)
        shift += radix.bit_length() - 1
    return slot


def pair_terms(target, field, total):
    apart = [field[index] - target[index] for index in range(3)]
    closing = [field[3 + index] - target[3 + index] for index in range(3)]
    distance = apart[0] * apart[0] + apart[1] * apart[1] + (apart[2] * apart[2] + softening)
    inverse = lax.rsqrt(distance)
    square = inverse * inverse
    weight = field[6] * inverse * square
    dot = apart[0] * closing[0] + apart[1] * closing[1] + apart[2] * closing[2]
    rate = 3.0 * dot * square
    pulled = [weight * apart[index] for index in range(3)]
    return [total[index] + pulled[index] for index in range(3)] + [
        total[3 + index] + (weight * closing[index] - rate * pulled[index]) for index in range(3)
    ]


def main_kernel(
    devices,
    own_count,
    sizes,
    listed_from,
    field,
    out_place,
    out_motion,
    out_pull,
    out_change,
    ahead,
    slab,
    table,
    names,
    guess,
    mid_field,
    mid_state,
    mid_names,
    result,
    listed,
    arrived,
):
    count_fine, count_mid, count_all = sizes
    blocks, blocks_fine = count_mid // 8, count_fine // 8
    groups = mid_field.shape[0]
    sub = lax.broadcasted_iota(jnp.int32, (8, lanes), 0)
    lane = lax.broadcasted_iota(jnp.int32, (8, lanes), 1)

    def spread(column):
        return jnp.broadcast_to(column, (8, lanes))

    def lane_total(value):
        return spread(jnp.sum(value, axis=1, keepdims=True))

    def loop(count, body):
        if count <= 4:
            for index in range(count):
                body(index)
        else:
            pl.loop(0, count)(body)

    def rows8(index):
        return pl.ds(index * 8 if isinstance(index, int) else pl.multiple_of(index * 8, 8), 8)

    halves = [slice(0, lanes), slice(lanes, 2 * lanes)]
    me = lax.axis_index("stars")
    first = me * own_count

    copy = pltpu.make_async_copy(listed_from, listed, arrived)
    copy.start()

    def look_ahead(index):
        for half in range(2):
            upper = field[pl.ds(pl.multiple_of(index * 16, 16), 8), halves[half]]
            lower = field[pl.ds(pl.multiple_of(index * 16 + 8, 8), 8), halves[half]]
            turned = pltpu.roll(lower, 4, 0)
            slope = unit * jnp.where(sub < 4, pltpu.roll(upper, 4, 0), turned)
            bend = unit**2 * lower
            twist = jnp.where(sub < 3, unit**3 * turned, 0.0)
            way = slope + 0.5 * bend + twist * (1.0 / 6.0)
            change, second = way, bend + twist
            for step in range(4):
                ahead[step, index * 2 + half] = upper + way
                if step < 3:
                    change = change + second
                    second = second + twist
                    way = way + change

    together = min(4, devices)

    @pl.loop(0, devices // together)
    def _(index):
        for inner in range(together):
            look_ahead(index * together + inner)

    copy.wait()
    count = listed[0]

    mine = pl.multiple_of(slot_of(me, me, devices) * 16, 16)

    def own(part, component, half):
        tile = field[pl.ds(pl.multiple_of(mine + part // 2 * 8, 8), 8), halves[half]]
        at = part % 2 * 4 + component
        return tile[at : at + 1, :]

    def fetch(block):
        room = block if isinstance(block, int) else 0
        name = jnp.zeros((8, lanes), jnp.int32)
        for row in range(8):
            at = 1 + padded(count_all, own_count) + block * 8 + row
            star = listed[at]
            base = pl.multiple_of(listed[at + count_mid], 16)
            side = pl.multiple_of(listed[at + 2 * count_mid], lanes)
            slab[room, 16 * row : 16 * row + 16, :] = field[pl.ds(base, 16), pl.ds(side, lanes)]
            name = jnp.where(sub == row, star, name)
        names[rows8(block), :] = name
        hit = (name & (lanes - 1)) == lane
        for part in range(4):
            for component in range(3):
                value = slab[room, pl.ds(4 * part + component, 8, stride=16), :]
                table[3 * part + component, rows8(block), :] = lane_total(jnp.where(hit, value, 0.0))
        mass = slab[room, pl.ds(15, 8, stride=16), :]
        table[12, rows8(block), :] = -lane_total(jnp.where(hit, mass, 0.0))

    loop(blocks, fetch)
    slow = [own(0, 3, half) > 0.0 for half in range(2)]

    def turn(ref, group, *at):
        total = jnp.zeros((8, lanes), ref.dtype)
        for inner in range(min(16, blocks)):
            value = ref[(*at, rows8(group * 16 + inner), slice(None))]
            total = total + jnp.where(lane == sub + inner * 8, value, jnp.zeros_like(value))
        return jnp.sum(total, axis=0, keepdims=True)

    def fixed(group):
        mid_field[group, 6:7, :] = turn(table, group, 12)
        found = turn(names, group)
        if blocks * 8 < lanes:
            found = jnp.where(lane[0:1, :] < blocks * 8, found, -2)
        mid_names[group, 0:1, :] = found

    def nothing():
        pass

    def elapse_of(step, fine):
        return unit * (1 if fine or step % 2 == 0 else 2)

    def guess_block(step, fine, block):
        state = [table[index, rows8(block), :] for index in range(12)]
        elapse = elapse_of(step, fine)
        for index in range(3):
            moved, sped = predict(
                state[index], state[3 + index], state[6 + index], state[9 + index], elapse
            )
            guess[index, rows8(block), :] = moved
            guess[3 + index, rows8(block), :] = sped

    def place_mid(group):
        for index in range(6):
            mid_field[group, index : index + 1, :] = turn(guess, group, index)

    def force(step, targets, beside):
        def add(totals, row):
            return [pair_terms(target, row, total) for target, total in zip(targets, totals)]

        def one(index, totals):
            for half in range(2):
                row = [ahead[step, index * 2 + half, k : k + 1, :] for k in (0, 1, 2, 4, 5, 6, 3)]
                totals = add(totals, row)
            return totals

        together = min(8, devices)

        def some(index, totals):
            for inner in range(together):
                totals = one(index * together + inner, totals)
            return totals

        zero = jnp.zeros((8, lanes), jnp.float32)
        totals = [[zero] * 6 for _ in targets]
        most = devices // together - 1
        totals = lax.fori_loop(0, most, some, totals)
        beside()
        totals = some(most, totals)
        for group in range(groups):
            totals = add(totals, [mid_field[group, k : k + 1, :] for k in range(7)])
        return [[lane_total(value) for value in total] for total in totals]

    for step in range(4):
        loop(blocks_fine, functools.partial(guess_block, step, True))

        def prepare(step=step):
            if step == 0:
                loop(groups, fixed)
            loop(blocks - blocks_fine, lambda block: guess_block(step, False, block + blocks_fine))
            loop(groups, place_mid)

        if step == 3:
            break
        apart = blocks_fine // 2 > 4
        if apart:
            prepare()

        def advance(pair, step, fine):
            targets = [
                [guess[index, rows8(2 * pair + side), :] for index in range(6)] for side in range(2)
            ]
            elapse = elapse_of(step, fine)
            early = apart or not fine or pair > 0
            for side, total in enumerate(force(step, targets, nothing if early else prepare)):
                rows = rows8(2 * pair + side)
                for index in range(3):
                    moved, sped = correct(
                        *[table[3 * part + index, rows, :] for part in range(4)],
                        total[index],
                        total[3 + index],
                        elapse,
                    )
                    table[index, rows, :] = moved
                    table[3 + index, rows, :] = sped
                    table[6 + index, rows, :] = total[index]
                    table[9 + index, rows, :] = total[3 + index]

        loop(blocks_fine // 2, functools.partial(advance, step=step, fine=True))
        if step == 1:
            loop(
                (blocks - blocks_fine) // 2,
                lambda pair: advance(pair + blocks_fine // 2, step=1, fine=False),
            )

    def keep(group):
        for index in range(12):
            mid_state[group, index : index + 1, :] = turn(table, group, index)

    loop(groups, keep)
    result[...] = jnp.zeros_like(result)

    def finish(wide, turn_at):
        hits, states, elapses, targets = [], [], [], []
        for side in range(wide):
            name = jnp.zeros((8, lanes), jnp.int32)
            for row in range(8):
                star = listed[1 + (turn_at * wide + side) * 8 + row]
                name = jnp.where(sub == row, star, name)
            own_hit = [name == lane + (first + half * lanes) for half in range(2)]
            coarse = [own_hit[half] & slow[half] for half in range(2)]
            mid_hit = [name == mid_names[group, 0:1, :] for group in range(groups)]

            def find(part, component):
                total = jnp.zeros((8, lanes), jnp.float32)
                for half in range(2):
                    total = jnp.where(coarse[half], own(part, component, half), total)
                for group in range(groups):
                    at = 3 * part + component
                    total = jnp.where(mid_hit[group], mid_state[group, at : at + 1, :], total)
                return lane_total(total)

            total = jnp.zeros((8, lanes), jnp.float32)
            for half in range(2):
                total = jnp.where(coarse[half], 4 * unit, total)
            for group in range(groups):
                fine = jnp.where(lane + group * lanes < count_fine, unit, 2 * unit)
                total = jnp.where(mid_hit[group], fine, total)
            elapse = lane_total(total)
            state = [[find(part, index) for index in range(3)] for part in range(4)]
            pairs = [
                predict(*[state[part][index] for part in range(4)], elapse) for index in range(3)
            ]
            hits.append(own_hit)
            states.append(state)
            elapses.append(elapse)
            targets.append([pair[0] for pair in pairs] + [pair[1] for pair in pairs])
        for side, total in enumerate(force(3, targets, prepare)):
            for index in range(3):
                moved, sped = correct(
                    *[states[side][part][index] for part in range(4)],
                    total[index],
                    total[3 + index],
                    elapses[side],
                )
                for part, value in enumerate((moved, sped, total[index], total[3 + index])):
                    for half in range(2):
                        result[part, half, index] += jnp.where(hits[side][half], value, 0.0)

    @pl.when((count > 0) & (count <= 16))
    def _():
        finish(2, 0)

    @pl.when(count > 16)
    def _():
        pl.loop(0, (count + 23) // 24)(functools.partial(finish, 3))

    for part, ref in enumerate((out_place, out_motion, out_pull, out_change)):
        for half in range(2):
            changed = own(3, 3, half) < 0.0
            for index in range(3):
                value = jnp.sum(result[part, half, index], axis=0, keepdims=True)
                ref[index : index + 1, halves[half]] = jnp.where(
                    changed, value, own(part, index, half)
                )


def body(devices, place, motion, pull, change, masses, star_level, fine, mid, every):
    own_count = place.shape[1]
    assert own_count == 2 * lanes
    sizes = (fine.shape[0], mid.shape[0], every.shape[0])
    groups = -(-sizes[1] // lanes)
    held = [pltpu.VMEM((3, own_count), jnp.float32)] * 4
    held += [pltpu.VMEM((2, lanes), jnp.float32), pltpu.VMEM((2, lanes), jnp.int32)]
    block = pl.pallas_call(
        pack_kernel,
        out_shape=jax.ShapeDtypeStruct((16, own_count), jnp.float32),
        in_specs=[pl.BlockSpec(memory_space=pl.ANY)] * 6,
        out_specs=vmem,
        scratch_shapes=held + [pltpu.SemaphoreType.DMA((6,))],
        name="pack",
    )(place, motion, pull, change, masses.reshape(2, lanes), star_level.reshape(2, lanes))

    listed_shape = (1 + padded(sizes[2], own_count) + 3 * sizes[1],)

    def plan(lists):
        return pl.pallas_call(
            functools.partial(plan_kernel, devices, own_count),
            out_shape=jax.ShapeDtypeStruct(listed_shape, jnp.int32),
            in_specs=[smem] * 3,
            out_specs=smem,
            compiler_params=pltpu.CompilerParams(vmem_limit_bytes=1024 * 1024),
            name="plan",
        )(*lists)

    whole, listed = gather(block, devices, (fine, mid, every), plan)
    room = devices * 52 * 1024 + sizes[1] * 12 * 1024 + 3 * 1024 * 1024
    result = jax.ShapeDtypeStruct((3, own_count), jnp.float32)
    return pl.pallas_call(
        functools.partial(main_kernel, devices, own_count, sizes),
        out_shape=(result,) * 4,
        in_specs=[pl.BlockSpec(memory_space=pl.ANY), vmem],
        out_specs=(vmem,) * 4,
        scratch_shapes=[
            pltpu.VMEM((4, devices * 2, 8, lanes), jnp.float32),
            pltpu.VMEM((min(4, sizes[1] // 8), 8 * 16, lanes), jnp.float32),
            pltpu.VMEM((13, sizes[1], lanes), jnp.float32),
            pltpu.VMEM((sizes[1], lanes), jnp.int32),
            pltpu.VMEM((6, sizes[1], lanes), jnp.float32),
            pltpu.VMEM((groups, 8, lanes), jnp.float32),
            pltpu.VMEM((groups, 16, lanes), jnp.float32),
            pltpu.VMEM((groups, 8, lanes), jnp.int32),
            pltpu.VMEM((4, 2, 3, 8, lanes), jnp.float32),
            pltpu.SMEM(listed_shape, jnp.int32),
            pltpu.SemaphoreType.DMA,
        ],
        compiler_params=pltpu.CompilerParams(vmem_limit_bytes=room),
        name="steps",
    )(listed, whole)


def solution(mesh):
    split = P(None, "stars")
    return jax.shard_map(
        functools.partial(body, mesh.shape["stars"]),
        mesh=mesh,
        in_specs=(split,) * 4 + (P("stars"),) * 2 + (P(),) * 3,
        out_specs=(split,) * 4,
        check_vma=False,
    )
```

```python
import functools

import jax
import jax.numpy as jnp
from jax import lax
from jax.experimental import pallas as pl
from jax.experimental.pallas import tpu as pltpu
from jax.sharding import PartitionSpec as P

softening = 0.0001
unit = 1.0 / 128.0
lanes = 128
vmem = pl.BlockSpec(memory_space=pltpu.VMEM)
smem = pl.BlockSpec(memory_space=pltpu.SMEM)


def predict(place, motion, pull, change, elapse):
    moved = place + elapse * (motion + elapse * (0.5 * pull + elapse * change * (1.0 / 6.0)))
    sped = motion + elapse * (pull + 0.5 * elapse * change)
    return moved, sped


def correct(place, motion, pull, change, pull_new, change_new, elapse):
    square = elapse * elapse * (1.0 / 12.0)
    sped = motion + 0.5 * elapse * (pull + pull_new) + square * (change - change_new)
    moved = place + 0.5 * elapse * (motion + sped) + square * (pull - pull_new)
    return moved, sped


def pack_kernel(place, motion, pull, change, mass, level, out, *held):
    place_at, motion_at, pull_at, change_at, mass_at, level_at, arrived = held
    sources = (place, motion, pull, change, mass, level)
    copies = [
        pltpu.make_async_copy(source, target, arrived.at[index])
        for index, (source, target) in enumerate(zip(sources, held))
    ]
    for copy in copies:
        copy.start()
    for copy in copies:
        copy.wait()
    out[7:8, :] = jnp.zeros((1, out.shape[1]), jnp.float32)
    out[11:12, :] = jnp.zeros((1, out.shape[1]), jnp.float32)
    for part, ref in enumerate((place_at, motion_at, pull_at, change_at)):
        out[4 * part : 4 * part + 3, :] = ref[...]
    for half in range(2):
        row = slice(half, half + 1)
        at = slice(half * lanes, (half + 1) * lanes)
        rank, heavy = level_at[row, :], mass_at[row, :]
        out[3:4, at] = jnp.where(rank <= 1, heavy, 0.0)
        out[15:16, at] = jnp.where(rank == 0, heavy, -heavy)


def padded(count_all, own):
    return -(-min(count_all, own) // 24) * 24


def plan_kernel(devices, own, fine, mid, every, listed):
    me = lax.axis_index("stars")
    first = me * own
    count_fine, count_mid, count_all = fine.shape[0], mid.shape[0], every.shape[0]
    room = padded(count_all, own)
    order = 1 + room

    def merge(index, seen):
        star = mid[index]
        listed[order + count_fine + index - seen] = star
        same = star == fine[jnp.minimum(seen, count_fine - 1)]
        return seen + same.astype(jnp.int32)

    lax.fori_loop(0, count_mid, merge, jnp.int32(0), unroll=8)

    def keep(index, carry):
        listed[order + index] = fine[index]
        return carry

    lax.fori_loop(0, count_fine, keep, 0, unroll=8)

    def locate(index, carry):
        star = listed[order + index]
        device = star >> (own.bit_length() - 1)
        listed[order + count_mid + index] = slot_of(device, me, devices) * 16
        listed[order + 2 * count_mid + index] = star & lanes
        return carry

    lax.fori_loop(0, count_mid, locate, 0, unroll=8)

    def below(bound):
        found = jnp.int32(0)
        for bit in reversed(range(count_all.bit_length())):
            at = found + (1 << bit)
            less = (at <= count_all) & (every[jnp.minimum(at, count_all) - 1] < bound)
            found = jnp.where(less, at, found)
        return found

    low = below(first)
    count = below(first + own) - low
    listed[0] = count

    def mine(index, carry):
        star = every[jnp.minimum(low + index, count_all - 1)]
        listed[1 + index] = jnp.where(index < count, star, -1)
        return carry

    lax.fori_loop(0, room, mine, 0, unroll=8)


def rounds_of(devices):
    bits = devices.bit_length() - 1
    assert devices == 1 << bits
    rounds = []
    high = bits
    while high > 1:
        width = 1 if high == 2 else 2
        high -= width
        rounds.append((1 << high, 1 << width))
    return rounds


def settle(value):
    return pl.pallas_call(
        lambda source, target: None,
        out_shape=jax.ShapeDtypeStruct(value.shape, value.dtype),
        in_specs=[pl.BlockSpec(memory_space=pl.ANY)],
        out_specs=pl.BlockSpec(memory_space=pl.ANY),
        input_output_aliases={0: 0},
        cost_estimate=pl.CostEstimate(flops=10**11, bytes_accessed=10**8, transcendentals=0),
        compiler_params=pltpu.CompilerParams(vmem_limit_bytes=1024 * 1024),
        name="settle",
    )(value)


def gather(block, devices, lists, plan):
    everyone = range(devices)
    odd = lax.axis_index("stars") % 2 == 1

    def fetch(value, even_by, odd_by):
        pairs = [(device, device ^ (odd_by if device % 2 else even_by)) for device in everyone]
        return lax.ppermute(value, "stars", pairs)

    def both(mine, other):
        return [jnp.where(odd, other, mine), jnp.where(odd, mine, other)]

    block = jnp.concatenate(both(block, fetch(block, 1, 1)), axis=0)
    rounds = rounds_of(devices)
    planned = None if rounds else plan(lists)
    for stride, radix in rounds:
        last = stride == rounds[-1][0]
        if last:
            block, lists = lax.optimization_barrier((block, lists))
            planned = plan(lists)
        if radix == 2:
            parts = [block, fetch(block, stride, stride)]
        elif last:
            half = block.shape[0] // 2
            one = fetch(block, stride, 3 * stride)
            two = jnp.where(odd, block[half:], block[:half])
            two = settle(fetch(two, 2 * stride, 2 * stride))
            parts = [block] + both(one, fetch(one, 1, 1)) + both(two, fetch(two, 1, 1))
        else:
            one = fetch(block, 2 * stride, 3 * stride)
            near = settle(fetch(block, stride, stride))
            second, third = both(one, fetch(one, 1, 1))
            parts = [block, second, near, third]
        block = jnp.concatenate(parts, axis=0)
    return block, planned


def slot_of(device, me, devices):
    slot, shift = device & 1, 1
    rounds = rounds_of(devices)
    for stride, radix in rounds:
        digit = ((device ^ me) >> (stride.bit_length() - 1)) & (radix - 1)
        if radix == 4:
            last = stride == rounds[-1][0]
            digit = digit ^ (digit >> 1) if last else (digit >> 1) | ((digit & 1) << 1)
        slot = slot | (digit << shift)
        shift += radix.bit_length() - 1
    return slot


def pair_terms(target, field, total):
    apart = [field[index] - target[index] for index in range(3)]
    closing = [field[3 + index] - target[3 + index] for index in range(3)]
    distance = apart[0] * apart[0] + apart[1] * apart[1] + (apart[2] * apart[2] + softening)
    inverse = lax.rsqrt(distance)
    square = inverse * inverse
    weight = field[6] * inverse * square
    dot = apart[0] * closing[0] + apart[1] * closing[1] + apart[2] * closing[2]
    rate = 3.0 * dot * square
    pulled = [weight * apart[index] for index in range(3)]
    return [total[index] + pulled[index] for index in range(3)] + [
        total[3 + index] + (weight * closing[index] - rate * pulled[index]) for index in range(3)
    ]


def main_kernel(
    devices,
    own_count,
    sizes,
    listed_from,
    field,
    out_place,
    out_motion,
    out_pull,
    out_change,
    ahead,
    slab,
    table,
    names,
    guess,
    mid_field,
    mid_state,
    mid_names,
    result,
    listed,
    arrived,
):
    count_fine, count_mid, count_all = sizes
    blocks, blocks_fine = count_mid // 8, count_fine // 8
    groups = mid_field.shape[0]
    sub = lax.broadcasted_iota(jnp.int32, (8, lanes), 0)
    lane = lax.broadcasted_iota(jnp.int32, (8, lanes), 1)

    def spread(column):
        return jnp.broadcast_to(column, (8, lanes))

    def lane_total(value):
        return spread(jnp.sum(value, axis=1, keepdims=True))

    def loop(count, body):
        if count <= 4:
            for index in range(count):
                body(index)
        else:
            pl.loop(0, count)(body)

    def rows8(index):
        return pl.ds(index * 8 if isinstance(index, int) else pl.multiple_of(index * 8, 8), 8)

    halves = [slice(0, lanes), slice(lanes, 2 * lanes)]
    me = lax.axis_index("stars")
    first = me * own_count

    copy = pltpu.make_async_copy(listed_from, listed, arrived)
    copy.start()

    def look_ahead(index):
        for half in range(2):
            upper = field[pl.ds(pl.multiple_of(index * 16, 16), 8), halves[half]]
            lower = field[pl.ds(pl.multiple_of(index * 16 + 8, 8), 8), halves[half]]
            turned = pltpu.roll(lower, 4, 0)
            slope = unit * jnp.where(sub < 4, pltpu.roll(upper, 4, 0), turned)
            bend = unit**2 * lower
            twist = jnp.where(sub < 3, unit**3 * turned, 0.0)
            way = slope + 0.5 * bend + twist * (1.0 / 6.0)
            change, second = way, bend + twist
            for step in range(4):
                ahead[step, index * 2 + half] = upper + way
                if step < 3:
                    change = change + second
                    second = second + twist
                    way = way + change

    together = min(4, devices)

    @pl.loop(0, devices // together)
    def _(index):
        for inner in range(together):
            look_ahead(index * together + inner)

    copy.wait()
    count = listed[0]

    mine = pl.multiple_of(slot_of(me, me, devices) * 16, 16)

    def own(part, component, half):
        tile = field[pl.ds(pl.multiple_of(mine + part // 2 * 8, 8), 8), halves[half]]
        at = part % 2 * 4 + component
        return tile[at : at + 1, :]

    def fetch(block):
        room = block if isinstance(block, int) else 0
        name = jnp.zeros((8, lanes), jnp.int32)
        for row in range(8):
            at = 1 + padded(count_all, own_count) + block * 8 + row
            star = listed[at]
            base = pl.multiple_of(listed[at + count_mid], 16)
            side = pl.multiple_of(listed[at + 2 * count_mid], lanes)
            slab[room, 16 * row : 16 * row + 16, :] = field[pl.ds(base, 16), pl.ds(side, lanes)]
            name = jnp.where(sub == row, star, name)
        names[rows8(block), :] = name
        hit = (name & (lanes - 1)) == lane
        for part in range(4):
            for component in range(3):
                value = slab[room, pl.ds(4 * part + component, 8, stride=16), :]
                table[3 * part + component, rows8(block), :] = lane_total(jnp.where(hit, value, 0.0))
        mass = slab[room, pl.ds(15, 8, stride=16), :]
        table[12, rows8(block), :] = -lane_total(jnp.where(hit, mass, 0.0))

    loop(blocks, fetch)
    slow = [own(0, 3, half) > 0.0 for half in range(2)]

    def turn(ref, group, *at):
        total = jnp.zeros((8, lanes), ref.dtype)
        for inner in range(min(16, blocks)):
            value = ref[(*at, rows8(group * 16 + inner), slice(None))]
            total = total + jnp.where(lane == sub + inner * 8, value, jnp.zeros_like(value))
        return jnp.sum(total, axis=0, keepdims=True)

    def fixed(group):
        mid_field[group, 6:7, :] = turn(table, group, 12)
        found = turn(names, group)
        if blocks * 8 < lanes:
            found = jnp.where(lane[0:1, :] < blocks * 8, found, -2)
        mid_names[group, 0:1, :] = found

    def nothing():
        pass

    def elapse_of(step, fine):
        return unit * (1 if fine or step % 2 == 0 else 2)

    def guess_block(step, fine, block):
        state = [table[index, rows8(block), :] for index in range(12)]
        elapse = elapse_of(step, fine)
        for index in range(3):
            moved, sped = predict(
                state[index], state[3 + index], state[6 + index], state[9 + index], elapse
            )
            guess[index, rows8(block), :] = moved
            guess[3 + index, rows8(block), :] = sped

    def place_mid(group):
        for index in range(6):
            mid_field[group, index : index + 1, :] = turn(guess, group, index)

    def force(step, targets, beside):
        def add(totals, row):
            return [pair_terms(target, row, total) for target, total in zip(targets, totals)]

        def one(index, totals):
            for half in range(2):
                row = [ahead[step, index * 2 + half, k : k + 1, :] for k in (0, 1, 2, 4, 5, 6, 3)]
                totals = add(totals, row)
            return totals

        together = min(4, devices)

        def some(index, totals):
            for inner in range(together):
                totals = one(index * together + inner, totals)
            return totals

        zero = jnp.zeros((8, lanes), jnp.float32)
        totals = [[zero] * 6 for _ in targets]
        most = devices // together - 1
        totals = lax.fori_loop(0, most, some, totals)
        beside()
        totals = some(most, totals)
        for group in range(groups):
            totals = add(totals, [mid_field[group, k : k + 1, :] for k in range(7)])
        return [[lane_total(value) for value in total] for total in totals]

    for step in range(4):
        loop(blocks_fine, functools.partial(guess_block, step, True))

        def prepare(step=step):
            if step == 0:
                loop(groups, fixed)
            loop(blocks - blocks_fine, lambda block: guess_block(step, False, block + blocks_fine))
            loop(groups, place_mid)

        if step == 3:
            break
        apart = blocks_fine // 2 > 4
        if apart:
            prepare()

        def advance(pair, step, fine):
            targets = [
                [guess[index, rows8(2 * pair + side), :] for index in range(6)] for side in range(2)
            ]
            elapse = elapse_of(step, fine)
            early = apart or not fine or pair > 0
            for side, total in enumerate(force(step, targets, nothing if early else prepare)):
                rows = rows8(2 * pair + side)
                for index in range(3):
                    moved, sped = correct(
                        *[table[3 * part + index, rows, :] for part in range(4)],
                        total[index],
                        total[3 + index],
                        elapse,
                    )
                    table[index, rows, :] = moved
                    table[3 + index, rows, :] = sped
                    table[6 + index, rows, :] = total[index]
                    table[9 + index, rows, :] = total[3 + index]

        loop(blocks_fine // 2, functools.partial(advance, step=step, fine=True))
        if step == 1:
            loop(
                (blocks - blocks_fine) // 2,
                lambda pair: advance(pair + blocks_fine // 2, step=1, fine=False),
            )

    def keep(group):
        for index in range(12):
            mid_state[group, index : index + 1, :] = turn(table, group, index)

    loop(groups, keep)
    result[...] = jnp.zeros_like(result)

    def finish(wide, turn_at):
        hits, states, elapses, targets = [], [], [], []
        for side in range(wide):
            name = jnp.zeros((8, lanes), jnp.int32)
            for row in range(8):
                star = listed[1 + (turn_at * wide + side) * 8 + row]
                name = jnp.where(sub == row, star, name)
            own_hit = [name == lane + (first + half * lanes) for half in range(2)]
            coarse = [own_hit[half] & slow[half] for half in range(2)]
            mid_hit = [name == mid_names[group, 0:1, :] for group in range(groups)]

            def find(part, component):
                total = jnp.zeros((8, lanes), jnp.float32)
                for half in range(2):
                    total = jnp.where(coarse[half], own(part, component, half), total)
                for group in range(groups):
                    at = 3 * part + component
                    total = jnp.where(mid_hit[group], mid_state[group, at : at + 1, :], total)
                return lane_total(total)

            total = jnp.zeros((8, lanes), jnp.float32)
            for half in range(2):
                total = jnp.where(coarse[half], 4 * unit, total)
            for group in range(groups):
                fine = jnp.where(lane + group * lanes < count_fine, unit, 2 * unit)
                total = jnp.where(mid_hit[group], fine, total)
            elapse = lane_total(total)
            state = [[find(part, index) for index in range(3)] for part in range(4)]
            pairs = [
                predict(*[state[part][index] for part in range(4)], elapse) for index in range(3)
            ]
            hits.append(own_hit)
            states.append(state)
            elapses.append(elapse)
            targets.append([pair[0] for pair in pairs] + [pair[1] for pair in pairs])
        for side, total in enumerate(force(3, targets, prepare)):
            for index in range(3):
                moved, sped = correct(
                    *[states[side][part][index] for part in range(4)],
                    total[index],
                    total[3 + index],
                    elapses[side],
                )
                for part, value in enumerate((moved, sped, total[index], total[3 + index])):
                    for half in range(2):
                        result[part, half, index] += jnp.where(hits[side][half], value, 0.0)

    @pl.when((count > 0) & (count <= 16))
    def _():
        finish(2, 0)

    @pl.when(count > 16)
    def _():
        pl.loop(0, (count + 23) // 24)(functools.partial(finish, 3))

    for part, ref in enumerate((out_place, out_motion, out_pull, out_change)):
        for half in range(2):
            changed = own(3, 3, half) < 0.0
            for index in range(3):
                value = jnp.sum(result[part, half, index], axis=0, keepdims=True)
                ref[index : index + 1, halves[half]] = jnp.where(
                    changed, value, own(part, index, half)
                )


def body(devices, place, motion, pull, change, masses, star_level, fine, mid, every):
    own_count = place.shape[1]
    assert own_count == 2 * lanes
    sizes = (fine.shape[0], mid.shape[0], every.shape[0])
    groups = -(-sizes[1] // lanes)
    held = [pltpu.VMEM((3, own_count), jnp.float32)] * 4
    held += [pltpu.VMEM((2, lanes), jnp.float32), pltpu.VMEM((2, lanes), jnp.int32)]
    block = pl.pallas_call(
        pack_kernel,
        out_shape=jax.ShapeDtypeStruct((16, own_count), jnp.float32),
        in_specs=[pl.BlockSpec(memory_space=pl.ANY)] * 6,
        out_specs=vmem,
        scratch_shapes=held + [pltpu.SemaphoreType.DMA((6,))],
        name="pack",
    )(place, motion, pull, change, masses.reshape(2, lanes), star_level.reshape(2, lanes))

    listed_shape = (1 + padded(sizes[2], own_count) + 3 * sizes[1],)

    def plan(lists):
        return pl.pallas_call(
            functools.partial(plan_kernel, devices, own_count),
            out_shape=jax.ShapeDtypeStruct(listed_shape, jnp.int32),
            in_specs=[smem] * 3,
            out_specs=smem,
            compiler_params=pltpu.CompilerParams(vmem_limit_bytes=1024 * 1024),
            name="plan",
        )(*lists)

    whole, listed = gather(block, devices, (fine, mid, every), plan)
    room = devices * 52 * 1024 + sizes[1] * 12 * 1024 + 3 * 1024 * 1024
    result = jax.ShapeDtypeStruct((3, own_count), jnp.float32)
    return pl.pallas_call(
        functools.partial(main_kernel, devices, own_count, sizes),
        out_shape=(result,) * 4,
        in_specs=[pl.BlockSpec(memory_space=pl.ANY), vmem],
        out_specs=(vmem,) * 4,
        scratch_shapes=[
            pltpu.VMEM((4, devices * 2, 8, lanes), jnp.float32),
            pltpu.VMEM((min(4, sizes[1] // 8), 8 * 16, lanes), jnp.float32),
            pltpu.VMEM((13, sizes[1], lanes), jnp.float32),
            pltpu.VMEM((sizes[1], lanes), jnp.int32),
            pltpu.VMEM((6, sizes[1], lanes), jnp.float32),
            pltpu.VMEM((groups, 8, lanes), jnp.float32),
            pltpu.VMEM((groups, 16, lanes), jnp.float32),
            pltpu.VMEM((groups, 8, lanes), jnp.int32),
            pltpu.VMEM((4, 2, 3, 8, lanes), jnp.float32),
            pltpu.SMEM(listed_shape, jnp.int32),
            pltpu.SemaphoreType.DMA,
        ],
        compiler_params=pltpu.CompilerParams(vmem_limit_bytes=room),
        name="steps",
    )(listed, whole)


def solution(mesh):
    split = P(None, "stars")
    return jax.shard_map(
        functools.partial(body, mesh.shape["stars"]),
        mesh=mesh,
        in_specs=(split,) * 4 + (P("stars"),) * 2 + (P(),) * 3,
        out_specs=(split,) * 4,
        check_vma=False,
    )
```

```python
import functools

import jax
import jax.numpy as jnp
from jax import lax
from jax.experimental import pallas as pl
from jax.experimental.pallas import tpu as pltpu
from jax.sharding import PartitionSpec as P

softening = 0.0001
unit = 1.0 / 128.0
lanes = 128
vmem = pl.BlockSpec(memory_space=pltpu.VMEM)
smem = pl.BlockSpec(memory_space=pltpu.SMEM)


def predict(place, motion, pull, change, elapse):
    moved = place + elapse * (motion + elapse * (0.5 * pull + elapse * change * (1.0 / 6.0)))
    sped = motion + elapse * (pull + 0.5 * elapse * change)
    return moved, sped


def correct(place, motion, pull, change, pull_new, change_new, elapse):
    square = elapse * elapse * (1.0 / 12.0)
    sped = motion + 0.5 * elapse * (pull + pull_new) + square * (change - change_new)
    moved = place + 0.5 * elapse * (motion + sped) + square * (pull - pull_new)
    return moved, sped


def pack_kernel(place, motion, pull, change, mass, level, out, *held):
    place_at, motion_at, pull_at, change_at, mass_at, level_at, arrived = held
    sources = (place, motion, pull, change, mass, level)
    copies = [
        pltpu.make_async_copy(source, target, arrived.at[index])
        for index, (source, target) in enumerate(zip(sources, held))
    ]
    for copy in copies:
        copy.start()
    for copy in copies:
        copy.wait()
    out[7:8, :] = jnp.zeros((1, out.shape[1]), jnp.float32)
    out[11:12, :] = jnp.zeros((1, out.shape[1]), jnp.float32)
    for part, ref in enumerate((place_at, motion_at, pull_at, change_at)):
        out[4 * part : 4 * part + 3, :] = ref[...]
    for half in range(2):
        row = slice(half, half + 1)
        at = slice(half * lanes, (half + 1) * lanes)
        rank, heavy = level_at[row, :], mass_at[row, :]
        out[3:4, at] = jnp.where(rank <= 1, heavy, 0.0)
        out[15:16, at] = jnp.where(rank == 0, heavy, -heavy)


def padded(count_all, own):
    return -(-min(count_all, own) // 24) * 24


def plan_kernel(devices, own, fine, mid, every, listed):
    me = lax.axis_index("stars")
    first = me * own
    count_fine, count_mid, count_all = fine.shape[0], mid.shape[0], every.shape[0]
    room = padded(count_all, own)
    order = 1 + room

    def merge(index, seen):
        star = mid[index]
        listed[order + count_fine + index - seen] = star
        same = star == fine[jnp.minimum(seen, count_fine - 1)]
        return seen + same.astype(jnp.int32)

    lax.fori_loop(0, count_mid, merge, jnp.int32(0), unroll=8)

    def keep(index, carry):
        listed[order + index] = fine[index]
        return carry

    lax.fori_loop(0, count_fine, keep, 0, unroll=8)

    def locate(index, carry):
        star = listed[order + index]
        device = star >> (own.bit_length() - 1)
        listed[order + count_mid + index] = slot_of(device, me, devices) * 16
        listed[order + 2 * count_mid + index] = star & lanes
        return carry

    lax.fori_loop(0, count_mid, locate, 0, unroll=8)

    def below(bound):
        found = jnp.int32(0)
        for bit in reversed(range(count_all.bit_length())):
            at = found + (1 << bit)
            less = (at <= count_all) & (every[jnp.minimum(at, count_all) - 1] < bound)
            found = jnp.where(less, at, found)
        return found

    low = below(first)
    count = below(first + own) - low
    listed[0] = count

    def mine(index, carry):
        star = every[jnp.minimum(low + index, count_all - 1)]
        listed[1 + index] = jnp.where(index < count, star, -1)
        return carry

    lax.fori_loop(0, room, mine, 0, unroll=8)


def rounds_of(devices):
    bits = devices.bit_length() - 1
    assert devices == 1 << bits
    rounds = []
    high = bits
    while high > 1:
        width = 1 if high == 2 else 2
        high -= width
        rounds.append((1 << high, 1 << width))
    return rounds


def settle(value):
    return pl.pallas_call(
        lambda source, target: None,
        out_shape=jax.ShapeDtypeStruct(value.shape, value.dtype),
        in_specs=[pl.BlockSpec(memory_space=pl.ANY)],
        out_specs=pl.BlockSpec(memory_space=pl.ANY),
        input_output_aliases={0: 0},
        cost_estimate=pl.CostEstimate(flops=10**11, bytes_accessed=10**8, transcendentals=0),
        compiler_params=pltpu.CompilerParams(vmem_limit_bytes=1024 * 1024),
        name="settle",
    )(value)


def gather(block, devices, lists, plan):
    everyone = range(devices)
    odd = lax.axis_index("stars") % 2 == 1

    def fetch(value, even_by, odd_by):
        pairs = [(device, device ^ (odd_by if device % 2 else even_by)) for device in everyone]
        return lax.ppermute(value, "stars", pairs)

    def both(mine, other):
        return [jnp.where(odd, other, mine), jnp.where(odd, mine, other)]

    block = jnp.concatenate(both(block, fetch(block, 1, 1)), axis=0)
    rounds = rounds_of(devices)
    planned = None if rounds else plan(lists)
    for stride, radix in rounds:
        last = stride == rounds[-1][0]
        if last:
            block, lists = lax.optimization_barrier((block, lists))
            planned = plan(lists)
        if radix == 2:
            parts = [block, fetch(block, stride, stride)]
        elif last:
            half = block.shape[0] // 2
            one = fetch(block, stride, 3 * stride)
            two = jnp.where(odd, block[half:], block[:half])
            two = settle(fetch(two, 2 * stride, 2 * stride))
            parts = [block] + both(one, fetch(one, 1, 1)) + both(two, fetch(two, 1, 1))
        else:
            one = fetch(block, 2 * stride, 3 * stride)
            near = settle(fetch(block, stride, stride))
            second, third = both(one, fetch(one, 1, 1))
            parts = [block, second, near, third]
        block = jnp.concatenate(parts, axis=0)
    return block, planned


def slot_of(device, me, devices):
    slot, shift = device & 1, 1
    rounds = rounds_of(devices)
    for stride, radix in rounds:
        digit = ((device ^ me) >> (stride.bit_length() - 1)) & (radix - 1)
        if radix == 4:
            last = stride == rounds[-1][0]
            digit = digit ^ (digit >> 1) if last else (digit >> 1) | ((digit & 1) << 1)
        slot = slot | (digit << shift)
        shift += radix.bit_length() - 1
    return slot


def pair_terms(target, field, total):
    apart = [field[index] - target[index] for index in range(3)]
    closing = [field[3 + index] - target[3 + index] for index in range(3)]
    distance = apart[0] * apart[0] + apart[1] * apart[1] + (apart[2] * apart[2] + softening)
    inverse = lax.rsqrt(distance)
    square = inverse * inverse
    weight = field[6] * inverse * square
    dot = apart[0] * closing[0] + apart[1] * closing[1] + apart[2] * closing[2]
    rate = 3.0 * dot * square
    pulled = [weight * apart[index] for index in range(3)]
    return [total[index] + pulled[index] for index in range(3)] + [
        total[3 + index] + (weight * closing[index] - rate * pulled[index]) for index in range(3)
    ]


def main_kernel(
    devices,
    own_count,
    sizes,
    listed_from,
    field,
    out_place,
    out_motion,
    out_pull,
    out_change,
    ahead,
    slab,
    table,
    names,
    guess,
    mid_field,
    mid_state,
    mid_names,
    result,
    listed,
    arrived,
):
    count_fine, count_mid, count_all = sizes
    blocks, blocks_fine = count_mid // 8, count_fine // 8
    groups = mid_field.shape[0]
    sub = lax.broadcasted_iota(jnp.int32, (8, lanes), 0)
    lane = lax.broadcasted_iota(jnp.int32, (8, lanes), 1)

    def spread(column):
        return jnp.broadcast_to(column, (8, lanes))

    def lane_total(value):
        return spread(jnp.sum(value, axis=1, keepdims=True))

    def loop(count, body):
        if count <= 4:
            for index in range(count):
                body(index)
        else:
            pl.loop(0, count)(body)

    def rows8(index):
        return pl.ds(index * 8 if isinstance(index, int) else pl.multiple_of(index * 8, 8), 8)

    halves = [slice(0, lanes), slice(lanes, 2 * lanes)]
    me = lax.axis_index("stars")
    first = me * own_count

    copy = pltpu.make_async_copy(listed_from, listed, arrived)
    copy.start()

    def look_ahead(index):
        for half in range(2):
            upper = field[pl.ds(pl.multiple_of(index * 16, 16), 8), halves[half]]
            lower = field[pl.ds(pl.multiple_of(index * 16 + 8, 8), 8), halves[half]]
            turned = pltpu.roll(lower, 4, 0)
            slope = unit * jnp.where(sub < 4, pltpu.roll(upper, 4, 0), turned)
            bend = unit**2 * lower
            twist = jnp.where(sub < 3, unit**3 * turned, 0.0)
            way = slope + 0.5 * bend + twist * (1.0 / 6.0)
            change, second = way, bend + twist
            for step in range(4):
                ahead[step, index * 2 + half] = upper + way
                if step < 3:
                    change = change + second
                    second = second + twist
                    way = way + change

    together = min(4, devices)

    @pl.loop(0, devices // together)
    def _(index):
        for inner in range(together):
            look_ahead(index * together + inner)

    copy.wait()
    count = listed[0]

    mine = pl.multiple_of(slot_of(me, me, devices) * 16, 16)

    def own(part, component, half):
        tile = field[pl.ds(pl.multiple_of(mine + part // 2 * 8, 8), 8), halves[half]]
        at = part % 2 * 4 + component
        return tile[at : at + 1, :]

    def fetch(block):
        room = block if isinstance(block, int) else 0
        name = jnp.zeros((8, lanes), jnp.int32)
        for row in range(8):
            at = 1 + padded(count_all, own_count) + block * 8 + row
            star = listed[at]
            base = pl.multiple_of(listed[at + count_mid], 16)
            side = pl.multiple_of(listed[at + 2 * count_mid], lanes)
            slab[room, 16 * row : 16 * row + 16, :] = field[pl.ds(base, 16), pl.ds(side, lanes)]
            name = jnp.where(sub == row, star, name)
        names[rows8(block), :] = name
        hit = (name & (lanes - 1)) == lane
        for part in range(4):
            for component in range(3):
                value = slab[room, pl.ds(4 * part + component, 8, stride=16), :]
                table[3 * part + component, rows8(block), :] = lane_total(jnp.where(hit, value, 0.0))
        mass = slab[room, pl.ds(15, 8, stride=16), :]
        table[12, rows8(block), :] = -lane_total(jnp.where(hit, mass, 0.0))

    loop(blocks, fetch)
    slow = [own(0, 3, half) > 0.0 for half in range(2)]

    def turn(ref, group, *at):
        total = jnp.zeros((8, lanes), ref.dtype)
        for inner in range(min(16, blocks)):
            value = ref[(*at, rows8(group * 16 + inner), slice(None))]
            total = total + jnp.where(lane == sub + inner * 8, value, jnp.zeros_like(value))
        return jnp.sum(total, axis=0, keepdims=True)

    def fixed(group):
        mid_field[group, 6:7, :] = turn(table, group, 12)
        found = turn(names, group)
        if blocks * 8 < lanes:
            found = jnp.where(lane[0:1, :] < blocks * 8, found, -2)
        mid_names[group, 0:1, :] = found

    def nothing():
        pass

    def elapse_of(step, fine):
        return unit * (1 if fine or step % 2 == 0 else 2)

    def guess_block(step, fine, block):
        state = [table[index, rows8(block), :] for index in range(12)]
        elapse = elapse_of(step, fine)
        for index in range(3):
            moved, sped = predict(
                state[index], state[3 + index], state[6 + index], state[9 + index], elapse
            )
            guess[index, rows8(block), :] = moved
            guess[3 + index, rows8(block), :] = sped

    def place_mid(group):
        for index in range(6):
            mid_field[group, index : index + 1, :] = turn(guess, group, index)

    def force(step, targets, beside):
        def add(totals, row):
            return [pair_terms(target, row, total) for target, total in zip(targets, totals)]

        def one(index, totals):
            for half in range(2):
                row = [ahead[step, index * 2 + half, k : k + 1, :] for k in (0, 1, 2, 4, 5, 6, 3)]
                totals = add(totals, row)
            return totals

        together = min(4, devices)

        def some(index, totals):
            for inner in range(together):
                totals = one(index * together + inner, totals)
            return totals

        zero = jnp.zeros((8, lanes), jnp.float32)
        totals = [[zero] * 6 for _ in targets]
        most = devices // together - 1
        totals = lax.fori_loop(0, most, some, totals)
        beside()
        totals = some(most, totals)
        for group in range(groups):
            totals = add(totals, [mid_field[group, k : k + 1, :] for k in range(7)])
        return [[lane_total(value) for value in total] for total in totals]

    for step in range(4):
        loop(blocks_fine, functools.partial(guess_block, step, True))

        def prepare(step=step):
            if step == 0:
                loop(groups, fixed)
            if step != 1 or blocks > 4:
                loop(
                    blocks - blocks_fine,
                    lambda block: guess_block(step, False, block + blocks_fine),
                )
            loop(groups, place_mid)

        if step == 3:
            break
        apart = blocks_fine // 2 > 4
        if apart:
            prepare()

        def advance(start, step, kinds, early):
            targets = [
                [guess[index, rows8(start + side), :] for index in range(6)]
                for side in range(len(kinds))
            ]
            totals = force(step, targets, nothing if early else prepare)
            for side, (fine, total) in enumerate(zip(kinds, totals)):
                rows = rows8(start + side)
                for index in range(3):
                    moved, sped = correct(
                        *[table[3 * part + index, rows, :] for part in range(4)],
                        total[index],
                        total[3 + index],
                        elapse_of(step, fine),
                    )
                    table[index, rows, :] = moved
                    table[3 + index, rows, :] = sped
                    table[6 + index, rows, :] = total[index]
                    table[9 + index, rows, :] = total[3 + index]

        if not apart:
            both = step == 1 and blocks <= 4
            kinds = [block < blocks_fine for block in range(blocks if both else blocks_fine)]
            if len(kinds) <= 4:
                for block in range(blocks_fine, len(kinds)):
                    guess_block(step, False, block)
                advance(0, step, kinds, False)
                if step == 1 and not both:
                    loop(
                        (blocks - blocks_fine) // 2,
                        lambda pair: advance(blocks_fine + 2 * pair, 1, [False] * 2, True),
                    )
                continue
            prepare()
        loop(blocks_fine // 2, lambda pair: advance(2 * pair, step, [True] * 2, True))
        if step == 1:
            loop(
                (blocks - blocks_fine) // 2,
                lambda pair: advance(blocks_fine + 2 * pair, 1, [False] * 2, True),
            )

    def keep(group):
        for index in range(12):
            mid_state[group, index : index + 1, :] = turn(table, group, index)

    loop(groups, keep)
    result[...] = jnp.zeros_like(result)

    def finish(wide, turn_at):
        hits, states, elapses, targets = [], [], [], []
        for side in range(wide):
            name = jnp.zeros((8, lanes), jnp.int32)
            for row in range(8):
                star = listed[1 + (turn_at * wide + side) * 8 + row]
                name = jnp.where(sub == row, star, name)
            own_hit = [name == lane + (first + half * lanes) for half in range(2)]
            coarse = [own_hit[half] & slow[half] for half in range(2)]
            mid_hit = [name == mid_names[group, 0:1, :] for group in range(groups)]

            def find(part, component):
                total = jnp.zeros((8, lanes), jnp.float32)
                for half in range(2):
                    total = jnp.where(coarse[half], own(part, component, half), total)
                for group in range(groups):
                    at = 3 * part + component
                    total = jnp.where(mid_hit[group], mid_state[group, at : at + 1, :], total)
                return lane_total(total)

            total = jnp.zeros((8, lanes), jnp.float32)
            for half in range(2):
                total = jnp.where(coarse[half], 4 * unit, total)
            for group in range(groups):
                fine = jnp.where(lane + group * lanes < count_fine, unit, 2 * unit)
                total = jnp.where(mid_hit[group], fine, total)
            elapse = lane_total(total)
            state = [[find(part, index) for index in range(3)] for part in range(4)]
            pairs = [
                predict(*[state[part][index] for part in range(4)], elapse) for index in range(3)
            ]
            hits.append(own_hit)
            states.append(state)
            elapses.append(elapse)
            targets.append([pair[0] for pair in pairs] + [pair[1] for pair in pairs])
        for side, total in enumerate(force(3, targets, prepare)):
            for index in range(3):
                moved, sped = correct(
                    *[states[side][part][index] for part in range(4)],
                    total[index],
                    total[3 + index],
                    elapses[side],
                )
                for part, value in enumerate((moved, sped, total[index], total[3 + index])):
                    for half in range(2):
                        result[part, half, index] += jnp.where(hits[side][half], value, 0.0)

    @pl.when((count > 0) & (count <= 16))
    def _():
        finish(2, 0)

    @pl.when(count > 16)
    def _():
        pl.loop(0, (count + 23) // 24)(functools.partial(finish, 3))

    for part, ref in enumerate((out_place, out_motion, out_pull, out_change)):
        for half in range(2):
            changed = own(3, 3, half) < 0.0
            for index in range(3):
                value = jnp.sum(result[part, half, index], axis=0, keepdims=True)
                ref[index : index + 1, halves[half]] = jnp.where(
                    changed, value, own(part, index, half)
                )


def body(devices, place, motion, pull, change, masses, star_level, fine, mid, every):
    own_count = place.shape[1]
    assert own_count == 2 * lanes
    sizes = (fine.shape[0], mid.shape[0], every.shape[0])
    groups = -(-sizes[1] // lanes)
    held = [pltpu.VMEM((3, own_count), jnp.float32)] * 4
    held += [pltpu.VMEM((2, lanes), jnp.float32), pltpu.VMEM((2, lanes), jnp.int32)]
    block = pl.pallas_call(
        pack_kernel,
        out_shape=jax.ShapeDtypeStruct((16, own_count), jnp.float32),
        in_specs=[pl.BlockSpec(memory_space=pl.ANY)] * 6,
        out_specs=vmem,
        scratch_shapes=held + [pltpu.SemaphoreType.DMA((6,))],
        name="pack",
    )(place, motion, pull, change, masses.reshape(2, lanes), star_level.reshape(2, lanes))

    listed_shape = (1 + padded(sizes[2], own_count) + 3 * sizes[1],)

    def plan(lists):
        return pl.pallas_call(
            functools.partial(plan_kernel, devices, own_count),
            out_shape=jax.ShapeDtypeStruct(listed_shape, jnp.int32),
            in_specs=[smem] * 3,
            out_specs=smem,
            compiler_params=pltpu.CompilerParams(vmem_limit_bytes=1024 * 1024),
            name="plan",
        )(*lists)

    whole, listed = gather(block, devices, (fine, mid, every), plan)
    room = devices * 52 * 1024 + sizes[1] * 12 * 1024 + 3 * 1024 * 1024
    result = jax.ShapeDtypeStruct((3, own_count), jnp.float32)
    return pl.pallas_call(
        functools.partial(main_kernel, devices, own_count, sizes),
        out_shape=(result,) * 4,
        in_specs=[pl.BlockSpec(memory_space=pl.ANY), vmem],
        out_specs=(vmem,) * 4,
        scratch_shapes=[
            pltpu.VMEM((4, devices * 2, 8, lanes), jnp.float32),
            pltpu.VMEM((min(4, sizes[1] // 8), 8 * 16, lanes), jnp.float32),
            pltpu.VMEM((13, sizes[1], lanes), jnp.float32),
            pltpu.VMEM((sizes[1], lanes), jnp.int32),
            pltpu.VMEM((6, sizes[1], lanes), jnp.float32),
            pltpu.VMEM((groups, 8, lanes), jnp.float32),
            pltpu.VMEM((groups, 16, lanes), jnp.float32),
            pltpu.VMEM((groups, 8, lanes), jnp.int32),
            pltpu.VMEM((4, 2, 3, 8, lanes), jnp.float32),
            pltpu.SMEM(listed_shape, jnp.int32),
            pltpu.SemaphoreType.DMA,
        ],
        compiler_params=pltpu.CompilerParams(vmem_limit_bytes=room),
        name="steps",
    )(listed, whole)


def solution(mesh):
    split = P(None, "stars")
    return jax.shard_map(
        functools.partial(body, mesh.shape["stars"]),
        mesh=mesh,
        in_specs=(split,) * 4 + (P("stars"),) * 2 + (P(),) * 3,
        out_specs=(split,) * 4,
        check_vma=False,
    )
```

```python
import functools

import jax
import jax.numpy as jnp
from jax import lax
from jax.experimental import pallas as pl
from jax.experimental.pallas import tpu as pltpu
from jax.sharding import PartitionSpec as P

softening = 0.0001
unit = 1.0 / 128.0
lanes = 128
vmem = pl.BlockSpec(memory_space=pltpu.VMEM)
smem = pl.BlockSpec(memory_space=pltpu.SMEM)


def predict(place, motion, pull, change, elapse):
    moved = place + elapse * (motion + elapse * (0.5 * pull + elapse * change * (1.0 / 6.0)))
    sped = motion + elapse * (pull + 0.5 * elapse * change)
    return moved, sped


def correct(place, motion, pull, change, pull_new, change_new, elapse):
    square = elapse * elapse * (1.0 / 12.0)
    sped = motion + 0.5 * elapse * (pull + pull_new) + square * (change - change_new)
    moved = place + 0.5 * elapse * (motion + sped) + square * (pull - pull_new)
    return moved, sped


def pack_kernel(place, motion, pull, change, mass, level, out):
    out[7:8, :] = jnp.zeros((1, out.shape[1]), jnp.float32)
    out[11:12, :] = jnp.zeros((1, out.shape[1]), jnp.float32)
    for part, ref in enumerate((place, motion, pull, change)):
        out[4 * part : 4 * part + 3, :] = ref[...]
    for half in range(2):
        row = slice(half, half + 1)
        at = slice(half * lanes, (half + 1) * lanes)
        rank, heavy = level[row, :], mass[row, :]
        out[3:4, at] = jnp.where(rank <= 1, heavy, 0.0)
        out[15:16, at] = jnp.where(rank == 0, heavy, -heavy)


def padded(count_all, own):
    return -(-min(count_all, own) // 24) * 24


def plan_kernel(devices, own, fine, mid, every, listed):
    me = lax.axis_index("stars")
    first = me * own
    count_fine, count_mid, count_all = fine.shape[0], mid.shape[0], every.shape[0]
    room = padded(count_all, own)
    order = 1 + room

    def merge(index, seen):
        star = mid[index]
        listed[order + count_fine + index - seen] = star
        same = star == fine[jnp.minimum(seen, count_fine - 1)]
        return seen + same.astype(jnp.int32)

    lax.fori_loop(0, count_mid, merge, jnp.int32(0), unroll=8)

    def keep(index, carry):
        listed[order + index] = fine[index]
        return carry

    lax.fori_loop(0, count_fine, keep, 0, unroll=8)

    def locate(index, carry):
        star = listed[order + index]
        device = star >> (own.bit_length() - 1)
        listed[order + count_mid + index] = slot_of(device, me, devices) * 16
        listed[order + 2 * count_mid + index] = star & lanes
        return carry

    lax.fori_loop(0, count_mid, locate, 0, unroll=8)

    def below(bound):
        found = jnp.int32(0)
        for bit in reversed(range(count_all.bit_length())):
            at = found + (1 << bit)
            less = (at <= count_all) & (every[jnp.minimum(at, count_all) - 1] < bound)
            found = jnp.where(less, at, found)
        return found

    low = below(first)
    count = below(first + own) - low
    listed[0] = count

    def mine(index, carry):
        star = every[jnp.minimum(low + index, count_all - 1)]
        listed[1 + index] = jnp.where(index < count, star, -1)
        return carry

    lax.fori_loop(0, room, mine, 0, unroll=8)


def rounds_of(devices):
    bits = devices.bit_length() - 1
    assert devices == 1 << bits
    rounds = []
    high = bits
    while high > 1:
        width = 1 if high == 2 else 2
        high -= width
        rounds.append((1 << high, 1 << width))
    return rounds


def settle(value):
    return pl.pallas_call(
        lambda source, target: None,
        out_shape=jax.ShapeDtypeStruct(value.shape, value.dtype),
        in_specs=[pl.BlockSpec(memory_space=pl.ANY)],
        out_specs=pl.BlockSpec(memory_space=pl.ANY),
        input_output_aliases={0: 0},
        cost_estimate=pl.CostEstimate(flops=10**11, bytes_accessed=10**8, transcendentals=0),
        compiler_params=pltpu.CompilerParams(vmem_limit_bytes=1024 * 1024),
        name="settle",
    )(value)


def gather(block, devices, lists, plan):
    everyone = range(devices)
    odd = lax.axis_index("stars") % 2 == 1

    def fetch(value, even_by, odd_by):
        pairs = [(device, device ^ (odd_by if device % 2 else even_by)) for device in everyone]
        return lax.ppermute(value, "stars", pairs)

    def both(mine, other):
        return [jnp.where(odd, other, mine), jnp.where(odd, mine, other)]

    block = jnp.concatenate(both(block, fetch(block, 1, 1)), axis=0)
    rounds = rounds_of(devices)
    planned = None if rounds else plan(lists)
    for stride, radix in rounds:
        last = stride == rounds[-1][0]
        if last:
            block, lists = lax.optimization_barrier((block, lists))
            planned = plan(lists)
        if radix == 2:
            parts = [block, fetch(block, stride, stride)]
        elif last:
            half = block.shape[0] // 2
            one = fetch(block, stride, 3 * stride)
            two = jnp.where(odd, block[half:], block[:half])
            two = settle(fetch(two, 2 * stride, 2 * stride))
            parts = [block] + both(one, fetch(one, 1, 1)) + both(two, fetch(two, 1, 1))
        else:
            one = fetch(block, 2 * stride, 3 * stride)
            near = settle(fetch(block, stride, stride))
            second, third = both(one, fetch(one, 1, 1))
            parts = [block, second, near, third]
        block = jnp.concatenate(parts, axis=0)
    return block, planned


def slot_of(device, me, devices):
    slot, shift = device & 1, 1
    rounds = rounds_of(devices)
    for stride, radix in rounds:
        digit = ((device ^ me) >> (stride.bit_length() - 1)) & (radix - 1)
        if radix == 4:
            last = stride == rounds[-1][0]
            digit = digit ^ (digit >> 1) if last else (digit >> 1) | ((digit & 1) << 1)
        slot = slot | (digit << shift)
        shift += radix.bit_length() - 1
    return slot


def pair_terms(target, field, total):
    apart = [field[index] - target[index] for index in range(3)]
    closing = [field[3 + index] - target[3 + index] for index in range(3)]
    distance = apart[0] * apart[0] + apart[1] * apart[1] + (apart[2] * apart[2] + softening)
    inverse = lax.rsqrt(distance)
    square = inverse * inverse
    weight = field[6] * inverse * square
    dot = apart[0] * closing[0] + apart[1] * closing[1] + apart[2] * closing[2]
    rate = 3.0 * dot * square
    pulled = [weight * apart[index] for index in range(3)]
    return [total[index] + pulled[index] for index in range(3)] + [
        total[3 + index] + (weight * closing[index] - rate * pulled[index]) for index in range(3)
    ]


def main_kernel(
    devices,
    own_count,
    sizes,
    listed_from,
    field,
    out_place,
    out_motion,
    out_pull,
    out_change,
    ahead,
    slab,
    table,
    names,
    guess,
    mid_field,
    mid_state,
    mid_names,
    result,
    listed,
    arrived,
):
    count_fine, count_mid, count_all = sizes
    blocks, blocks_fine = count_mid // 8, count_fine // 8
    groups = mid_field.shape[0]
    sub = lax.broadcasted_iota(jnp.int32, (8, lanes), 0)
    lane = lax.broadcasted_iota(jnp.int32, (8, lanes), 1)

    def spread(column):
        return jnp.broadcast_to(column, (8, lanes))

    def lane_total(value):
        return spread(jnp.sum(value, axis=1, keepdims=True))

    def loop(count, body):
        if count <= 4:
            for index in range(count):
                body(index)
        else:
            pl.loop(0, count)(body)

    def rows8(index):
        return pl.ds(index * 8 if isinstance(index, int) else pl.multiple_of(index * 8, 8), 8)

    halves = [slice(0, lanes), slice(lanes, 2 * lanes)]
    me = lax.axis_index("stars")
    first = me * own_count

    copy = pltpu.make_async_copy(listed_from, listed, arrived)
    copy.start()

    def look_ahead(index):
        for half in range(2):
            upper = field[pl.ds(pl.multiple_of(index * 16, 16), 8), halves[half]]
            lower = field[pl.ds(pl.multiple_of(index * 16 + 8, 8), 8), halves[half]]
            turned = pltpu.roll(lower, 4, 0)
            slope = unit * jnp.where(sub < 4, pltpu.roll(upper, 4, 0), turned)
            bend = unit**2 * lower
            twist = jnp.where(sub < 3, unit**3 * turned, 0.0)
            way = slope + 0.5 * bend + twist * (1.0 / 6.0)
            change, second = way, bend + twist
            for step in range(4):
                ahead[step, index * 2 + half] = upper + way
                if step < 3:
                    change = change + second
                    second = second + twist
                    way = way + change

    together = min(4, devices)

    @pl.loop(0, devices // together)
    def _(index):
        for inner in range(together):
            look_ahead(index * together + inner)

    copy.wait()
    count = listed[0]

    mine = pl.multiple_of(slot_of(me, me, devices) * 16, 16)

    def own(part, component, half):
        tile = field[pl.ds(pl.multiple_of(mine + part // 2 * 8, 8), 8), halves[half]]
        at = part % 2 * 4 + component
        return tile[at : at + 1, :]

    def fetch(block):
        room = block if isinstance(block, int) else 0
        name = jnp.zeros((8, lanes), jnp.int32)
        for row in range(8):
            at = 1 + padded(count_all, own_count) + block * 8 + row
            star = listed[at]
            base = pl.multiple_of(listed[at + count_mid], 16)
            side = pl.multiple_of(listed[at + 2 * count_mid], lanes)
            slab[room, 16 * row : 16 * row + 16, :] = field[pl.ds(base, 16), pl.ds(side, lanes)]
            name = jnp.where(sub == row, star, name)
        names[rows8(block), :] = name
        hit = (name & (lanes - 1)) == lane
        for part in range(4):
            for component in range(3):
                value = slab[room, pl.ds(4 * part + component, 8, stride=16), :]
                table[3 * part + component, rows8(block), :] = lane_total(jnp.where(hit, value, 0.0))
        mass = slab[room, pl.ds(15, 8, stride=16), :]
        table[12, rows8(block), :] = -lane_total(jnp.where(hit, mass, 0.0))

    loop(blocks, fetch)
    slow = [own(0, 3, half) > 0.0 for half in range(2)]

    def turn(ref, group, *at):
        total = jnp.zeros((8, lanes), ref.dtype)
        for inner in range(min(16, blocks)):
            value = ref[(*at, rows8(group * 16 + inner), slice(None))]
            total = total + jnp.where(lane == sub + inner * 8, value, jnp.zeros_like(value))
        return jnp.sum(total, axis=0, keepdims=True)

    def fixed(group):
        mid_field[group, 6:7, :] = turn(table, group, 12)
        found = turn(names, group)
        if blocks * 8 < lanes:
            found = jnp.where(lane[0:1, :] < blocks * 8, found, -2)
        mid_names[group, 0:1, :] = found

    def nothing():
        pass

    def elapse_of(step, fine):
        return unit * (1 if fine or step % 2 == 0 else 2)

    def guess_block(step, fine, block):
        state = [table[index, rows8(block), :] for index in range(12)]
        elapse = elapse_of(step, fine)
        for index in range(3):
            moved, sped = predict(
                state[index], state[3 + index], state[6 + index], state[9 + index], elapse
            )
            guess[index, rows8(block), :] = moved
            guess[3 + index, rows8(block), :] = sped

    def place_mid(group):
        for index in range(6):
            mid_field[group, index : index + 1, :] = turn(guess, group, index)

    def force(step, targets, beside):
        def add(totals, row):
            return [pair_terms(target, row, total) for target, total in zip(targets, totals)]

        def one(index, totals):
            for half in range(2):
                row = [ahead[step, index * 2 + half, k : k + 1, :] for k in (0, 1, 2, 4, 5, 6, 3)]
                totals = add(totals, row)
            return totals

        together = min(4, devices)

        def some(index, totals):
            for inner in range(together):
                totals = one(index * together + inner, totals)
            return totals

        zero = jnp.zeros((8, lanes), jnp.float32)
        totals = [[zero] * 6 for _ in targets]
        most = devices // together - 1
        totals = lax.fori_loop(0, most, some, totals)
        beside()
        totals = some(most, totals)
        for group in range(groups):
            totals = add(totals, [mid_field[group, k : k + 1, :] for k in range(7)])
        return [[lane_total(value) for value in total] for total in totals]

    for step in range(4):
        loop(blocks_fine, functools.partial(guess_block, step, True))

        def prepare(step=step):
            if step == 0:
                loop(groups, fixed)
            if step != 1 or blocks > 4:
                loop(
                    blocks - blocks_fine,
                    lambda block: guess_block(step, False, block + blocks_fine),
                )
            loop(groups, place_mid)

        if step == 3:
            break
        apart = blocks_fine // 2 > 4
        if apart:
            prepare()

        def advance(start, step, kinds, early):
            targets = [
                [guess[index, rows8(start + side), :] for index in range(6)]
                for side in range(len(kinds))
            ]
            totals = force(step, targets, nothing if early else prepare)
            for side, (fine, total) in enumerate(zip(kinds, totals)):
                rows = rows8(start + side)
                for index in range(3):
                    moved, sped = correct(
                        *[table[3 * part + index, rows, :] for part in range(4)],
                        total[index],
                        total[3 + index],
                        elapse_of(step, fine),
                    )
                    table[index, rows, :] = moved
                    table[3 + index, rows, :] = sped
                    table[6 + index, rows, :] = total[index]
                    table[9 + index, rows, :] = total[3 + index]

        if not apart:
            both = step == 1 and blocks <= 4
            kinds = [block < blocks_fine for block in range(blocks if both else blocks_fine)]
            if len(kinds) <= 4:
                for block in range(blocks_fine, len(kinds)):
                    guess_block(step, False, block)
                advance(0, step, kinds, False)
                if step == 1 and not both:
                    loop(
                        (blocks - blocks_fine) // 2,
                        lambda pair: advance(blocks_fine + 2 * pair, 1, [False] * 2, True),
                    )
                continue
            prepare()
        loop(blocks_fine // 2, lambda pair: advance(2 * pair, step, [True] * 2, True))
        if step == 1:
            loop(
                (blocks - blocks_fine) // 2,
                lambda pair: advance(blocks_fine + 2 * pair, 1, [False] * 2, True),
            )

    def keep(group):
        for index in range(12):
            mid_state[group, index : index + 1, :] = turn(table, group, index)

    loop(groups, keep)
    result[...] = jnp.zeros_like(result)

    def finish(wide, turn_at):
        hits, states, elapses, targets = [], [], [], []
        for side in range(wide):
            name = jnp.zeros((8, lanes), jnp.int32)
            for row in range(8):
                star = listed[1 + (turn_at * wide + side) * 8 + row]
                name = jnp.where(sub == row, star, name)
            own_hit = [name == lane + (first + half * lanes) for half in range(2)]
            coarse = [own_hit[half] & slow[half] for half in range(2)]
            mid_hit = [name == mid_names[group, 0:1, :] for group in range(groups)]

            def find(part, component):
                total = jnp.zeros((8, lanes), jnp.float32)
                for half in range(2):
                    total = jnp.where(coarse[half], own(part, component, half), total)
                for group in range(groups):
                    at = 3 * part + component
                    total = jnp.where(mid_hit[group], mid_state[group, at : at + 1, :], total)
                return lane_total(total)

            total = jnp.zeros((8, lanes), jnp.float32)
            for half in range(2):
                total = jnp.where(coarse[half], 4 * unit, total)
            for group in range(groups):
                fine = jnp.where(lane + group * lanes < count_fine, unit, 2 * unit)
                total = jnp.where(mid_hit[group], fine, total)
            elapse = lane_total(total)
            state = [[find(part, index) for index in range(3)] for part in range(4)]
            pairs = [
                predict(*[state[part][index] for part in range(4)], elapse) for index in range(3)
            ]
            hits.append(own_hit)
            states.append(state)
            elapses.append(elapse)
            targets.append([pair[0] for pair in pairs] + [pair[1] for pair in pairs])
        for side, total in enumerate(force(3, targets, prepare)):
            for index in range(3):
                moved, sped = correct(
                    *[states[side][part][index] for part in range(4)],
                    total[index],
                    total[3 + index],
                    elapses[side],
                )
                for part, value in enumerate((moved, sped, total[index], total[3 + index])):
                    for half in range(2):
                        result[part, half, index] += jnp.where(hits[side][half], value, 0.0)

    @pl.when((count > 0) & (count <= 16))
    def _():
        finish(2, 0)

    @pl.when(count > 16)
    def _():
        pl.loop(0, (count + 23) // 24)(functools.partial(finish, 3))

    for part, ref in enumerate((out_place, out_motion, out_pull, out_change)):
        for half in range(2):
            changed = own(3, 3, half) < 0.0
            for index in range(3):
                value = jnp.sum(result[part, half, index], axis=0, keepdims=True)
                ref[index : index + 1, halves[half]] = jnp.where(
                    changed, value, own(part, index, half)
                )


def body(devices, place, motion, pull, change, masses, star_level, fine, mid, every):
    own_count = place.shape[1]
    assert own_count == 2 * lanes
    sizes = (fine.shape[0], mid.shape[0], every.shape[0])
    groups = -(-sizes[1] // lanes)
    block = pl.pallas_call(
        pack_kernel,
        out_shape=jax.ShapeDtypeStruct((16, own_count), jnp.float32),
        in_specs=[vmem] * 6,
        out_specs=vmem,
        compiler_params=pltpu.CompilerParams(vmem_limit_bytes=1024 * 1024),
        name="pack",
    )(place, motion, pull, change, masses.reshape(2, lanes), star_level.reshape(2, lanes))

    listed_shape = (1 + padded(sizes[2], own_count) + 3 * sizes[1],)

    def plan(lists):
        return pl.pallas_call(
            functools.partial(plan_kernel, devices, own_count),
            out_shape=jax.ShapeDtypeStruct(listed_shape, jnp.int32),
            in_specs=[smem] * 3,
            out_specs=smem,
            compiler_params=pltpu.CompilerParams(vmem_limit_bytes=1024 * 1024),
            name="plan",
        )(*lists)

    whole, listed = gather(block, devices, (fine, mid, every), plan)
    room = devices * 52 * 1024 + sizes[1] * 12 * 1024 + 3 * 1024 * 1024
    result = jax.ShapeDtypeStruct((3, own_count), jnp.float32)
    return pl.pallas_call(
        functools.partial(main_kernel, devices, own_count, sizes),
        out_shape=(result,) * 4,
        in_specs=[pl.BlockSpec(memory_space=pl.ANY), vmem],
        out_specs=(vmem,) * 4,
        scratch_shapes=[
            pltpu.VMEM((4, devices * 2, 8, lanes), jnp.float32),
            pltpu.VMEM((min(4, sizes[1] // 8), 8 * 16, lanes), jnp.float32),
            pltpu.VMEM((13, sizes[1], lanes), jnp.float32),
            pltpu.VMEM((sizes[1], lanes), jnp.int32),
            pltpu.VMEM((6, sizes[1], lanes), jnp.float32),
            pltpu.VMEM((groups, 8, lanes), jnp.float32),
            pltpu.VMEM((groups, 16, lanes), jnp.float32),
            pltpu.VMEM((groups, 8, lanes), jnp.int32),
            pltpu.VMEM((4, 2, 3, 8, lanes), jnp.float32),
            pltpu.SMEM(listed_shape, jnp.int32),
            pltpu.SemaphoreType.DMA,
        ],
        compiler_params=pltpu.CompilerParams(vmem_limit_bytes=room),
        name="steps",
    )(listed, whole)


def solution(mesh):
    split = P(None, "stars")
    return jax.shard_map(
        functools.partial(body, mesh.shape["stars"]),
        mesh=mesh,
        in_specs=(split,) * 4 + (P("stars"),) * 2 + (P(),) * 3,
        out_specs=(split,) * 4,
        check_vma=False,
    )
```
